512 devices in a mesh: inst: 8 (over z), axial: 16 (over y, core), span: 4 (over x).
Axes of the slice: x: 4, y: 8, z: 8, core: 2. Of those that a mesh axis runs over, the one named last changes fastest.
Arguments:
- state: float32 [8, 256, 5, 2048], P('inst', 'axial', None, 'span'), may hold values from -6 to 6
- source_terms: float32 [8, 256, 5, 2048], P('inst', 'axial', None, 'span'), may hold values from -6 to 6
- pivot_inverse: float32 [8, 256, 5, 5, 2048], P('inst', 'axial', None, None, 'span'), may hold values from -0.002 to 0.024
- coupling: float32 [8, 256, 5, 5, 2048], P('inst', 'axial', None, None, 'span'), may hold values from -1 to 1
- back_coupling: float32 [8, 256, 5, 5, 2048], P('inst', 'axial', None, None, 'span'), may hold values from -1 to 1
- wall_flags: int32 [256, 2048], P('axial', 'span'), may hold values 0 or 1
Outputs:
- smoothed: float32 [8, 256, 5, 2048], P('inst', 'axial', None, 'span')
The draws below stay inside these ranges and needn't reach their ends.
All inputs are finite; a program needn't handle non-finite values. No bound on the sum of `wall_flags` on one device may be relied on, other than what follows from the above.
Results may differ from the reference program's by a relative error of at most 0.0003.
Values sent between devices are 32-bit elements; how exact they have to be, the bound alone decides.
No kernel may reach another device: no remote copies, remote signals or barrier semaphores. Data moves between devices by JAX's collectives and lax.ppermute only.
A program may use at most 64 MiB of HBM per device.

```python
import math
import jax
import jax.numpy as jnp
from jax import lax

INST = 8
VARS = 5
SWEEPS = 2
STREAMWISE_NODES = 256
LINES = 2048


def chain_blocks(key, share):
    stochastic_seeds = jax.random.split(key, 8)
    slow = jax.random.uniform(stochastic_seeds[0], (INST, 1, 1, LINES)) < share
    slow_rate = 1.0 - jax.random.uniform(stochastic_seeds[1], (INST, 1, VARS, LINES), minval=0.2, maxval=1.0) * 2.0 / STREAMWISE_NODES
    fast_rate = jax.random.uniform(stochastic_seeds[2], (INST, 1, VARS, LINES), minval=0.8, maxval=0.92)
    rate = jnp.where(slow, slow_rate, fast_rate)
    volume_locations = jax.random.randint(stochastic_seeds[3], (3,), 0, STREAMWISE_NODES)
    volume_quantities = jnp.arange(STREAMWISE_NODES)
    contiguous_extent = jnp.any(volume_quantities[:, None] == volume_locations[None, :], axis=1)
    decay_multiplier = jnp.where(contiguous_extent, jax.random.uniform(stochastic_seeds[4], (STREAMWISE_NODES,), minval=0.5, maxval=0.8), 1.0)
    rate = rate * decay_multiplier[None, :, None, None]
    angles = jax.random.uniform(stochastic_seeds[5], (2, INST, STREAMWISE_NODES, LINES), minval=0.2, maxval=1.2)
    cos_one = jnp.cos(angles[0])
    sine_first = jnp.sin(angles[0])
    cos_two = jnp.cos(angles[1])
    sin_two = jnp.sin(angles[1])
    magnitude = jax.random.uniform(stochastic_seeds[6], (VARS, INST, STREAMWISE_NODES, LINES), minval=0.5, maxval=1.5)
    signs = (2 * jax.random.randint(stochastic_seeds[7], (VARS, INST, STREAMWISE_NODES, LINES), 0, 2) - 1).astype(jnp.float32)
    vector = magnitude * signs
    length_sq = jnp.sum(vector * vector, axis=0)
    reflect = [[(1.0 if row == col else 0.0) - 2.0 * vector[row] * vector[col] / length_sq for col in range(VARS)] for row in range(VARS)]
    rows = []
    for row in range(VARS):
        entries = reflect[row]
        rows.append([entries[0] * cos_one + entries[1] * sine_first, entries[1] * cos_one - entries[0] * sine_first, entries[2] * cos_two + entries[3] * sin_two, entries[3] * cos_two - entries[2] * sin_two, entries[4]])
    mixing = jnp.stack([jnp.stack(row, axis=2) for row in rows], axis=2)
    return (-rate[:, :, :, None, :] * mixing).astype(jnp.float32)


def draw_coupling(key, part):
    share = 0.5
    return chain_blocks(jax.random.fold_in(key, 11), share)


def draw_back_coupling(key, part):
    share = 0.5
    return chain_blocks(jax.random.fold_in(key, 23), share)


def draw_pivot_inverse(key, part):
    stochastic_seeds = jax.random.split(jax.random.fold_in(key, 37), 2)
    diag = jax.random.uniform(stochastic_seeds[0], (INST, STREAMWISE_NODES, VARS, LINES), minval=0.006, maxval=0.018)
    off = jax.random.uniform(stochastic_seeds[1], (INST, STREAMWISE_NODES, VARS, VARS, LINES), minval=-0.002, maxval=0.002)
    eye = (jnp.arange(VARS)[:, None] == jnp.arange(VARS)[None, :]).astype(jnp.float32)[None, None, :, :, None]
    return (off * (1.0 - eye) + eye * diag[:, :, :, None, :]).astype(jnp.float32)


def touch_ends(result, stream_key, smallest, largest):
    place = [jax.random.randint(jax.random.fold_in(stream_key, axis), (), 0, length) for axis, length in enumerate(result.shape)]
    main_axis = result.shape.index(max(result.shape))
    neighbour = place[:main_axis] + [(place[main_axis] + 1) % result.shape[main_axis]] + place[main_axis + 1:]
    return result.at[tuple(place)].set(smallest).at[tuple(neighbour)].set(largest)


def level_of(key, shape, cuts, smallest, largest):
    level, own = 1.0, jax.random.fold_in(key, 6)
    for position, shards_of in cuts:
        steps = jnp.exp(jax.random.uniform(jax.random.fold_in(own, position), (shards_of,), jnp.float32, smallest / len(cuts), largest / len(cuts)))
        level = level * jnp.repeat(steps, shape[position] // shards_of).reshape([-1 if axis == position else 1 for axis in range(len(shape))])
    return level


def bell_draw(stream_key, dims, width, limit, cuts=(), held_as=jnp.bfloat16):
    array = jax.random.normal(stream_key, dims, jnp.float32) * width
    if len(cuts) > 0:
        array = level_of(stream_key, dims, cuts, -0.22, 0.18) * array
    return jnp.clip(array, min=-limit, max=limit).astype(held_as)


def setup_inputs(seed: int = 0) -> dict:
    streams_of = jax.random.split(jax.random.key(seed), 7)
    return {
        "state": bell_draw(streams_of[0], (INST, STREAMWISE_NODES, VARS, LINES), 1.0, 6.0, ((0, 8), (1, 16), (3, 4)), jnp.float32),
        "source_terms": bell_draw(streams_of[1], (INST, STREAMWISE_NODES, VARS, LINES), 1.0, 6.0, ((0, 8), (1, 16), (3, 4)), jnp.float32),
        "pivot_inverse": draw_pivot_inverse(jax.random.fold_in(streams_of[6], 71), 0),
        "coupling": draw_coupling(jax.random.fold_in(streams_of[6], 71), 0),
        "back_coupling": draw_back_coupling(jax.random.fold_in(streams_of[6], 71), 0),
        "wall_flags": touch_ends((jax.random.randint(streams_of[5], (STREAMWISE_NODES, LINES), 0, 8) < 1).astype(jnp.int32), jax.random.fold_in(streams_of[5], 1), 0, 1),
    }


time_weight = 0.5
convection_term = 0.6
viscosity = 0.2
circular = 0.2
dissipation = 0.5


def spectral(rows, cols):
    diff = rows[:, None] - cols[None, :]
    sign = (1 - 2 * jnp.mod(diff, 2)).astype(jnp.float32)
    angle = math.pi * diff.astype(jnp.float32) / INST
    safe = jnp.where(diff == 0, 0.5 * math.pi, angle)
    first = jnp.where(diff == 0, 0.0, 0.5 * sign * jnp.cos(safe) / jnp.sin(safe))
    sine = jnp.sin(safe)
    second = jnp.where(diff == 0, -(INST * INST + 2.0) / 12.0, -0.5 * sign / (sine * sine))
    return (first - dissipation * second).astype(jnp.float32)


def cell_apply(matrix, vector):
    return jnp.sum(matrix * vector[:, None, :, :], axis=2)


def run_chain(source, coupling, start, reverse):
    count = source.shape[1]
    order = jnp.arange(count)
    if reverse:
        order = order[::-1]

    def advance(prev, index):
        src = lax.dynamic_index_in_dim(source, index, 1, keepdims=False)
        cpl = lax.dynamic_index_in_dim(coupling, index, 1, keepdims=False)
        now = src - cell_apply(cpl, prev)
        return now, now

    _, values = lax.scan(advance, start, order)
    if reverse:
        values = values[::-1]
    return jnp.moveaxis(values, 0, 1)


def reference(state, source_terms, pivot_inverse, coupling, back_coupling, wall_flags):
    keep = (1 - wall_flags).astype(jnp.float32)[None, :, None, :]
    index = jnp.arange(INST)
    weights = spectral(index, index)
    for sweep in range(SWEEPS):
        time = jnp.sum(weights[:, :, None, None, None] * state[None], axis=1)
        padded = jnp.pad(state, ((0, 0), (1, 1), (0, 0), (0, 0)))
        below = padded[:, :-2]
        above = padded[:, 2:]
        left = jnp.roll(state, 1, axis=3)
        right = jnp.roll(state, -1, axis=3)
        rhs = keep * (source_terms - time_weight * time - 0.5 * convection_term * (above - below)
                      + viscosity * (above - 2.0 * state + below)
                      + circular * (right - 2.0 * state + left))
        source = jnp.sum(pivot_inverse * rhs[:, :, None], axis=3)
        zeros = jnp.zeros((state.shape[0], state.shape[2], state.shape[3]), jnp.float32)
        downstream_elimination = run_chain(source, coupling, zeros, False)
        backward = run_chain(downstream_elimination, back_coupling, zeros, True)
        state = state + backward
    return state
```

```python
import math

import jax
import jax.numpy as jnp
import numpy as np
from jax import lax
from jax.experimental import pallas as pl
from jax.experimental.pallas import tpu as pltpu
from jax.sharding import PartitionSpec as P

INST = 8
SWEEPS = 2
VARS = 5
STEPS = 8
TILES = 4
SEGMENTS = 16
F32 = jnp.float32
FIELD = STEPS * VARS * 8
MATRIX = STEPS * VARS * VARS * 8
FULL_GROUPS = 24
VEC_GROUPS = 4


def spectral():
    index = np.arange(INST)
    diff = index[:, None] - index[None, :]
    sign = 1.0 - 2.0 * np.mod(diff, 2)
    safe = np.where(diff == 0, 0.5 * math.pi, math.pi * diff / INST)
    first = np.where(diff == 0, 0.0, 0.5 * sign * np.cos(safe) / np.sin(safe))
    second = np.where(diff == 0, -(INST * INST + 2.0) / 12.0, -0.5 * sign / np.sin(safe) ** 2)
    return first - 0.5 * second


def iotas():
    sub = lax.broadcasted_iota(jnp.int32, (8, 128), 0)
    lane = lax.broadcasted_iota(jnp.int32, (8, 128), 1)
    return sub, lane


def row(ref, index):
    return ref[pl.ds(pl.multiple_of(index * 8, 8), 8), :]


def rows(ref, start, count):
    return [row(ref, start + n) for n in range(count)]


def put(ref, index, value):
    ref[pl.ds(pl.multiple_of(index * 8, 8), 8), :] = value


def total(terms):
    terms = list(terms)
    while len(terms) > 1:
        terms = [terms[n] + terms[n + 1] if n + 1 < len(terms) else terms[n] for n in range(0, len(terms), 2)]
    return terms[0]


def matvec(m, v):
    return [total(m[i * VARS + j] * v[j] for j in range(VARS)) for i in range(VARS)]


def matmul(a, b):
    return [
        total(a[i * VARS + j] * b[j * VARS + m] for j in range(VARS))
        for i in range(VARS)
        for m in range(VARS)
    ]


def plus(a, b):
    return [x + y for x, y in zip(a, b)]


def minus(a, b):
    return [x - y for x, y in zip(a, b)]


def swap(a):
    return [pltpu.roll(x, 4, 0) for x in a]


def pick(mask, a, b):
    return [jnp.where(mask, x, y) for x, y in zip(a, b)]


def lane_roll(x, shift):
    shift = shift % 128
    return x if shift == 0 else pltpu.roll(x, shift, 1)


def blocks4(block, parts):
    out = parts[0]
    for p in range(1, 4):
        out = jnp.where(block == p, parts[p], out)
    return out


def pack_lines(out_ref, block, values, first, groups):
    for g in range((len(values) + 3) // 4):
        four = [values[min(4 * g + p, len(values) - 1)] for p in range(4)]
        for q in range(4):
            chunk = blocks4(block, [lane_roll(four[p], 32 * (p - q)) for p in range(4)])
            out_ref[pl.ds(q * groups + first + g, 4, stride=4 * groups), :] = chunk[:4]


def edge_lines(sub, lane, u, last_ref, first_ref):
    last = jnp.zeros((8, 128), F32)
    initial = jnp.zeros((8, 128), F32)
    for n in range(STEPS * VARS):
        last = jnp.where(lane == n, lane_roll(u[n], n - 127), last)
        initial = jnp.where(lane == n, lane_roll(u[n], n), initial)
    last_ref[...] = pltpu.roll(last, 5, 0)
    first_ref[...] = pltpu.roll(initial, 3, 0)


def field_to_packed(raw_ref, out_ref):
    for k in range(2 * STEPS):
        for t in range(TILES):
            start = (k % STEPS) * VARS * 8 + (k // STEPS) * TILES + t
            out_ref[pl.ds(start, VARS, stride=8), :] = raw_ref[k, :, t * 128 : (t + 1) * 128]


def pack_kernel(state_ref, u_ref, last_ref, first_ref):
    sub, lane = iotas()
    field_to_packed(state_ref, u_ref)
    edge_lines(sub, lane, rows(u_ref, 0, STEPS * VARS), last_ref, first_ref)


def maps_kernel(
    u_ref, source_ref, flags_ref, pivot_raw, coupling_raw, back_raw,
    src_ref, keep_ref, pivot_ref, coupling_ref, back_ref, halves_ref, packed_ref, up_ref,
    prefix_ref,
):
    sub, lane = iotas()
    block = lane // 32
    field_to_packed(source_ref, src_ref)
    for k in range(2 * STEPS):
        for t in range(TILES):
            start = (k % STEPS) * 8 + (k // STEPS) * TILES + t
            keep_ref[start : start + 1, :] = (1 - flags_ref[k : k + 1, t * 128 : (t + 1) * 128]).astype(F32)

    def relayout(k, carry):
        for raw, out in ((pivot_raw, pivot_ref), (coupling_raw, coupling_ref), (back_raw, back_ref)):
            for half in range(2):
                for i in range(VARS):
                    for t in range(TILES):
                        start = (k * VARS + i) * VARS * 8 + half * TILES + t
                        out[pl.ds(start, VARS, stride=8), :] = raw[k + half * STEPS, i, :, t * 128 : (t + 1) * 128]
        return carry

    lax.fori_loop(0, STEPS, relayout, 0)
    size = VARS * VARS

    def forward(k, p):
        p = [-x for x in matmul(rows(coupling_ref, k * size, size), p)]
        for n in range(size):
            put(prefix_ref, k * size + n, p[n])
        return p

    first = [-x for x in rows(coupling_ref, 0, size)]
    for n in range(size):
        put(prefix_ref, n, first[n])
    ahead = lax.fori_loop(1, STEPS, forward, first)

    def backward(step, carry):
        k = STEPS - 2 - step
        return minus(rows(prefix_ref, k * size, size), matmul(rows(back_ref, k * size, size), carry))

    mixed = lax.fori_loop(0, STEPS - 1, backward, ahead)

    def behind_step(step, carry):
        k = STEPS - 2 - step
        return [-x for x in matmul(rows(back_ref, k * size, size), carry)]

    behind = lax.fori_loop(0, STEPS - 1, behind_step, [-x for x in rows(back_ref, (STEPS - 1) * size, size)])
    for n in range(size):
        put(halves_ref, n, ahead[n])
        put(halves_ref, size + n, mixed[n])
        put(halves_ref, 2 * size + n, behind[n])
    whole_ahead = matmul(swap(ahead), ahead)
    for n in range(size):
        put(prefix_ref, n, whole_ahead[n])
    whole_mixed = plus(mixed, matmul(behind, matmul(swap(mixed), ahead)))
    for n in range(size):
        put(prefix_ref, size + n, whole_mixed[n])
    whole_behind = matmul(behind, swap(behind))
    for n in range(size):
        put(prefix_ref, 2 * size + n, whole_behind[n])
    pack_lines(packed_ref, block, rows(prefix_ref, 0, 3 * size), VEC_GROUPS, FULL_GROUPS)
    up_ref[: VARS * 8, :] = u_ref[(STEPS - 1) * VARS * 8 :, :]
    up_ref[VARS * 8 :, :] = back_ref[(STEPS - 1) * size * 8 :, :]


def time_kernel(weights, u_ref, out_ref):
    for v in range(VARS):
        fields = [row(u_ref, j * VARS + v) for j in range(INST)]
        for i in range(INST):
            put(out_ref, i * VARS + v, total(fields[j] * F32(weights[i, j]) for j in range(INST)))


def stencil_kernel(u_ref, src_ref, below_ref, above_ref, left_ref, right_ref, out_ref):
    sub, lane = iotas()
    top = sub < TILES
    left_all = left_ref[...]
    right_all = right_ref[...]
    for k in range(STEPS):
        for v in range(VARS):
            n = k * VARS + v
            u = row(u_ref, n)
            if k == 0:
                below = pltpu.roll(jnp.where(top, row(u_ref, (STEPS - 1) * VARS + v), row(below_ref, v)), 4, 0)
            else:
                below = row(u_ref, n - VARS)
            if k == STEPS - 1:
                above = pltpu.roll(jnp.where(top, row(above_ref, v), row(u_ref, v)), 4, 0)
            else:
                above = row(u_ref, n + VARS)
            turned = pltpu.roll(u, 1, 1)
            edge = jnp.where(sub % TILES == 0, lane_roll(left_all, -n), pltpu.roll(turned, 1, 0))
            left = jnp.where(lane == 0, edge, turned)
            turned = pltpu.roll(u, 127, 1)
            edge = jnp.where(sub % TILES == TILES - 1, lane_roll(right_all, 127 - n), pltpu.roll(turned, 7, 0))
            right = jnp.where(lane == 127, edge, turned)
            value = row(src_ref, n) - 0.1 * above + 0.5 * below - 0.8 * u + 0.2 * (left + right)
            put(out_ref, n, value)


def local_kernel(base_ref, time_ref, keep_ref, pivot_ref, coupling_ref, back_ref, halves_ref, *rest):
    if len(rest) == 5:
        maps_ref, source_ref, ends_ref, packed_ref, y_ref = rest
        groups = FULL_GROUPS
        packed_ref[...] = maps_ref[...]
    else:
        source_ref, ends_ref, packed_ref, y_ref = rest
        groups = VEC_GROUPS
    sub, lane = iotas()
    block = lane // 32
    size = VARS * VARS

    def source_step(k, carry):
        keep = row(keep_ref, k)
        rhs = [keep * (row(base_ref, k * VARS + v) + row(time_ref, k * VARS + v)) for v in range(VARS)]
        for v, value in enumerate(matvec(rows(pivot_ref, k * size, size), rhs)):
            put(source_ref, k * VARS + v, value)
        return carry

    lax.fori_loop(0, STEPS, source_step, 0)
    y = rows(source_ref, 0, VARS)
    kept = [y]
    for k in range(1, STEPS):
        y = minus(rows(source_ref, k * VARS, VARS), matvec(rows(coupling_ref, k * size, size), y))
        kept.append(y)
    end = y
    x = y
    for k in range(STEPS - 2, -1, -1):
        x = minus(kept[k], matvec(rows(back_ref, k * size, size), x))
    for v in range(VARS):
        put(ends_ref, v, end[v])
        put(ends_ref, VARS + v, x[v])
    ahead = rows(halves_ref, 0, size)
    mixed = rows(halves_ref, size, size)
    behind = rows(halves_ref, 2 * size, size)
    whole_end = plus(swap(end), matvec(swap(ahead), end))
    inner = plus(swap(x), matvec(swap(mixed), end))
    whole_first = plus(x, matvec(behind, inner))
    values = whole_end + whole_first + [jnp.zeros((8, 128), F32)] * (4 * VEC_GROUPS - 2 * VARS)
    pack_lines(packed_ref, block, values, 0, groups)


def shift_in(sub, values, entry):
    return [jnp.where(sub == 0, e, pltpu.roll(x, 1, 0)) for x, e in zip(values, entry)]


def shift_out(sub, values, entry):
    return [jnp.where(sub == 7, e, pltpu.roll(x, 7, 0)) for x, e in zip(values, entry)]


def reduced_kernel(first, recv_ref, maps_in_ref, out_ref, *rest):
    sub, lane = iotas()
    block = lane // 32
    size = VARS * VARS
    groups = FULL_GROUPS if first else VEC_GROUPS

    def value(r, part):
        stacked = recv_ref[pl.ds(part * 8 * groups + r // 4, 8, stride=groups), :]
        return lane_roll(stacked, -32 * (r % 4))

    if first:
        maps_ref = rest[0]
        for r in range(3 * size):
            for part in range(2):
                put(maps_ref, part * 3 * size + r, value(4 * VEC_GROUPS + r, part))
    else:
        maps_ref = maps_in_ref
    zero = [jnp.zeros((8, 128), F32)] * VARS

    def solve(part, which, source, entry, shift):
        maps = rows(maps_ref, part * 3 * size + which * size, size)

        def step(_, now):
            return plus(source, matvec(maps, shift(sub, now, entry)))

        out = lax.fori_loop(0, 7, step, plus(source, matvec(maps, shift(sub, zero, entry))))
        return out, shift(sub, out, entry)

    ends = [[value(r, part) for r in range(VARS)] for part in range(2)]
    firsts = [[value(VARS + r, part) for r in range(VARS)] for part in range(2)]
    out, low_entry = solve(0, 0, ends[0], zero, shift_in)
    out, high_entry = solve(1, 0, ends[1], [pltpu.roll(x, 1, 0) for x in out], shift_in)
    entries = [low_entry, high_entry]
    drive = [
        plus(firsts[part], matvec(rows(maps_ref, part * 3 * size + size, size), entries[part])) for part in range(2)
    ]
    out, high_next = solve(1, 2, drive[1], zero, shift_out)
    out, low_next = solve(0, 2, drive[0], [pltpu.roll(x, 7, 0) for x in out], shift_out)
    nexts = [low_next, high_next]
    for part in range(2):
        values = entries[part] + nexts[part] + zero + zero[:1]
        for g in range(VEC_GROUPS):
            packed = blocks4(block, [lane_roll(values[4 * g + p], 32 * p) for p in range(4)])
            out_ref[pl.ds(part * 8 * VEC_GROUPS + g, 8, stride=VEC_GROUPS), :] = packed


def finish_kernel(
    last, recv_ref, u_ref, source_ref, ends_ref, coupling_ref, back_ref, halves_ref, *rest
):
    if last:
        out_ref, new_ref = rest
    else:
        up_ref, above_ref, new_ref, last_ref, first_ref, new_below_ref, new_above_ref = rest
    sub, lane = iotas()
    block = lane // 32
    top = sub < TILES
    size = VARS * VARS
    stacked = [
        [
            recv_ref[pl.ds(q * VEC_GROUPS + g, TILES, stride=4 * VEC_GROUPS), :]
            for g in range((2 * VARS + 3) // 4)
        ]
        for q in range(4)
    ]
    stacked = [[jnp.concatenate([x, x], axis=0) for x in line] for line in stacked]

    def value(r):
        return blocks4(block, [lane_roll(stacked[q][r // 4], 32 * (q - r % 4)) for q in range(4)])

    entry = [value(r) for r in range(VARS)]
    after = [value(VARS + r) for r in range(VARS)]
    end = rows(ends_ref, 0, VARS)
    begin = rows(ends_ref, VARS, VARS)
    middle = plus(end, matvec(rows(halves_ref, 0, size), entry))
    start = pick(top, entry, swap(middle))
    follow = plus(
        plus(begin, matvec(rows(halves_ref, size, size), start)),
        matvec(rows(halves_ref, 2 * size, size), after),
    )
    finish = pick(top, swap(follow), after)
    y = start
    kept = []
    for k in range(STEPS):
        y = minus(rows(source_ref, k * VARS, VARS), matvec(rows(coupling_ref, k * size, size), y))
        kept.append(y)
    x = finish
    for k in range(STEPS - 1, -1, -1):
        x = minus(kept[k], matvec(rows(back_ref, k * size, size), x))
        for v in range(VARS):
            put(new_ref, k * VARS + v, row(u_ref, k * VARS + v) + x[v])
    if last:
        for k in range(2 * STEPS):
            for t in range(TILES):
                begin_row = (k % STEPS) * VARS * 8 + (k // STEPS) * TILES + t
                out_ref[k, :, t * 128 : (t + 1) * 128] = new_ref[pl.ds(begin_row, VARS, stride=8), :]
    else:
        edge_lines(sub, lane, rows(new_ref, 0, STEPS * VARS), last_ref, first_ref)
        before = minus(entry, matvec(rows(up_ref, VARS, size), swap(x)))
        for v in range(VARS):
            put(new_below_ref, v, row(up_ref, v) + before[v])
            put(new_above_ref, v, row(above_ref, v) + after[v])


def call(kernel, shapes, *args, scratch=(), flops=100_000, limit=24):
    outs = [jax.ShapeDtypeStruct(shape, F32) for shape in shapes]
    moved = 4 * (sum(math.prod(shape) for shape in shapes) + sum(a.size for a in args))
    return pl.pallas_call(
        kernel,
        out_shape=outs,
        scratch_shapes=[pltpu.VMEM(shape, F32) for shape in scratch],
        cost_estimate=pl.CostEstimate(flops=flops, bytes_accessed=moved, transcendentals=0),
        compiler_params=pltpu.CompilerParams(vmem_limit_bytes=limit * 1024 * 1024),
    )(*args)


def exchange(value, axis, count):
    shape = value.shape
    out = lax.all_to_all(value.reshape(count, shape[0] // count, 128), axis, 0, 0)
    return out.reshape(shape)


def moved(value, axis, step, wrap):
    count = lax.axis_size(axis)
    pairs = [(i, (i + step) % count) for i in range(count) if wrap or 0 <= i + step < count]
    return lax.ppermute(value, axis, pairs)


def body(state, source_terms, pivot_inverse, coupling, back_coupling, wall_flags):
    weights = np.float32(-0.5 * spectral())
    edge = (8, 128)
    u, last_line, first_line = call(pack_kernel, [(FIELD, 128), edge, edge], state[0])
    src, keep, pivot, forth, back, halves, packed_maps, up = call(
        maps_kernel,
        [
            (FIELD, 128), (STEPS * 8, 128), (MATRIX, 128), (MATRIX, 128), (MATRIX, 128),
            (3 * VARS * VARS * 8, 128), (SEGMENTS * FULL_GROUPS, 128), ((VARS + VARS * VARS) * 8, 128),
        ],
        u, source_terms[0], wall_flags, pivot_inverse[0], coupling[0], back_coupling[0],
        scratch=[(MATRIX, 128)],
        flops=8_000_000,
    )
    above = below = None
    maps = None
    for sweep in range(SWEEPS):
        first = sweep == 0
        left = moved(last_line, "span", 1, True)
        right = moved(first_line, "span", -1, True)
        if first:
            up = moved(up, "axial", 1, False)
            above = moved(u[: VARS * 8], "axial", -1, False)
            below = up[: VARS * 8]
        spread = exchange(u, "inst", INST)
        (term,) = call(lambda *refs: time_kernel(weights, *refs), [(FIELD, 128)], spread)
        time = exchange(term, "inst", INST)
        (base,) = call(stencil_kernel, [(FIELD, 128)], u, src, below, above, left, right)
        groups = FULL_GROUPS if first else VEC_GROUPS
        source, ends, packed = call(
            local_kernel,
            [(FIELD, 128), (2 * VARS * 8, 128), (SEGMENTS * groups, 128)],
            base, time, keep, pivot, forth, back, halves, *((packed_maps,) if first else ()),
            scratch=[(8, 128)],
        )
        recv = exchange(packed, "axial", SEGMENTS)
        shapes = [(SEGMENTS * VEC_GROUPS, 128)]
        if first:
            shapes.append((6 * VARS * VARS * 8, 128))
        out = call(
            lambda *refs, f=first: reduced_kernel(f, *((refs[0], None) + refs[1:] if f else refs)),
            shapes, recv, *(() if first else (maps,)),
        )
        if first:
            maps = out[1]
        back_recv = exchange(out[0], "axial", SEGMENTS)
        last = sweep == SWEEPS - 1
        common = (back_recv, u, source, ends, forth, back, halves)
        if last:
            (result,) = call(
                lambda *refs: finish_kernel(True, *refs), [(2 * STEPS, VARS, TILES * 128)], *common,
                scratch=[(FIELD, 128)],
            )
        else:
            halo = (VARS * 8, 128)
            u, last_line, first_line, below, above = call(
                lambda *refs: finish_kernel(False, *refs), [(FIELD, 128), edge, edge, halo, halo],
                *common, up, above,
            )
    return result[None]


def solution(mesh):
    return jax.shard_map(
        body,
        mesh=mesh,
        in_specs=(
            P("inst", "axial", None, "span"),
            P("inst", "axial", None, "span"),
            P("inst", "axial", None, None, "span"),
            P("inst", "axial", None, None, "span"),
            P("inst", "axial", None, None, "span"),
            P("axial", "span"),
        ),
        out_specs=P("inst", "axial", None, "span"),
        check_vma=False,
    )
```

```python
import math

import jax
import jax.numpy as jnp
import numpy as np
from jax import lax
from jax.experimental import pallas as pl
from jax.experimental.pallas import tpu as pltpu
from jax.sharding import PartitionSpec as P

INST = 8
SWEEPS = 2
VARS = 5
STEPS = 8
TILES = 4
SEGMENTS = 16
F32 = jnp.float32
FIELD = STEPS * VARS * 8
MATRIX = STEPS * VARS * VARS * 8
SIZE = VARS * VARS
MAP_BLOCKS = SIZE + (SIZE + 1) // 2


def spectral():
    index = np.arange(INST)
    diff = index[:, None] - index[None, :]
    sign = 1.0 - 2.0 * np.mod(diff, 2)
    safe = np.where(diff == 0, 0.5 * math.pi, math.pi * diff / INST)
    first = np.where(diff == 0, 0.0, 0.5 * sign * np.cos(safe) / np.sin(safe))
    second = np.where(diff == 0, -(INST * INST + 2.0) / 12.0, -0.5 * sign / np.sin(safe) ** 2)
    return first - 0.5 * second


def iotas():
    sub = lax.broadcasted_iota(jnp.int32, (8, 128), 0)
    lane = lax.broadcasted_iota(jnp.int32, (8, 128), 1)
    return sub, lane


def row(ref, index):
    return ref[pl.ds(pl.multiple_of(index * 8, 8), 8), :]


def rows(ref, start, count):
    return [row(ref, start + n) for n in range(count)]


def put(ref, index, value):
    ref[pl.ds(pl.multiple_of(index * 8, 8), 8), :] = value


def total(terms):
    terms = list(terms)
    while len(terms) > 1:
        terms = [terms[n] + terms[n + 1] if n + 1 < len(terms) else terms[n] for n in range(0, len(terms), 2)]
    return terms[0]


def matvec(m, v):
    return [total(m[i * VARS + j] * v[j] for j in range(VARS)) for i in range(VARS)]


def matmul(a, b):
    return [
        total(a[i * VARS + j] * b[j * VARS + m] for j in range(VARS))
        for i in range(VARS)
        for m in range(VARS)
    ]


def plus(a, b):
    return [x + y for x, y in zip(a, b)]


def minus(a, b):
    return [x - y for x, y in zip(a, b)]


def swap(a):
    return [pltpu.roll(x, 4, 0) for x in a]


def pick(mask, a, b):
    return [jnp.where(mask, x, y) for x, y in zip(a, b)]


def lane_roll(x, shift):
    shift = shift % 128
    return x if shift == 0 else pltpu.roll(x, shift, 1)


def blocks4(block, parts):
    out = parts[0]
    for p in range(1, 4):
        out = jnp.where(block == p, parts[p], out)
    return out


def halves_of(top, a, b):
    return jnp.where(top, a, pltpu.roll(b, 4, 0))


def both(top, a):
    return [jnp.where(top, x, pltpu.roll(x, 4, 0)) for x in a]


def both_low(top, a):
    return [jnp.where(top, pltpu.roll(x, 4, 0), x) for x in a]


def edge_lines(sub, lane, u, last_ref, first_ref):
    last = jnp.zeros((8, 128), F32)
    initial = jnp.zeros((8, 128), F32)
    for n in range(STEPS * VARS):
        last = jnp.where(lane == n, lane_roll(u[n], n - 127), last)
        initial = jnp.where(lane == n, lane_roll(u[n], n), initial)
    last_ref[...] = pltpu.roll(last, 5, 0)
    first_ref[...] = pltpu.roll(initial, 3, 0)


def field_to_packed(raw_ref, out_ref, start=0):
    for v in range(VARS):
        for half in range(2):
            for t in range(TILES):
                tile = raw_ref[v, half * STEPS : (half + 1) * STEPS, t * 128 : (t + 1) * 128]
                out_ref[pl.ds(start + v * 8 + half * TILES + t, STEPS, stride=VARS * 8), :] = tile


def matrix_to_packed(raw_ref, out_ref, start=0):
    for i in range(VARS):
        for j in range(VARS):
            for half in range(2):
                for t in range(TILES):
                    tile = raw_ref[i, j, half * STEPS : (half + 1) * STEPS, t * 128 : (t + 1) * 128]
                    begin = start + (i * VARS + j) * 8 + half * TILES + t
                    out_ref[pl.ds(begin, STEPS, stride=SIZE * 8), :] = tile


def maps_kernel(
    state_ref, coupling_raw, back_raw,
    u_ref, last_ref, first_ref, lines_ref, maps_ref, up_ref,
    prefix_ref,
):
    sub, lane = iotas()
    top = sub < TILES
    field_to_packed(state_ref, u_ref)
    matrix_to_packed(coupling_raw, lines_ref, 0)
    matrix_to_packed(back_raw, lines_ref, MATRIX)

    def coupling(k):
        return rows(lines_ref, k * SIZE, SIZE)

    def back(k):
        return rows(lines_ref, STEPS * SIZE + k * SIZE, SIZE)

    def forward(k, p):
        p = [-x for x in matmul(coupling(k), p)]
        for n in range(SIZE):
            put(prefix_ref, k * SIZE + n, p[n])
        return p

    first = [-x for x in coupling(0)]
    for n in range(SIZE):
        put(prefix_ref, n, first[n])
    ahead = lax.fori_loop(1, STEPS, forward, first)

    def backward(step, carry):
        k = STEPS - 2 - step
        return minus(rows(prefix_ref, k * SIZE, SIZE), matmul(back(k), carry))

    mixed = lax.fori_loop(0, STEPS - 1, backward, ahead)

    def behind_step(step, carry):
        return [-x for x in matmul(back(STEPS - 2 - step), carry)]

    behind = lax.fori_loop(0, STEPS - 1, behind_step, [-x for x in back(STEPS - 1)])
    base = 2 * STEPS * SIZE
    for n in range(SIZE):
        put(lines_ref, base + n, ahead[n])
        put(lines_ref, base + SIZE + n, mixed[n])
        put(lines_ref, base + 2 * SIZE + n, behind[n])
    whole_ahead = matmul(swap(ahead), ahead)
    whole_behind = matmul(behind, swap(behind))
    for n in range(SIZE):
        put(maps_ref, n, halves_of(top, whole_ahead[n], whole_behind[n]))
    whole_mixed = plus(mixed, matmul(behind, matmul(swap(mixed), ahead)))
    for n in range(0, SIZE, 2):
        put(maps_ref, SIZE + n // 2, halves_of(top, whole_mixed[n], whole_mixed[min(n + 1, SIZE - 1)]))
    edge_lines(sub, lane, rows(u_ref, 0, STEPS * VARS), last_ref, first_ref)
    up_ref[: VARS * 8, :] = u_ref[(STEPS - 1) * VARS * 8 :, :]
    up_ref[VARS * 8 : (VARS + SIZE) * 8, :] = lines_ref[2 * MATRIX - SIZE * 8 : 2 * MATRIX, :]
    up_ref[(VARS + SIZE) * 8 :, :] = u_ref[: VARS * 8, :]


def cells_kernel(source_ref, flags_ref, pivot_raw, out_ref):
    field_to_packed(source_ref, out_ref, 0)
    for half in range(2):
        for t in range(TILES):
            flags = flags_ref[half * STEPS : (half + 1) * STEPS, t * 128 : (t + 1) * 128]
            out_ref[pl.ds(FIELD + half * TILES + t, STEPS, stride=8), :] = (1 - flags).astype(F32)
    matrix_to_packed(pivot_raw, out_ref, FIELD + STEPS * 8)


def time_kernel(weights, u_ref, wait_ref, later_ref, out_ref, *later_out):
    for v in range(VARS):
        fields = [row(u_ref, j * VARS + v) for j in range(INST)]
        for i in range(INST):
            put(out_ref, i * VARS + v, total(fields[j] * F32(weights[i, j]) for j in range(INST)))
    begin = 0
    for ref in later_out:
        ref[...] = later_ref[begin : begin + ref.shape[0], :]
        begin += ref.shape[0]


def stencil_kernel(u_ref, src_ref, below_ref, above_ref, left_ref, right_ref, out_ref):
    sub, lane = iotas()
    top = sub < TILES
    left_all = left_ref[...]
    right_all = right_ref[...]
    for k in range(STEPS):
        for v in range(VARS):
            n = k * VARS + v
            u = row(u_ref, n)
            if k == 0:
                below = pltpu.roll(jnp.where(top, row(u_ref, (STEPS - 1) * VARS + v), row(below_ref, v)), 4, 0)
            else:
                below = row(u_ref, n - VARS)
            if k == STEPS - 1:
                above = pltpu.roll(jnp.where(top, row(above_ref, v), row(u_ref, v)), 4, 0)
            else:
                above = row(u_ref, n + VARS)
            turned = pltpu.roll(u, 1, 1)
            edge = jnp.where(sub % TILES == 0, lane_roll(left_all, -n), pltpu.roll(turned, 1, 0))
            left = jnp.where(lane == 0, edge, turned)
            turned = pltpu.roll(u, 127, 1)
            edge = jnp.where(sub % TILES == TILES - 1, lane_roll(right_all, 127 - n), pltpu.roll(turned, 7, 0))
            right = jnp.where(lane == 127, edge, turned)
            value = row(src_ref, n) - 0.1 * above + 0.5 * below - 0.8 * u + 0.2 * (left + right)
            put(out_ref, n, value)


def local_kernel(base_ref, time_ref, cells_ref, lines_ref, source_ref, ends_ref, packed_ref):
    sub, lane = iotas()
    top = sub < TILES
    pivot_row = STEPS * VARS + STEPS

    def source_step(k, carry):
        keep = row(cells_ref, STEPS * VARS + k)
        rhs = [keep * (row(base_ref, k * VARS + v) + row(time_ref, k * VARS + v)) for v in range(VARS)]
        for v, value in enumerate(matvec(rows(cells_ref, pivot_row + k * SIZE, SIZE), rhs)):
            put(source_ref, k * VARS + v, value)
        return carry

    lax.fori_loop(0, STEPS, source_step, 0)
    y = rows(source_ref, 0, VARS)
    kept = [y]
    for k in range(1, STEPS):
        y = minus(rows(source_ref, k * VARS, VARS), matvec(rows(lines_ref, k * SIZE, SIZE), y))
        kept.append(y)
    end = y
    x = y
    for k in range(STEPS - 2, -1, -1):
        x = minus(kept[k], matvec(rows(lines_ref, (STEPS + k) * SIZE, SIZE), x))
    for v in range(VARS):
        put(ends_ref, v, end[v])
        put(ends_ref, VARS + v, x[v])
    base = 2 * STEPS * SIZE
    ahead = rows(lines_ref, base, SIZE)
    mixed = rows(lines_ref, base + SIZE, SIZE)
    behind = rows(lines_ref, base + 2 * SIZE, SIZE)
    whole_end = plus(swap(end), matvec(swap(ahead), end))
    inner = plus(swap(x), matvec(swap(mixed), end))
    whole_first = plus(x, matvec(behind, inner))
    for v in range(VARS):
        put(packed_ref, v, halves_of(top, whole_end[v], whole_first[v]))


def interface(top, place, ends_ref, maps_ref, entry_ref):
    zero = [jnp.zeros((8, 128), F32)] * VARS

    def pairs(d):
        return rows(ends_ref, d * VARS, VARS)

    def maps(d):
        return rows(maps_ref, d * MAP_BLOCKS, SIZE)

    def forward(d, e):
        for v in range(VARS):
            put(entry_ref, d * VARS + v, e[v])
        return plus(pairs(d), matvec(maps(d), e))

    last = lax.fori_loop(0, SEGMENTS - 1, forward, zero)
    for v in range(VARS):
        put(entry_ref, (SEGMENTS - 1) * VARS + v, last[v])

    def backward(step, f):
        d = SEGMENTS - 1 - step
        mixed = rows(maps_ref, d * MAP_BLOCKS + SIZE, (SIZE + 1) // 2)
        mixed = [mixed[n // 2] if n % 2 else pltpu.roll(mixed[n // 2], 4, 0) for n in range(SIZE)]
        entry = swap(rows(entry_ref, d * VARS, VARS))
        return plus(plus(pairs(d), matvec(mixed, entry)), matvec(maps(d), f))

    after = lax.fori_loop(0, SEGMENTS - 1 - place, backward, zero)
    entry = rows(entry_ref, place * VARS, VARS)
    return both(top, entry), both_low(top, after)


def finish_kernel(
    last, place_ref, gathered_ref, maps_ref, u_ref, source_ref, ends_ref, lines_ref, *rest
):
    if last:
        out_ref, new_ref, entry_ref = rest
    else:
        up_ref, above_ref, new_ref, last_ref, first_ref, new_below_ref, new_above_ref, entry_ref = rest
    sub, lane = iotas()
    top = sub < TILES
    entry, after = interface(top, place_ref[0], gathered_ref, maps_ref, entry_ref)
    base = 2 * STEPS * SIZE
    end = rows(ends_ref, 0, VARS)
    begin = rows(ends_ref, VARS, VARS)
    middle = plus(end, matvec(rows(lines_ref, base, SIZE), entry))
    start = pick(top, entry, swap(middle))
    follow = plus(
        plus(begin, matvec(rows(lines_ref, base + SIZE, SIZE), start)),
        matvec(rows(lines_ref, base + 2 * SIZE, SIZE), after),
    )
    finish = pick(top, swap(follow), after)
    y = start
    kept = []
    for k in range(STEPS):
        y = minus(rows(source_ref, k * VARS, VARS), matvec(rows(lines_ref, k * SIZE, SIZE), y))
        kept.append(y)
    x = finish
    for k in range(STEPS - 1, -1, -1):
        x = minus(kept[k], matvec(rows(lines_ref, (STEPS + k) * SIZE, SIZE), x))
        for v in range(VARS):
            put(new_ref, k * VARS + v, row(u_ref, k * VARS + v) + x[v])
    if last:
        for v in range(VARS):
            for half in range(2):
                for t in range(TILES):
                    tile = new_ref[pl.ds(v * 8 + half * TILES + t, STEPS, stride=VARS * 8), :]
                    out_ref[v, half * STEPS : (half + 1) * STEPS, t * 128 : (t + 1) * 128] = tile
    else:
        edge_lines(sub, lane, rows(new_ref, 0, STEPS * VARS), last_ref, first_ref)
        before = minus(entry, matvec(rows(up_ref, VARS, SIZE), swap(x)))
        for v in range(VARS):
            put(new_below_ref, v, row(up_ref, v) + before[v])
            put(new_above_ref, v, row(above_ref, v) + after[v])


def call(kernel, shapes, *args, scratch=(), flops=100_000, limit=8, place=None):
    outs = [jax.ShapeDtypeStruct(shape, F32) for shape in shapes]
    moved = 4 * (sum(math.prod(shape) for shape in shapes) + sum(a.size for a in args))
    specs = [pl.BlockSpec(memory_space=pltpu.VMEM)] * len(args)
    if place is not None:
        specs.insert(0, pl.BlockSpec(memory_space=pltpu.SMEM))
        args = (place,) + args
    return pl.pallas_call(
        kernel,
        out_shape=outs,
        in_specs=specs,
        scratch_shapes=[pltpu.VMEM(shape, F32) for shape in scratch],
        cost_estimate=pl.CostEstimate(flops=flops, bytes_accessed=moved, transcendentals=0),
        compiler_params=pltpu.CompilerParams(vmem_limit_bytes=limit * 1024 * 1024),
    )(*args)


def exchange(value, axis, count):
    shape = value.shape
    out = lax.all_to_all(value.reshape(count, shape[0] // count, 128), axis, 0, 0)
    return out.reshape(shape)


def moved(value, axis, step, wrap):
    count = lax.axis_size(axis)
    pairs = [(i, (i + step) % count) for i in range(count) if wrap or 0 <= i + step < count]
    return lax.ppermute(value, axis, pairs)


def body(state, source_terms, pivot_inverse, coupling, back_coupling, wall_flags):
    weights = np.float32(-0.5 * spectral())
    place = lax.axis_index("axial").astype(jnp.int32).reshape(1)
    edge = (8, 128)
    halo = (VARS * 8, 128)
    carried = ((VARS + SIZE) * 8, 128)
    u, last_line, first_line, lines, maps, halos = call(
        maps_kernel,
        [
            (FIELD, 128), edge, edge, (2 * MATRIX + 3 * SIZE * 8, 128), (MAP_BLOCKS * 8, 128),
            (carried[0] + halo[0], 128),
        ],
        state[0].transpose(1, 0, 2), coupling[0].transpose(1, 2, 0, 3), back_coupling[0].transpose(1, 2, 0, 3),
        scratch=[(MATRIX, 128)],
        flops=8_000_000,
        limit=16,
    )
    maps = lax.all_gather(maps, "axial", axis=0, tiled=True)
    (cells,) = call(
        cells_kernel,
        [(FIELD + STEPS * 8 + MATRIX, 128)],
        source_terms[0].transpose(1, 0, 2), wall_flags, pivot_inverse[0].transpose(1, 2, 0, 3),
    )
    for sweep in range(SWEEPS):
        spread = exchange(u, "inst", INST)
        left = moved(last_line, "span", 1, True)
        if sweep == 0:
            right = moved(first_line, "span", -1, True)
            term, up, above = call(
                lambda a, b, c, *refs: time_kernel(weights, a, b, c, *refs),
                [(FIELD, 128), carried, halo], spread, jnp.concatenate([left, right]), halos,
            )
            up = moved(up, "axial", 1, False)
            above = moved(above, "axial", -1, False)
            below = up[: VARS * 8]
        else:
            term, right = call(
                lambda *refs: time_kernel(weights, *refs), [(FIELD, 128), edge], spread, left, first_line
            )
            right = moved(right, "span", -1, True)
        time = exchange(term, "inst", INST)
        (base,) = call(stencil_kernel, [(FIELD, 128)], u, cells, below, above, left, right)
        source, ends, packed = call(
            local_kernel, [(FIELD, 128), (2 * VARS * 8, 128), (VARS * 8, 128)], base, time, cells, lines
        )
        gathered = lax.all_gather(packed, "axial", axis=0, tiled=True)
        last = sweep == SWEEPS - 1
        common = (gathered, maps, u, source, ends, lines)
        entries = (SEGMENTS * VARS * 8, 128)
        if last:
            (result,) = call(
                lambda *refs: finish_kernel(True, *refs), [(VARS, 2 * STEPS, TILES * 128)], *common,
                scratch=[(FIELD, 128), entries], place=place,
            )
        else:
            u, last_line, first_line, below, above = call(
                lambda *refs: finish_kernel(False, *refs), [(FIELD, 128), edge, edge, halo, halo],
                *common, up, above, scratch=[entries], place=place,
            )
    return result.transpose(1, 0, 2)[None]


def solution(mesh):
    return jax.shard_map(
        body,
        mesh=mesh,
        in_specs=(
            P("inst", "axial", None, "span"),
            P("inst", "axial", None, "span"),
            P("inst", "axial", None, None, "span"),
            P("inst", "axial", None, None, "span"),
            P("inst", "axial", None, None, "span"),
            P("axial", "span"),
        ),
        out_specs=P("inst", "axial", None, "span"),
        check_vma=False,
    )
```

```python
import math

import jax
import jax.numpy as jnp
import numpy as np
from jax import lax
from jax.experimental import pallas as pl
from jax.experimental.pallas import tpu as pltpu
from jax.sharding import PartitionSpec as P

INST = 8
SWEEPS = 2
VARS = 5
STEPS = 8
TILES = 4
SEGMENTS = 16
F32 = jnp.float32
FIELD = STEPS * VARS * 8
MATRIX = STEPS * VARS * VARS * 8
SIZE = VARS * VARS
FULL_GROUPS = 24
VEC_GROUPS = 4
PACKED = 2 * MATRIX + 3 * SIZE * 8


def spectral():
    index = np.arange(INST)
    diff = index[:, None] - index[None, :]
    sign = 1.0 - 2.0 * np.mod(diff, 2)
    safe = np.where(diff == 0, 0.5 * math.pi, math.pi * diff / INST)
    first = np.where(diff == 0, 0.0, 0.5 * sign * np.cos(safe) / np.sin(safe))
    second = np.where(diff == 0, -(INST * INST + 2.0) / 12.0, -0.5 * sign / np.sin(safe) ** 2)
    return first - 0.5 * second


def iotas():
    sub = lax.broadcasted_iota(jnp.int32, (8, 128), 0)
    lane = lax.broadcasted_iota(jnp.int32, (8, 128), 1)
    return sub, lane


def row(ref, index):
    return ref[pl.ds(pl.multiple_of(index * 8, 8), 8), :]


def rows(ref, start, count):
    return [row(ref, start + n) for n in range(count)]


def put(ref, index, value):
    ref[pl.ds(pl.multiple_of(index * 8, 8), 8), :] = value


def total(terms):
    terms = list(terms)
    while len(terms) > 1:
        terms = [terms[n] + terms[n + 1] if n + 1 < len(terms) else terms[n] for n in range(0, len(terms), 2)]
    return terms[0]


def matvec(m, v):
    return [total(m[i * VARS + j] * v[j] for j in range(VARS)) for i in range(VARS)]


def matmul(a, b):
    return [
        total(a[i * VARS + j] * b[j * VARS + m] for j in range(VARS))
        for i in range(VARS)
        for m in range(VARS)
    ]


def plus(a, b):
    return [x + y for x, y in zip(a, b)]


def minus(a, b):
    return [x - y for x, y in zip(a, b)]


def swap(a):
    return [pltpu.roll(x, 4, 0) for x in a]


def pick(mask, a, b):
    return [jnp.where(mask, x, y) for x, y in zip(a, b)]


def lane_roll(x, shift):
    shift = shift % 128
    return x if shift == 0 else pltpu.roll(x, shift, 1)


def blocks4(block, parts):
    out = parts[0]
    for p in range(1, 4):
        out = jnp.where(block == p, parts[p], out)
    return out


def blocks4(block, parts):
    out = parts[0]
    for p in range(1, 4):
        out = jnp.where(block == p, parts[p], out)
    return out


def pack_lines(out_ref, start, block, values, first, groups):
    for g in range((len(values) + 3) // 4):
        four = [values[min(4 * g + p, len(values) - 1)] for p in range(4)]
        for q in range(4):
            chunk = blocks4(block, [lane_roll(four[p], 32 * (p - q)) for p in range(4)])
            out_ref[pl.ds(start + q * groups + first + g, 4, stride=4 * groups), :] = chunk[:4]


def edge_lines(sub, lane, u, edges_ref):
    last = jnp.zeros((8, 128), F32)
    initial = jnp.zeros((8, 128), F32)
    for n in range(STEPS * VARS):
        last = jnp.where(lane == n, lane_roll(u[n], n - 127), last)
        initial = jnp.where(lane == n, lane_roll(u[n], n), initial)
    put(edges_ref, 0, pltpu.roll(last, 5, 0))
    put(edges_ref, 1, pltpu.roll(initial, 3, 0))


def field_to_packed(raw_ref, out_ref, start=0):
    for v in range(VARS):
        for half in range(2):
            for t in range(TILES):
                tile = raw_ref[v, half * STEPS : (half + 1) * STEPS, t * 128 : (t + 1) * 128]
                out_ref[pl.ds(start + v * 8 + half * TILES + t, STEPS, stride=VARS * 8), :] = tile


def matrix_to_packed(raw_ref, out_ref, start=0):
    for i in range(VARS):
        for j in range(VARS):
            for half in range(2):
                for t in range(TILES):
                    tile = raw_ref[i, j, half * STEPS : (half + 1) * STEPS, t * 128 : (t + 1) * 128]
                    begin = start + (i * VARS + j) * 8 + half * TILES + t
                    out_ref[pl.ds(begin, STEPS, stride=SIZE * 8), :] = tile


def pack_kernel(state_ref, u_ref, edges_ref):
    sub, lane = iotas()
    field_to_packed(state_ref, u_ref)
    edge_lines(sub, lane, rows(u_ref, 0, STEPS * VARS), edges_ref)


def maps_kernel(u_ref, coupling_raw, back_raw, lines_ref, up_ref, down_ref, prefix_ref):
    sub, lane = iotas()
    block = lane // 32
    matrix_to_packed(coupling_raw, lines_ref, 0)
    matrix_to_packed(back_raw, lines_ref, MATRIX)

    def coupling(k):
        return rows(lines_ref, k * SIZE, SIZE)

    def back(k):
        return rows(lines_ref, STEPS * SIZE + k * SIZE, SIZE)

    def forward(k, p):
        p = [-x for x in matmul(coupling(k), p)]
        for n in range(SIZE):
            put(prefix_ref, k * SIZE + n, p[n])
        return p

    first = [-x for x in coupling(0)]
    for n in range(SIZE):
        put(prefix_ref, n, first[n])
    ahead = lax.fori_loop(1, STEPS, forward, first)

    def backward(step, carry):
        k = STEPS - 2 - step
        return minus(rows(prefix_ref, k * SIZE, SIZE), matmul(back(k), carry))

    mixed = lax.fori_loop(0, STEPS - 1, backward, ahead)

    def behind_step(step, carry):
        return [-x for x in matmul(back(STEPS - 2 - step), carry)]

    behind = lax.fori_loop(0, STEPS - 1, behind_step, [-x for x in back(STEPS - 1)])
    base = 2 * STEPS * SIZE
    for n in range(SIZE):
        put(lines_ref, base + n, ahead[n])
        put(lines_ref, base + SIZE + n, mixed[n])
        put(lines_ref, base + 2 * SIZE + n, behind[n])
    whole = matmul(swap(ahead), ahead)
    for n in range(SIZE):
        put(prefix_ref, n, whole[n])
    whole = plus(mixed, matmul(behind, matmul(swap(mixed), ahead)))
    for n in range(SIZE):
        put(prefix_ref, SIZE + n, whole[n])
    whole = matmul(behind, swap(behind))
    for n in range(SIZE):
        put(prefix_ref, 2 * SIZE + n, whole[n])
    pack_lines(lines_ref, PACKED, block, rows(prefix_ref, 0, 3 * SIZE), VEC_GROUPS, FULL_GROUPS)
    up_ref[: VARS * 8, :] = u_ref[(STEPS - 1) * VARS * 8 :, :]
    up_ref[VARS * 8 :, :] = lines_ref[2 * MATRIX - SIZE * 8 : 2 * MATRIX, :]
    down_ref[...] = u_ref[: VARS * 8, :]


def cells_kernel(source_ref, flags_ref, pivot_raw, out_ref):
    field_to_packed(source_ref, out_ref, 0)
    for half in range(2):
        for t in range(TILES):
            flags = flags_ref[half * STEPS : (half + 1) * STEPS, t * 128 : (t + 1) * 128]
            out_ref[pl.ds(FIELD + half * TILES + t, STEPS, stride=8), :] = (1 - flags).astype(F32)
    matrix_to_packed(pivot_raw, out_ref, FIELD + STEPS * 8)


def time_kernel(weights, u_ref, *rest):
    for v in range(VARS):
        fields = [row(u_ref, j * VARS + v) for j in range(INST)]
        for i in range(INST):
            put(rest[2], i * VARS + v, total(fields[j] * F32(weights[i, j]) for j in range(INST)))
    if len(rest) > 3:
        edges_ref, last_ref, first_ref = rest[3:]
        last_ref[...] = row(edges_ref, 0)
        first_ref[...] = row(edges_ref, 1)


def stencil_kernel(u_ref, src_ref, below_ref, above_ref, left_ref, right_ref, out_ref):
    sub, lane = iotas()
    top = sub < TILES
    left_all = left_ref[...]
    right_all = right_ref[...]
    for k in range(STEPS):
        for v in range(VARS):
            n = k * VARS + v
            u = row(u_ref, n)
            if k == 0:
                below = pltpu.roll(jnp.where(top, row(u_ref, (STEPS - 1) * VARS + v), row(below_ref, v)), 4, 0)
            else:
                below = row(u_ref, n - VARS)
            if k == STEPS - 1:
                above = pltpu.roll(jnp.where(top, row(above_ref, v), row(u_ref, v)), 4, 0)
            else:
                above = row(u_ref, n + VARS)
            turned = pltpu.roll(u, 1, 1)
            edge = jnp.where(sub % TILES == 0, lane_roll(left_all, -n), pltpu.roll(turned, 1, 0))
            left = jnp.where(lane == 0, edge, turned)
            turned = pltpu.roll(u, 127, 1)
            edge = jnp.where(sub % TILES == TILES - 1, lane_roll(right_all, 127 - n), pltpu.roll(turned, 7, 0))
            right = jnp.where(lane == 127, edge, turned)
            value = row(src_ref, n) - 0.1 * above + 0.5 * below - 0.8 * u + 0.2 * (left + right)
            put(out_ref, n, value)


def local_kernel(base_ref, time_ref, cells_ref, lines_ref, source_ref, packed_ref):
    sub, lane = iotas()
    block = lane // 32
    groups = packed_ref.shape[0] // SEGMENTS
    if groups == FULL_GROUPS:
        packed_ref[...] = lines_ref[PACKED:, :]
    pivot_row = STEPS * VARS + STEPS

    def source_step(k, carry):
        keep = row(cells_ref, STEPS * VARS + k)
        rhs = [keep * (row(base_ref, k * VARS + v) + row(time_ref, k * VARS + v)) for v in range(VARS)]
        for v, value in enumerate(matvec(rows(cells_ref, pivot_row + k * SIZE, SIZE), rhs)):
            put(source_ref, k * VARS + v, value)
        return carry

    lax.fori_loop(0, STEPS, source_step, 0)
    y = rows(source_ref, 0, VARS)
    kept = [y]
    for k in range(1, STEPS):
        y = minus(rows(source_ref, k * VARS, VARS), matvec(rows(lines_ref, k * SIZE, SIZE), y))
        kept.append(y)
    end = y
    x = y
    for k in range(STEPS - 2, -1, -1):
        x = minus(kept[k], matvec(rows(lines_ref, (STEPS + k) * SIZE, SIZE), x))
    for v in range(VARS):
        put(source_ref, STEPS * VARS + v, end[v])
        put(source_ref, STEPS * VARS + VARS + v, x[v])
    base = 2 * STEPS * SIZE
    ahead = rows(lines_ref, base, SIZE)
    mixed = rows(lines_ref, base + SIZE, SIZE)
    behind = rows(lines_ref, base + 2 * SIZE, SIZE)
    whole_end = plus(swap(end), matvec(swap(ahead), end))
    inner = plus(swap(x), matvec(swap(mixed), end))
    whole_first = plus(x, matvec(behind, inner))
    values = whole_end + whole_first + [jnp.zeros((8, 128), F32)] * (4 * VEC_GROUPS - 2 * VARS)
    pack_lines(packed_ref, 0, block, values, 0, groups)


def shift_in(sub, values, entry):
    return [jnp.where(sub == 0, e, pltpu.roll(x, 1, 0)) for x, e in zip(values, entry)]


def shift_out(sub, values, entry):
    return [jnp.where(sub == 7, e, pltpu.roll(x, 7, 0)) for x, e in zip(values, entry)]


def reduced_kernel(first, recv_ref, maps_in_ref, out_ref, *rest):
    sub, lane = iotas()
    block = lane // 32
    groups = FULL_GROUPS if first else VEC_GROUPS

    def value(r, part):
        stacked = recv_ref[pl.ds(part * 8 * groups + r // 4, 8, stride=groups), :]
        return lane_roll(stacked, -32 * (r % 4))

    if first:
        maps_ref = rest[0]
        for r in range(3 * SIZE):
            for part in range(2):
                put(maps_ref, part * 3 * SIZE + r, value(4 * VEC_GROUPS + r, part))
    else:
        maps_ref = maps_in_ref
    zero = [jnp.zeros((8, 128), F32)] * VARS

    def solve(part, which, source, entry, shift):
        maps = rows(maps_ref, part * 3 * SIZE + which * SIZE, SIZE)

        def step(_, now):
            return plus(source, matvec(maps, shift(sub, now, entry)))

        out = lax.fori_loop(0, 7, step, plus(source, matvec(maps, shift(sub, zero, entry))))
        return out, shift(sub, out, entry)

    ends = [[value(r, part) for r in range(VARS)] for part in range(2)]
    firsts = [[value(VARS + r, part) for r in range(VARS)] for part in range(2)]
    out, low_entry = solve(0, 0, ends[0], zero, shift_in)
    out, high_entry = solve(1, 0, ends[1], [pltpu.roll(x, 1, 0) for x in out], shift_in)
    entries = [low_entry, high_entry]
    drive = [
        plus(firsts[part], matvec(rows(maps_ref, part * 3 * SIZE + SIZE, SIZE), entries[part])) for part in range(2)
    ]
    out, high_next = solve(1, 2, drive[1], zero, shift_out)
    out, low_next = solve(0, 2, drive[0], [pltpu.roll(x, 7, 0) for x in out], shift_out)
    nexts = [low_next, high_next]
    for part in range(2):
        values = entries[part] + nexts[part] + zero + zero[:1]
        for g in range(VEC_GROUPS):
            packed = blocks4(block, [lane_roll(values[4 * g + p], 32 * p) for p in range(4)])
            out_ref[pl.ds(part * 8 * VEC_GROUPS + g, 8, stride=VEC_GROUPS), :] = packed


def finish_kernel(last, recv_ref, u_ref, source_ref, lines_ref, *rest):
    if last:
        out_ref, new_ref = rest
    else:
        up_ref, above_ref, new_ref, edges_ref, new_below_ref, new_above_ref = rest
    sub, lane = iotas()
    block = lane // 32
    top = sub < TILES
    stacked = [
        [
            recv_ref[pl.ds(q * VEC_GROUPS + g, TILES, stride=4 * VEC_GROUPS), :]
            for g in range((2 * VARS + 3) // 4)
        ]
        for q in range(4)
    ]
    stacked = [[jnp.concatenate([x, x], axis=0) for x in line] for line in stacked]

    def value(r):
        return blocks4(block, [lane_roll(stacked[q][r // 4], 32 * (q - r % 4)) for q in range(4)])

    entry = [value(r) for r in range(VARS)]
    after = [value(VARS + r) for r in range(VARS)]
    base = 2 * STEPS * SIZE
    end = rows(source_ref, STEPS * VARS, VARS)
    begin = rows(source_ref, STEPS * VARS + VARS, VARS)
    middle = plus(end, matvec(rows(lines_ref, base, SIZE), entry))
    start = pick(top, entry, swap(middle))
    follow = plus(
        plus(begin, matvec(rows(lines_ref, base + SIZE, SIZE), start)),
        matvec(rows(lines_ref, base + 2 * SIZE, SIZE), after),
    )
    finish = pick(top, swap(follow), after)
    y = start
    kept = []
    for k in range(STEPS):
        y = minus(rows(source_ref, k * VARS, VARS), matvec(rows(lines_ref, k * SIZE, SIZE), y))
        kept.append(y)
    x = finish
    for k in range(STEPS - 1, -1, -1):
        x = minus(kept[k], matvec(rows(lines_ref, (STEPS + k) * SIZE, SIZE), x))
        for v in range(VARS):
            put(new_ref, k * VARS + v, row(u_ref, k * VARS + v) + x[v])
    if last:
        for v in range(VARS):
            for half in range(2):
                for t in range(TILES):
                    tile = new_ref[pl.ds(v * 8 + half * TILES + t, STEPS, stride=VARS * 8), :]
                    out_ref[v, half * STEPS : (half + 1) * STEPS, t * 128 : (t + 1) * 128] = tile
    else:
        edge_lines(sub, lane, rows(new_ref, 0, STEPS * VARS), edges_ref)
        before = minus(entry, matvec(rows(up_ref, VARS, SIZE), swap(x)))
        for v in range(VARS):
            put(new_below_ref, v, row(up_ref, v) + before[v])
            put(new_above_ref, v, row(above_ref, v) + after[v])


def call(kernel, shapes, *args, scratch=(), flops=100_000, limit=8):
    outs = [jax.ShapeDtypeStruct(shape, F32) for shape in shapes]
    moved = 4 * (sum(math.prod(shape) for shape in shapes) + sum(a.size for a in args))
    return pl.pallas_call(
        kernel,
        out_shape=outs,
        scratch_shapes=[pltpu.VMEM(shape, F32) for shape in scratch],
        cost_estimate=pl.CostEstimate(flops=flops, bytes_accessed=moved, transcendentals=0),
        compiler_params=pltpu.CompilerParams(vmem_limit_bytes=limit * 1024 * 1024),
    )(*args)


def exchange(value, axis, count):
    shape = value.shape
    out = lax.all_to_all(value.reshape(count, shape[0] // count, 128), axis, 0, 0)
    return out.reshape(shape)


def moved(value, axis, step, wrap):
    count = lax.axis_size(axis)
    pairs = [(i, (i + step) % count) for i in range(count) if wrap or 0 <= i + step < count]
    return lax.ppermute(value, axis, pairs)


def body(state, source_terms, pivot_inverse, coupling, back_coupling, wall_flags):
    weights = np.float32(-0.5 * spectral())
    edge = (8, 128)
    halo = (VARS * 8, 128)
    u, edges = call(pack_kernel, [(FIELD, 128), (16, 128)], state[0].transpose(1, 0, 2))
    lines, up, above = call(
        maps_kernel,
        [(PACKED + SEGMENTS * FULL_GROUPS, 128), ((VARS + SIZE) * 8, 128), halo],
        u, coupling[0].transpose(1, 2, 0, 3), back_coupling[0].transpose(1, 2, 0, 3),
        scratch=[(MATRIX, 128)],
        flops=8_000_000,
        limit=16,
    )
    (cells,) = call(
        cells_kernel,
        [(FIELD + STEPS * 8 + MATRIX, 128)],
        source_terms[0].transpose(1, 0, 2), wall_flags, pivot_inverse[0].transpose(1, 2, 0, 3),
    )
    time_call = lambda *refs: time_kernel(weights, *refs)
    for sweep in range(SWEEPS):
        first = sweep == 0
        last = sweep == SWEEPS - 1
        spread = exchange(u, "inst", INST)
        if first:
            up = moved(up, "axial", 1, False)
            above = moved(above, "axial", -1, False)
            below = up[: VARS * 8]
            term, left, right = call(
                lambda a, b, c, d, *outs: time_kernel(weights, a, b, c, outs[0], d, *outs[1:]),
                [(FIELD, 128), edge, edge], spread, up, above, edges,
            )
            left = moved(left, "span", 1, True)
            right = moved(right, "span", -1, True)
        else:
            left = moved(edges[:8], "span", 1, True)
            right = moved(edges[8:], "span", -1, True)
            (term,) = call(time_call, [(FIELD, 128)], spread, left, right)
        time = exchange(term, "inst", INST)
        (base,) = call(stencil_kernel, [(FIELD, 128)], u, cells, below, above, left, right)
        groups = FULL_GROUPS if first else VEC_GROUPS
        source, packed = call(
            local_kernel,
            [(FIELD + 2 * VARS * 8, 128), (SEGMENTS * groups, 128)],
            base, time, cells, lines,
        )
        recv = exchange(packed, "axial", SEGMENTS)
        shapes = [(SEGMENTS * VEC_GROUPS, 128)]
        if first:
            shapes.append((6 * SIZE * 8, 128))
        out = call(
            lambda *refs, f=first: reduced_kernel(f, *((refs[0], None) + refs[1:] if f else refs)),
            shapes, recv, *(() if first else (maps,)),
        )
        if first:
            maps = out[1]
        back_recv = exchange(out[0], "axial", SEGMENTS)
        common = (back_recv, u, source, lines)
        if last:
            (result,) = call(
                lambda *refs: finish_kernel(True, *refs), [(VARS, 2 * STEPS, TILES * 128)], *common,
                scratch=[(FIELD, 128)],
            )
        else:
            u, edges, below, above = call(
                lambda *refs: finish_kernel(False, *refs), [(FIELD, 128), (16, 128), halo, halo],
                *common, up, above,
            )
    return result.transpose(1, 0, 2)[None]


def solution(mesh):
    return jax.shard_map(
        body,
        mesh=mesh,
        in_specs=(
            P("inst", "axial", None, "span"),
            P("inst", "axial", None, "span"),
            P("inst", "axial", None, None, "span"),
            P("inst", "axial", None, None, "span"),
            P("inst", "axial", None, None, "span"),
            P("axial", "span"),
        ),
        out_specs=P("inst", "axial", None, "span"),
        check_vma=False,
    )
```

```python
import math

import jax
import jax.numpy as jnp
import numpy as np
from jax import lax
from jax.experimental import pallas as pl
from jax.experimental.pallas import tpu as pltpu
from jax.sharding import PartitionSpec as P

INST = 8
SWEEPS = 2
VARS = 5
STEPS = 8
TILES = 4
SEGMENTS = 16
F32 = jnp.float32
FIELD = STEPS * VARS * 8
MATRIX = STEPS * VARS * VARS * 8
SIZE = VARS * VARS
FULL_GROUPS = 24
VEC_GROUPS = 4
PACKED = 2 * MATRIX + 3 * SIZE * 8
CELLS = PACKED + SEGMENTS * FULL_GROUPS
KEEP = CELLS + FIELD
PIVOT = KEEP + STEPS * 8
LINES = PIVOT + MATRIX


def spectral():
    index = np.arange(INST)
    diff = index[:, None] - index[None, :]
    sign = 1.0 - 2.0 * np.mod(diff, 2)
    safe = np.where(diff == 0, 0.5 * math.pi, math.pi * diff / INST)
    first = np.where(diff == 0, 0.0, 0.5 * sign * np.cos(safe) / np.sin(safe))
    second = np.where(diff == 0, -(INST * INST + 2.0) / 12.0, -0.5 * sign / np.sin(safe) ** 2)
    return first - 0.5 * second


def iotas():
    sub = lax.broadcasted_iota(jnp.int32, (8, 128), 0)
    lane = lax.broadcasted_iota(jnp.int32, (8, 128), 1)
    return sub, lane


def row(ref, index):
    return ref[pl.ds(pl.multiple_of(index * 8, 8), 8), :]


def rows(ref, start, count):
    return [row(ref, start + n) for n in range(count)]


def put(ref, index, value):
    ref[pl.ds(pl.multiple_of(index * 8, 8), 8), :] = value


def total(terms):
    terms = list(terms)
    while len(terms) > 1:
        terms = [terms[n] + terms[n + 1] if n + 1 < len(terms) else terms[n] for n in range(0, len(terms), 2)]
    return terms[0]


def matvec(m, v):
    return [total(m[i * VARS + j] * v[j] for j in range(VARS)) for i in range(VARS)]


def matmul(a, b):
    return [
        total(a[i * VARS + j] * b[j * VARS + m] for j in range(VARS))
        for i in range(VARS)
        for m in range(VARS)
    ]


def plus(a, b):
    return [x + y for x, y in zip(a, b)]


def minus(a, b):
    return [x - y for x, y in zip(a, b)]


def swap(a):
    return [pltpu.roll(x, 4, 0) for x in a]


def pick(mask, a, b):
    return [jnp.where(mask, x, y) for x, y in zip(a, b)]


def lane_roll(x, shift):
    shift = shift % 128
    return x if shift == 0 else pltpu.roll(x, shift, 1)


def blocks4(block, parts):
    out = parts[0]
    for p in range(1, 4):
        out = jnp.where(block == p, parts[p], out)
    return out


def blocks4(block, parts):
    out = parts[0]
    for p in range(1, 4):
        out = jnp.where(block == p, parts[p], out)
    return out


def pack_lines(out_ref, start, block, values, first, groups):
    for g in range((len(values) + 3) // 4):
        four = [values[min(4 * g + p, len(values) - 1)] for p in range(4)]
        for q in range(4):
            chunk = blocks4(block, [lane_roll(four[p], 32 * (p - q)) for p in range(4)])
            out_ref[pl.ds(start + q * groups + first + g, 4, stride=4 * groups), :] = chunk[:4]


def edge_lines(sub, lane, u, edges_ref):
    last = jnp.zeros((8, 128), F32)
    initial = jnp.zeros((8, 128), F32)
    for n in range(STEPS * VARS):
        last = jnp.where(lane == n, lane_roll(u[n], n - 127), last)
        initial = jnp.where(lane == n, lane_roll(u[n], n), initial)
    put(edges_ref, 0, pltpu.roll(last, 5, 0))
    put(edges_ref, 1, pltpu.roll(initial, 3, 0))


def field_to_packed(raw_ref, out_ref, start=0):
    for v in range(VARS):
        for half in range(2):
            for t in range(TILES):
                tile = raw_ref[v, half * STEPS : (half + 1) * STEPS, t * 128 : (t + 1) * 128]
                out_ref[pl.ds(start + v * 8 + half * TILES + t, STEPS, stride=VARS * 8), :] = tile


def matrix_to_packed(raw_ref, out_ref, start=0):
    for i in range(VARS):
        for j in range(VARS):
            for half in range(2):
                for t in range(TILES):
                    tile = raw_ref[i, j, half * STEPS : (half + 1) * STEPS, t * 128 : (t + 1) * 128]
                    begin = start + (i * VARS + j) * 8 + half * TILES + t
                    out_ref[pl.ds(begin, STEPS, stride=SIZE * 8), :] = tile


def fetch(source, target, sems, first):
    copies = [pltpu.make_async_copy(source.at[i], target.at[i], sems.at[first + i]) for i in range(VARS)]
    for copy in copies:
        copy.start()
    return copies


def arrive(copies):
    for copy in copies:
        copy.wait()


def pack_kernel(state_hbm, sent_ref, u_ref, edges_ref, state_ref, sems):
    sub, lane = iotas()
    arrive(fetch(state_hbm, state_ref, sems, 0))
    field_to_packed(state_ref, u_ref)
    sent_ref[...] = u_ref[...]
    edge_lines(sub, lane, rows(u_ref, 0, STEPS * VARS), edges_ref)


def maps_kernel(
    u_ref, coupling_hbm, back_hbm, pivot_hbm, source_hbm, flags_hbm,
    lines_ref, halos_ref,
    prefix_ref, coupling_raw, back_raw, pivot_raw, source_raw, flags_ref, sems,
):
    sub, lane = iotas()
    block = lane // 32
    flags_copy = pltpu.make_async_copy(flags_hbm, flags_ref, sems.at[4 * VARS])
    coupling_copies = fetch(coupling_hbm, coupling_raw, sems, 0)
    back_copies = fetch(back_hbm, back_raw, sems, VARS)
    pivot_copies = fetch(pivot_hbm, pivot_raw, sems, 2 * VARS)
    source_copies = fetch(source_hbm, source_raw, sems, 3 * VARS)
    flags_copy.start()
    arrive(coupling_copies)
    matrix_to_packed(coupling_raw, lines_ref, 0)
    arrive(back_copies)
    matrix_to_packed(back_raw, lines_ref, MATRIX)

    def coupling(k):
        return rows(lines_ref, k * SIZE, SIZE)

    def back(k):
        return rows(lines_ref, STEPS * SIZE + k * SIZE, SIZE)

    def forward(k, p):
        p = [-x for x in matmul(coupling(k), p)]
        for n in range(SIZE):
            put(prefix_ref, k * SIZE + n, p[n])
        return p

    first = [-x for x in coupling(0)]
    for n in range(SIZE):
        put(prefix_ref, n, first[n])
    ahead = lax.fori_loop(1, STEPS, forward, first)

    def backward(step, carry):
        k = STEPS - 2 - step
        return minus(rows(prefix_ref, k * SIZE, SIZE), matmul(back(k), carry))

    mixed = lax.fori_loop(0, STEPS - 1, backward, ahead)

    def behind_step(step, carry):
        return [-x for x in matmul(back(STEPS - 2 - step), carry)]

    behind = lax.fori_loop(0, STEPS - 1, behind_step, [-x for x in back(STEPS - 1)])
    base = 2 * STEPS * SIZE
    for n in range(SIZE):
        put(lines_ref, base + n, ahead[n])
        put(lines_ref, base + SIZE + n, mixed[n])
        put(lines_ref, base + 2 * SIZE + n, behind[n])
    whole = matmul(swap(ahead), ahead)
    for n in range(SIZE):
        put(prefix_ref, n, whole[n])
    whole = plus(mixed, matmul(behind, matmul(swap(mixed), ahead)))
    for n in range(SIZE):
        put(prefix_ref, SIZE + n, whole[n])
    whole = matmul(behind, swap(behind))
    for n in range(SIZE):
        put(prefix_ref, 2 * SIZE + n, whole[n])
    pack_lines(lines_ref, PACKED, block, rows(prefix_ref, 0, 3 * SIZE), VEC_GROUPS, FULL_GROUPS)
    halos_ref[: VARS * 8, :] = u_ref[(STEPS - 1) * VARS * 8 :, :]
    halos_ref[VARS * 8 : (VARS + SIZE) * 8, :] = lines_ref[2 * MATRIX - SIZE * 8 : 2 * MATRIX, :]
    halos_ref[(VARS + SIZE) * 8 :, :] = u_ref[: VARS * 8, :]
    arrive(pivot_copies)
    matrix_to_packed(pivot_raw, lines_ref, PIVOT)
    arrive(source_copies)
    field_to_packed(source_raw, lines_ref, CELLS)
    flags_copy.wait()
    for half in range(2):
        for t in range(TILES):
            flags = flags_ref[half * STEPS : (half + 1) * STEPS, t * 128 : (t + 1) * 128]
            lines_ref[pl.ds(KEEP + half * TILES + t, STEPS, stride=8), :] = (1 - flags).astype(F32)


def time_kernel(weights, count, u_ref, *rest):
    out_ref = rest[count]
    for v in range(VARS):
        fields = [row(u_ref, j * VARS + v) for j in range(INST)]
        for i in range(INST):
            put(out_ref, i * VARS + v, total(fields[j] * F32(weights[i, j]) for j in range(INST)))
    outs = list(rest[count + 1 :])
    for ref in rest[:count]:
        begin = 0
        while begin < ref.shape[0]:
            out = outs.pop(0)
            out[...] = ref[begin : begin + out.shape[0], :]
            begin += out.shape[0]


def stencil_kernel(u_ref, lines_ref, below_ref, above_ref, left_ref, right_ref, out_ref):
    sub, lane = iotas()
    top = sub < TILES
    left_all = left_ref[...]
    right_all = right_ref[...]
    for k in range(STEPS):
        for v in range(VARS):
            n = k * VARS + v
            u = row(u_ref, n)
            if k == 0:
                below = pltpu.roll(jnp.where(top, row(u_ref, (STEPS - 1) * VARS + v), row(below_ref, v)), 4, 0)
            else:
                below = row(u_ref, n - VARS)
            if k == STEPS - 1:
                above = pltpu.roll(jnp.where(top, row(above_ref, v), row(u_ref, v)), 4, 0)
            else:
                above = row(u_ref, n + VARS)
            turned = pltpu.roll(u, 1, 1)
            edge = jnp.where(sub % TILES == 0, lane_roll(left_all, -n), pltpu.roll(turned, 1, 0))
            left = jnp.where(lane == 0, edge, turned)
            turned = pltpu.roll(u, 127, 1)
            edge = jnp.where(sub % TILES == TILES - 1, lane_roll(right_all, 127 - n), pltpu.roll(turned, 7, 0))
            right = jnp.where(lane == 127, edge, turned)
            value = row(lines_ref, CELLS // 8 + n) - 0.1 * above + 0.5 * below - 0.8 * u + 0.2 * (left + right)
            put(out_ref, n, value)


def local_kernel(base_ref, time_ref, lines_ref, source_ref, packed_ref):
    sub, lane = iotas()
    block = lane // 32
    groups = packed_ref.shape[0] // SEGMENTS
    if groups == FULL_GROUPS:
        packed_ref[...] = lines_ref[PACKED:CELLS, :]

    def source_step(k, carry):
        keep = row(lines_ref, KEEP // 8 + k)
        rhs = [keep * (row(base_ref, k * VARS + v) + row(time_ref, k * VARS + v)) for v in range(VARS)]
        for v, value in enumerate(matvec(rows(lines_ref, PIVOT // 8 + k * SIZE, SIZE), rhs)):
            put(source_ref, k * VARS + v, value)
        return carry

    lax.fori_loop(0, STEPS, source_step, 0)
    y = rows(source_ref, 0, VARS)
    kept = [y]
    for k in range(1, STEPS):
        y = minus(rows(source_ref, k * VARS, VARS), matvec(rows(lines_ref, k * SIZE, SIZE), y))
        kept.append(y)
    end = y
    x = y
    for k in range(STEPS - 2, -1, -1):
        x = minus(kept[k], matvec(rows(lines_ref, (STEPS + k) * SIZE, SIZE), x))
    for v in range(VARS):
        put(source_ref, STEPS * VARS + v, end[v])
        put(source_ref, STEPS * VARS + VARS + v, x[v])
    base = 2 * STEPS * SIZE
    ahead = rows(lines_ref, base, SIZE)
    mixed = rows(lines_ref, base + SIZE, SIZE)
    behind = rows(lines_ref, base + 2 * SIZE, SIZE)
    whole_end = plus(swap(end), matvec(swap(ahead), end))
    inner = plus(swap(x), matvec(swap(mixed), end))
    whole_first = plus(x, matvec(behind, inner))
    values = whole_end + whole_first + [jnp.zeros((8, 128), F32)] * (4 * VEC_GROUPS - 2 * VARS)
    pack_lines(packed_ref, 0, block, values, 0, groups)


def shift_in(sub, values, entry):
    return [jnp.where(sub == 0, e, pltpu.roll(x, 1, 0)) for x, e in zip(values, entry)]


def shift_out(sub, values, entry):
    return [jnp.where(sub == 7, e, pltpu.roll(x, 7, 0)) for x, e in zip(values, entry)]


def reduced_kernel(first, recv_ref, *rest):
    maps_recv_ref = recv_ref if first else rest[0]
    out_ref, maps_ref = rest[-2:]
    sub, lane = iotas()
    block = lane // 32

    def stacked(ref, groups, r, part):
        values = ref[pl.ds(part * 8 * groups + r // 4, 8, stride=groups), :]
        return lane_roll(values, -32 * (r % 4))

    def value(r, part):
        return stacked(recv_ref, FULL_GROUPS if first else VEC_GROUPS, r, part)

    for r in range(3 * SIZE):
        for part in range(2):
            put(maps_ref, part * 3 * SIZE + r, stacked(maps_recv_ref, FULL_GROUPS, 4 * VEC_GROUPS + r, part))
    zero = [jnp.zeros((8, 128), F32)] * VARS

    def solve(part, which, source, entry, shift):
        maps = rows(maps_ref, part * 3 * SIZE + which * SIZE, SIZE)

        def step(_, now):
            return plus(source, matvec(maps, shift(sub, now, entry)))

        out = lax.fori_loop(0, 7, step, plus(source, matvec(maps, shift(sub, zero, entry))))
        return out, shift(sub, out, entry)

    ends = [[value(r, part) for r in range(VARS)] for part in range(2)]
    firsts = [[value(VARS + r, part) for r in range(VARS)] for part in range(2)]
    out, low_entry = solve(0, 0, ends[0], zero, shift_in)
    out, high_entry = solve(1, 0, ends[1], [pltpu.roll(x, 1, 0) for x in out], shift_in)
    entries = [low_entry, high_entry]
    drive = [
        plus(firsts[part], matvec(rows(maps_ref, part * 3 * SIZE + SIZE, SIZE), entries[part])) for part in range(2)
    ]
    out, high_next = solve(1, 2, drive[1], zero, shift_out)
    out, low_next = solve(0, 2, drive[0], [pltpu.roll(x, 7, 0) for x in out], shift_out)
    nexts = [low_next, high_next]
    for part in range(2):
        values = entries[part] + nexts[part] + zero + zero[:1]
        for g in range(VEC_GROUPS):
            packed = blocks4(block, [lane_roll(values[4 * g + p], 32 * p) for p in range(4)])
            out_ref[pl.ds(part * 8 * VEC_GROUPS + g, 8, stride=VEC_GROUPS), :] = packed


def finish_kernel(last, recv_ref, u_ref, source_ref, lines_ref, *rest):
    if last:
        out_ref, new_ref = rest
    else:
        up_ref, above_ref, new_ref, edges_ref, new_below_ref, new_above_ref = rest
    sub, lane = iotas()
    block = lane // 32
    top = sub < TILES
    stacked = [
        [
            recv_ref[pl.ds(q * VEC_GROUPS + g, TILES, stride=4 * VEC_GROUPS), :]
            for g in range((2 * VARS + 3) // 4)
        ]
        for q in range(4)
    ]
    stacked = [[jnp.concatenate([x, x], axis=0) for x in line] for line in stacked]

    def value(r):
        return blocks4(block, [lane_roll(stacked[q][r // 4], 32 * (q - r % 4)) for q in range(4)])

    entry = [value(r) for r in range(VARS)]
    after = [value(VARS + r) for r in range(VARS)]
    base = 2 * STEPS * SIZE
    end = rows(source_ref, STEPS * VARS, VARS)
    begin = rows(source_ref, STEPS * VARS + VARS, VARS)
    middle = plus(end, matvec(rows(lines_ref, base, SIZE), entry))
    start = pick(top, entry, swap(middle))
    follow = plus(
        plus(begin, matvec(rows(lines_ref, base + SIZE, SIZE), start)),
        matvec(rows(lines_ref, base + 2 * SIZE, SIZE), after),
    )
    finish = pick(top, swap(follow), after)
    y = start
    kept = []
    for k in range(STEPS):
        y = minus(rows(source_ref, k * VARS, VARS), matvec(rows(lines_ref, k * SIZE, SIZE), y))
        kept.append(y)
    x = finish
    for k in range(STEPS - 1, -1, -1):
        x = minus(kept[k], matvec(rows(lines_ref, (STEPS + k) * SIZE, SIZE), x))
        for v in range(VARS):
            put(new_ref, k * VARS + v, row(u_ref, k * VARS + v) + x[v])
    if last:
        for v in range(VARS):
            for half in range(2):
                for t in range(TILES):
                    tile = new_ref[pl.ds(v * 8 + half * TILES + t, STEPS, stride=VARS * 8), :]
                    out_ref[v, half * STEPS : (half + 1) * STEPS, t * 128 : (t + 1) * 128] = tile
    else:
        edge_lines(sub, lane, rows(new_ref, 0, STEPS * VARS), edges_ref)
        before = minus(entry, matvec(rows(up_ref, VARS, SIZE), swap(x)))
        for v in range(VARS):
            put(new_below_ref, v, row(up_ref, v) + before[v])
            put(new_above_ref, v, row(above_ref, v) + after[v])


def call(kernel, shapes, *args, scratch=(), flops=100_000, limit=8, far=0):
    outs = [jax.ShapeDtypeStruct(shape, F32) for shape in shapes]
    moved = 4 * (sum(math.prod(shape) for shape in shapes) + sum(a.size for a in args))
    near = len(args) - far
    specs = [pl.BlockSpec(memory_space=pltpu.VMEM if n < near else pltpu.HBM) for n in range(len(args))]
    return pl.pallas_call(
        kernel,
        out_shape=outs,
        in_specs=specs,
        scratch_shapes=[pltpu.VMEM(item, F32) if isinstance(item, tuple) else item for item in scratch],
        cost_estimate=pl.CostEstimate(flops=flops, bytes_accessed=moved, transcendentals=0),
        compiler_params=pltpu.CompilerParams(vmem_limit_bytes=limit * 1024 * 1024),
    )(*args)


def exchange(value, axis, count):
    shape = value.shape
    out = lax.all_to_all(value.reshape(count, shape[0] // count, 128), axis, 0, 0)
    return out.reshape(shape)


def moved(value, axis, step, wrap):
    count = lax.axis_size(axis)
    pairs = [(i, (i + step) % count) for i in range(count) if wrap or 0 <= i + step < count]
    return lax.ppermute(value, axis, pairs)


def body(state, source_terms, pivot_inverse, coupling, back_coupling, wall_flags):
    weights = np.float32(-0.5 * spectral())
    edge = (8, 128)
    halo = (VARS * 8, 128)
    up_shape = ((VARS + SIZE) * 8, 128)
    raw_field = (VARS, 2 * STEPS, TILES * 128)
    raw_matrix = (VARS,) + raw_field
    sent, u, edges = call(
        pack_kernel, [(FIELD, 128), (FIELD, 128), (16, 128)], state[0].transpose(1, 0, 2),
        scratch=[raw_field, pltpu.SemaphoreType.DMA((VARS,))], far=1,
    )
    lines, halos = call(
        maps_kernel,
        [(LINES, 128), (up_shape[0] + halo[0], 128)],
        u, coupling[0].transpose(1, 2, 0, 3), back_coupling[0].transpose(1, 2, 0, 3),
        pivot_inverse[0].transpose(1, 2, 0, 3), source_terms[0].transpose(1, 0, 2), wall_flags,
        scratch=[
            (MATRIX, 128), raw_matrix, raw_matrix, raw_matrix, raw_field,
            pltpu.VMEM((2 * STEPS, TILES * 128), jnp.int32), pltpu.SemaphoreType.DMA((4 * VARS + 1,)),
        ],
        flops=8_000_000,
        limit=16,
        far=5,
    )
    for sweep in range(SWEEPS):
        first = sweep == 0
        last = sweep == SWEEPS - 1
        spread = exchange(sent, "inst", INST)
        if first:
            term, left, right, up, above = call(
                lambda *refs: time_kernel(weights, 2, *refs),
                [(FIELD, 128), edge, edge, up_shape, halo], spread, edges, halos,
            )
            up = moved(up, "axial", 1, False)
            above = moved(above, "axial", -1, False)
            below = up[: VARS * 8]
        else:
            term, left, right = call(
                lambda *refs: time_kernel(weights, 1, *refs), [(FIELD, 128), edge, edge], spread, edges
            )
        left = moved(left, "span", 1, True)
        right = moved(right, "span", -1, True)
        time = exchange(term, "inst", INST)
        (base,) = call(stencil_kernel, [(FIELD, 128)], u, lines, below, above, left, right)
        groups = FULL_GROUPS if first else VEC_GROUPS
        source, packed = call(
            local_kernel,
            [(FIELD + 2 * VARS * 8, 128), (SEGMENTS * groups, 128)],
            base, time, lines,
        )
        recv = exchange(packed, "axial", SEGMENTS)
        if first:
            maps_recv = recv
        (solved,) = call(
            lambda *refs, f=first: reduced_kernel(f, *refs),
            [(SEGMENTS * VEC_GROUPS, 128)], recv, *(() if first else (maps_recv,)),
            scratch=[(6 * SIZE * 8, 128)],
        )
        back_recv = exchange(solved, "axial", SEGMENTS)
        common = (back_recv, u, source, lines)
        if last:
            (result,) = call(
                lambda *refs: finish_kernel(True, *refs), [raw_field], *common, scratch=[(FIELD, 128)],
            )
        else:
            u, edges, below, above = call(
                lambda *refs: finish_kernel(False, *refs), [(FIELD, 128), (16, 128), halo, halo],
                *common, up, above,
            )
            sent = u
    return result.transpose(1, 0, 2)[None]


def solution(mesh):
    return jax.shard_map(
        body,
        mesh=mesh,
        in_specs=(
            P("inst", "axial", None, "span"),
            P("inst", "axial", None, "span"),
            P("inst", "axial", None, None, "span"),
            P("inst", "axial", None, None, "span"),
            P("inst", "axial", None, None, "span"),
            P("axial", "span"),
        ),
        out_specs=P("inst", "axial", None, "span"),
        check_vma=False,
    )
```

```python
import math

import jax
import jax.numpy as jnp
import numpy as np
from jax import lax
from jax.experimental import pallas as pl
from jax.experimental.pallas import tpu as pltpu
from jax.sharding import PartitionSpec as P

INST = 8
SWEEPS = 2
VARS = 5
STEPS = 8
TILES = 4
SEGMENTS = 16
F32 = jnp.float32
FIELD = STEPS * VARS * 8
MATRIX = STEPS * VARS * VARS * 8
SIZE = VARS * VARS
FULL_GROUPS = 24
VEC_GROUPS = 4
PACKED = 2 * MATRIX + 3 * SIZE * 8
PIVOT = PACKED
CELLS = PIVOT + MATRIX
LINES = CELLS + FIELD


def spectral():
    index = np.arange(INST)
    diff = index[:, None] - index[None, :]
    sign = 1.0 - 2.0 * np.mod(diff, 2)
    safe = np.where(diff == 0, 0.5 * math.pi, math.pi * diff / INST)
    first = np.where(diff == 0, 0.0, 0.5 * sign * np.cos(safe) / np.sin(safe))
    second = np.where(diff == 0, -(INST * INST + 2.0) / 12.0, -0.5 * sign / np.sin(safe) ** 2)
    return first - 0.5 * second


def iotas():
    sub = lax.broadcasted_iota(jnp.int32, (8, 128), 0)
    lane = lax.broadcasted_iota(jnp.int32, (8, 128), 1)
    return sub, lane


def row(ref, index):
    return ref[pl.ds(pl.multiple_of(index * 8, 8), 8), :]


def rows(ref, start, count):
    return [row(ref, start + n) for n in range(count)]


def put(ref, index, value):
    ref[pl.ds(pl.multiple_of(index * 8, 8), 8), :] = value


def total(terms):
    terms = list(terms)
    while len(terms) > 1:
        terms = [terms[n] + terms[n + 1] if n + 1 < len(terms) else terms[n] for n in range(0, len(terms), 2)]
    return terms[0]


def matvec(m, v):
    return [total(m[i * VARS + j] * v[j] for j in range(VARS)) for i in range(VARS)]


def matmul(a, b):
    return [
        total(a[i * VARS + j] * b[j * VARS + m] for j in range(VARS))
        for i in range(VARS)
        for m in range(VARS)
    ]


def plus(a, b):
    return [x + y for x, y in zip(a, b)]


def minus(a, b):
    return [x - y for x, y in zip(a, b)]


def swap(a):
    return [pltpu.roll(x, 4, 0) for x in a]


def pick(mask, a, b):
    return [jnp.where(mask, x, y) for x, y in zip(a, b)]


def lane_roll(x, shift):
    shift = shift % 128
    return x if shift == 0 else pltpu.roll(x, shift, 1)


def blocks4(block, parts):
    out = parts[0]
    for p in range(1, 4):
        out = jnp.where(block == p, parts[p], out)
    return out


def blocks4(block, parts):
    out = parts[0]
    for p in range(1, 4):
        out = jnp.where(block == p, parts[p], out)
    return out


def pack_lines(out_ref, start, block, values, first, groups):
    for g in range((len(values) + 3) // 4):
        four = [values[min(4 * g + p, len(values) - 1)] for p in range(4)]
        for q in range(4):
            chunk = blocks4(block, [lane_roll(four[p], 32 * (p - q)) for p in range(4)])
            out_ref[pl.ds(start + q * groups + first + g, 4, stride=4 * groups), :] = chunk[:4]


def edge_lines(sub, lane, u, edges_ref):
    last = jnp.zeros((8, 128), F32)
    initial = jnp.zeros((8, 128), F32)
    for n in range(STEPS * VARS):
        last = jnp.where(lane == n, lane_roll(u[n], n - 127), last)
        initial = jnp.where(lane == n, lane_roll(u[n], n), initial)
    put(edges_ref, 0, pltpu.roll(last, 5, 0))
    put(edges_ref, 1, pltpu.roll(initial, 3, 0))


def field_to_packed(raw_ref, out_ref, start=0):
    for v in range(VARS):
        for half in range(2):
            for t in range(TILES):
                tile = raw_ref[v, half * STEPS : (half + 1) * STEPS, t * 128 : (t + 1) * 128]
                out_ref[pl.ds(start + v * 8 + half * TILES + t, STEPS, stride=VARS * 8), :] = tile


def matrix_to_packed(raw_ref, out_ref, start=0):
    for i in range(VARS):
        for j in range(VARS):
            for half in range(2):
                for t in range(TILES):
                    tile = raw_ref[i, j, half * STEPS : (half + 1) * STEPS, t * 128 : (t + 1) * 128]
                    begin = start + (i * VARS + j) * 8 + half * TILES + t
                    out_ref[pl.ds(begin, STEPS, stride=SIZE * 8), :] = tile


def pack_kernel(state_ref, u_ref, edges_ref):
    sub, lane = iotas()
    field_to_packed(state_ref, u_ref)
    edge_lines(sub, lane, rows(u_ref, 0, STEPS * VARS), edges_ref)


def time_term(weights, u_ref, out_ref):
    for v in range(VARS):
        fields = [row(u_ref, j * VARS + v) for j in range(INST)]
        for i in range(INST):
            put(out_ref, i * VARS + v, total(fields[j] * F32(weights[i, j]) for j in range(INST)))


def time_kernel(weights, spread_ref, edges_ref, out_ref, last_ref, first_ref):
    time_term(weights, spread_ref, out_ref)
    last_ref[...] = row(edges_ref, 0)
    first_ref[...] = row(edges_ref, 1)


def maps_kernel(
    weights,
    spread_ref, edges_ref, u_ref, coupling_raw, back_raw, pivot_raw, source_raw, flags_ref,
    out_ref, last_ref, first_ref, up_ref, down_ref, lines_ref, packed_ref,
    prefix_ref, keep_ref,
):
    sub, lane = iotas()
    block = lane // 32
    time_kernel(weights, spread_ref, edges_ref, out_ref, last_ref, first_ref)
    matrix_to_packed(coupling_raw, lines_ref, 0)
    matrix_to_packed(back_raw, lines_ref, MATRIX)
    matrix_to_packed(pivot_raw, lines_ref, PIVOT)
    field_to_packed(source_raw, lines_ref, CELLS)
    for half in range(2):
        for t in range(TILES):
            flags = flags_ref[half * STEPS : (half + 1) * STEPS, t * 128 : (t + 1) * 128]
            keep_ref[pl.ds(half * TILES + t, STEPS, stride=8), :] = (1 - flags).astype(F32)

    def mask(k, carry):
        keep = row(keep_ref, k)
        for n in range(SIZE):
            put(lines_ref, PIVOT // 8 + k * SIZE + n, keep * row(lines_ref, PIVOT // 8 + k * SIZE + n))
        return carry

    lax.fori_loop(0, STEPS, mask, 0)

    def coupling(k):
        return rows(lines_ref, k * SIZE, SIZE)

    def back(k):
        return rows(lines_ref, STEPS * SIZE + k * SIZE, SIZE)

    def forward(k, p):
        p = [-x for x in matmul(coupling(k), p)]
        for n in range(SIZE):
            put(prefix_ref, k * SIZE + n, p[n])
        return p

    first = [-x for x in coupling(0)]
    for n in range(SIZE):
        put(prefix_ref, n, first[n])
    ahead = lax.fori_loop(1, STEPS, forward, first)

    def backward(step, carry):
        k = STEPS - 2 - step
        return minus(rows(prefix_ref, k * SIZE, SIZE), matmul(back(k), carry))

    mixed = lax.fori_loop(0, STEPS - 1, backward, ahead)

    def behind_step(step, carry):
        return [-x for x in matmul(back(STEPS - 2 - step), carry)]

    behind = lax.fori_loop(0, STEPS - 1, behind_step, [-x for x in back(STEPS - 1)])
    base = 2 * STEPS * SIZE
    for n in range(SIZE):
        put(lines_ref, base + n, ahead[n])
        put(lines_ref, base + SIZE + n, mixed[n])
        put(lines_ref, base + 2 * SIZE + n, behind[n])
    whole = matmul(swap(ahead), ahead)
    for n in range(SIZE):
        put(prefix_ref, n, whole[n])
    whole = plus(mixed, matmul(behind, matmul(swap(mixed), ahead)))
    for n in range(SIZE):
        put(prefix_ref, SIZE + n, whole[n])
    whole = matmul(behind, swap(behind))
    for n in range(SIZE):
        put(prefix_ref, 2 * SIZE + n, whole[n])
    pack_lines(packed_ref, 0, block, rows(prefix_ref, 0, 3 * SIZE), VEC_GROUPS, FULL_GROUPS)
    up_ref[: VARS * 8, :] = u_ref[(STEPS - 1) * VARS * 8 :, :]
    up_ref[VARS * 8 :, :] = lines_ref[2 * MATRIX - SIZE * 8 : 2 * MATRIX, :]
    down_ref[...] = u_ref[: VARS * 8, :]


def stencil(sub, lane, u_ref, lines_ref, below_ref, above_ref, left_ref, right_ref, time_ref, out_ref):
    top = sub < TILES
    left_all = left_ref[...]
    right_all = right_ref[...]
    for k in range(STEPS):
        for v in range(VARS):
            n = k * VARS + v
            u = row(u_ref, n)
            if k == 0:
                below = pltpu.roll(jnp.where(top, row(u_ref, (STEPS - 1) * VARS + v), row(below_ref, v)), 4, 0)
            else:
                below = row(u_ref, n - VARS)
            if k == STEPS - 1:
                above = pltpu.roll(jnp.where(top, row(above_ref, v), row(u_ref, v)), 4, 0)
            else:
                above = row(u_ref, n + VARS)
            turned = pltpu.roll(u, 1, 1)
            edge = jnp.where(sub % TILES == 0, lane_roll(left_all, -n), pltpu.roll(turned, 1, 0))
            left = jnp.where(lane == 0, edge, turned)
            turned = pltpu.roll(u, 127, 1)
            edge = jnp.where(sub % TILES == TILES - 1, lane_roll(right_all, 127 - n), pltpu.roll(turned, 7, 0))
            right = jnp.where(lane == 127, edge, turned)
            value = row(lines_ref, CELLS // 8 + n) - 0.1 * above + 0.5 * below - 0.8 * u + 0.2 * (left + right)
            put(out_ref, n, value + row(time_ref, n))


def local_kernel(
    time_ref, u_ref, lines_ref, below_ref, above_ref, left_ref, right_ref, *rest
):
    source_ref, packed_ref, rhs_ref = rest[-3:]
    sub, lane = iotas()
    block = lane // 32
    groups = VEC_GROUPS
    if len(rest) > 3:
        groups = FULL_GROUPS
        packed_ref[...] = rest[0][...]
    stencil(sub, lane, u_ref, lines_ref, below_ref, above_ref, left_ref, right_ref, time_ref, rhs_ref)

    def source_step(k, carry):
        rhs = rows(rhs_ref, k * VARS, VARS)
        for v, value in enumerate(matvec(rows(lines_ref, PIVOT // 8 + k * SIZE, SIZE), rhs)):
            put(source_ref, k * VARS + v, value)
        return carry

    lax.fori_loop(0, STEPS, source_step, 0)
    y = rows(source_ref, 0, VARS)
    kept = [y]
    for k in range(1, STEPS):
        y = minus(rows(source_ref, k * VARS, VARS), matvec(rows(lines_ref, k * SIZE, SIZE), y))
        kept.append(y)
    end = y
    x = y
    for k in range(STEPS - 2, -1, -1):
        x = minus(kept[k], matvec(rows(lines_ref, (STEPS + k) * SIZE, SIZE), x))
    for v in range(VARS):
        put(source_ref, STEPS * VARS + v, end[v])
        put(source_ref, STEPS * VARS + VARS + v, x[v])
    base = 2 * STEPS * SIZE
    ahead = rows(lines_ref, base, SIZE)
    mixed = rows(lines_ref, base + SIZE, SIZE)
    behind = rows(lines_ref, base + 2 * SIZE, SIZE)
    whole_end = plus(swap(end), matvec(swap(ahead), end))
    inner = plus(swap(x), matvec(swap(mixed), end))
    whole_first = plus(x, matvec(behind, inner))
    values = whole_end + whole_first + [jnp.zeros((8, 128), F32)] * (4 * VEC_GROUPS - 2 * VARS)
    pack_lines(packed_ref, 0, block, values, 0, groups)


def shift_in(sub, values, entry):
    return [jnp.where(sub == 0, e, pltpu.roll(x, 1, 0)) for x, e in zip(values, entry)]


def shift_out(sub, values, entry):
    return [jnp.where(sub == 7, e, pltpu.roll(x, 7, 0)) for x, e in zip(values, entry)]


def reduced_kernel(first, recv_ref, *rest):
    maps_recv_ref = recv_ref if first else rest[0]
    out_ref, maps_ref = rest[-2:]
    sub, lane = iotas()
    block = lane // 32

    def stacked(ref, groups, r, part):
        values = ref[pl.ds(part * 8 * groups + r // 4, 8, stride=groups), :]
        return lane_roll(values, -32 * (r % 4))

    def value(r, part):
        return stacked(recv_ref, FULL_GROUPS if first else VEC_GROUPS, r, part)

    for r in range(3 * SIZE):
        for part in range(2):
            put(maps_ref, part * 3 * SIZE + r, stacked(maps_recv_ref, FULL_GROUPS, 4 * VEC_GROUPS + r, part))
    zero = [jnp.zeros((8, 128), F32)] * VARS

    def solve(part, which, source, entry, shift):
        maps = rows(maps_ref, part * 3 * SIZE + which * SIZE, SIZE)

        def step(_, now):
            return plus(source, matvec(maps, shift(sub, now, entry)))

        out = lax.fori_loop(0, 7, step, plus(source, matvec(maps, shift(sub, zero, entry))))
        return out, shift(sub, out, entry)

    ends = [[value(r, part) for r in range(VARS)] for part in range(2)]
    firsts = [[value(VARS + r, part) for r in range(VARS)] for part in range(2)]
    out, low_entry = solve(0, 0, ends[0], zero, shift_in)
    out, high_entry = solve(1, 0, ends[1], [pltpu.roll(x, 1, 0) for x in out], shift_in)
    entries = [low_entry, high_entry]
    drive = [
        plus(firsts[part], matvec(rows(maps_ref, part * 3 * SIZE + SIZE, SIZE), entries[part])) for part in range(2)
    ]
    out, high_next = solve(1, 2, drive[1], zero, shift_out)
    out, low_next = solve(0, 2, drive[0], [pltpu.roll(x, 7, 0) for x in out], shift_out)
    nexts = [low_next, high_next]
    for part in range(2):
        values = entries[part] + nexts[part] + zero + zero[:1]
        for g in range(VEC_GROUPS):
            packed = blocks4(block, [lane_roll(values[4 * g + p], 32 * p) for p in range(4)])
            out_ref[pl.ds(part * 8 * VEC_GROUPS + g, 8, stride=VEC_GROUPS), :] = packed


def finish_kernel(last, recv_ref, u_ref, source_ref, lines_ref, *rest):
    if last:
        out_ref, new_ref = rest
    else:
        up_ref, above_ref, new_ref, edges_ref, new_below_ref, new_above_ref = rest
    sub, lane = iotas()
    block = lane // 32
    top = sub < TILES
    stacked = [
        [
            recv_ref[pl.ds(q * VEC_GROUPS + g, TILES, stride=4 * VEC_GROUPS), :]
            for g in range((2 * VARS + 3) // 4)
        ]
        for q in range(4)
    ]
    stacked = [[jnp.concatenate([x, x], axis=0) for x in line] for line in stacked]

    def value(r):
        return blocks4(block, [lane_roll(stacked[q][r // 4], 32 * (q - r % 4)) for q in range(4)])

    entry = [value(r) for r in range(VARS)]
    after = [value(VARS + r) for r in range(VARS)]
    base = 2 * STEPS * SIZE
    end = rows(source_ref, STEPS * VARS, VARS)
    begin = rows(source_ref, STEPS * VARS + VARS, VARS)
    middle = plus(end, matvec(rows(lines_ref, base, SIZE), entry))
    start = pick(top, entry, swap(middle))
    follow = plus(
        plus(begin, matvec(rows(lines_ref, base + SIZE, SIZE), start)),
        matvec(rows(lines_ref, base + 2 * SIZE, SIZE), after),
    )
    finish = pick(top, swap(follow), after)
    y = start
    kept = []
    for k in range(STEPS):
        y = minus(rows(source_ref, k * VARS, VARS), matvec(rows(lines_ref, k * SIZE, SIZE), y))
        kept.append(y)
    x = finish
    for k in range(STEPS - 1, -1, -1):
        x = minus(kept[k], matvec(rows(lines_ref, (STEPS + k) * SIZE, SIZE), x))
        for v in range(VARS):
            put(new_ref, k * VARS + v, row(u_ref, k * VARS + v) + x[v])
    if last:
        for v in range(VARS):
            for half in range(2):
                for t in range(TILES):
                    tile = new_ref[pl.ds(v * 8 + half * TILES + t, STEPS, stride=VARS * 8), :]
                    out_ref[v, half * STEPS : (half + 1) * STEPS, t * 128 : (t + 1) * 128] = tile
    else:
        edge_lines(sub, lane, rows(new_ref, 0, STEPS * VARS), edges_ref)
        before = minus(entry, matvec(rows(up_ref, VARS, SIZE), swap(x)))
        for v in range(VARS):
            put(new_below_ref, v, row(up_ref, v) + before[v])
            put(new_above_ref, v, row(above_ref, v) + after[v])


def call(kernel, shapes, *args, scratch=(), flops=100_000, limit=8):
    outs = [jax.ShapeDtypeStruct(shape, F32) for shape in shapes]
    moved = 4 * (sum(math.prod(shape) for shape in shapes) + sum(a.size for a in args))
    return pl.pallas_call(
        kernel,
        out_shape=outs,
        scratch_shapes=[pltpu.VMEM(shape, F32) for shape in scratch],
        cost_estimate=pl.CostEstimate(flops=flops, bytes_accessed=moved, transcendentals=0),
        compiler_params=pltpu.CompilerParams(vmem_limit_bytes=limit * 1024 * 1024),
    )(*args)


def exchange(value, axis, count):
    shape = value.shape
    out = lax.all_to_all(value.reshape(count, shape[0] // count, 128), axis, 0, 0)
    return out.reshape(shape)


def moved(value, axis, step, wrap):
    count = lax.axis_size(axis)
    pairs = [(i, (i + step) % count) for i in range(count) if wrap or 0 <= i + step < count]
    return lax.ppermute(value, axis, pairs)


def body(state, source_terms, pivot_inverse, coupling, back_coupling, wall_flags):
    weights = np.float32(-0.5 * spectral())
    edge = (8, 128)
    halo = (VARS * 8, 128)
    raw_field = (VARS, 2 * STEPS, TILES * 128)
    u, edges = call(pack_kernel, [(FIELD, 128), (16, 128)], state[0].transpose(1, 0, 2))
    for sweep in range(SWEEPS):
        first = sweep == 0
        last = sweep == SWEEPS - 1
        spread = exchange(u, "inst", INST)
        if first:
            term, left, right, up, above, lines, packed_maps = call(
                lambda *refs: maps_kernel(weights, *refs),
                [
                    (FIELD, 128), edge, edge, ((VARS + SIZE) * 8, 128), halo, (LINES, 128),
                    (SEGMENTS * FULL_GROUPS, 128),
                ],
                spread, edges, u,
                coupling[0].transpose(1, 2, 0, 3), back_coupling[0].transpose(1, 2, 0, 3),
                pivot_inverse[0].transpose(1, 2, 0, 3), source_terms[0].transpose(1, 0, 2), wall_flags,
                scratch=[(MATRIX, 128), (STEPS * 8, 128)],
                flops=8_000_000,
                limit=12,
            )
            up = moved(up, "axial", 1, False)
            above = moved(above, "axial", -1, False)
            below = up[: VARS * 8]
        else:
            term, left, right = call(
                lambda *refs: time_kernel(weights, *refs), [(FIELD, 128), edge, edge], spread, edges
            )
        left = moved(left, "span", 1, True)
        right = moved(right, "span", -1, True)
        time = exchange(term, "inst", INST)
        groups = FULL_GROUPS if first else VEC_GROUPS
        source, packed = call(
            local_kernel,
            [(FIELD + 2 * VARS * 8, 128), (SEGMENTS * groups, 128)],
            time, u, lines, below, above, left, right, *((packed_maps,) if first else ()),
            scratch=[(FIELD, 128)],
        )
        recv = exchange(packed, "axial", SEGMENTS)
        if first:
            maps_recv = recv
        (solved,) = call(
            lambda *refs, f=first: reduced_kernel(f, *refs),
            [(SEGMENTS * VEC_GROUPS, 128)], recv, *(() if first else (maps_recv,)),
            scratch=[(6 * SIZE * 8, 128)],
        )
        back_recv = exchange(solved, "axial", SEGMENTS)
        common = (back_recv, u, source, lines)
        if last:
            (result,) = call(
                lambda *refs: finish_kernel(True, *refs), [raw_field], *common, scratch=[(FIELD, 128)],
            )
        else:
            u, edges, below, above = call(
                lambda *refs: finish_kernel(False, *refs), [(FIELD, 128), (16, 128), halo, halo],
                *common, up, above,
            )
    return result.transpose(1, 0, 2)[None]


def solution(mesh):
    return jax.shard_map(
        body,
        mesh=mesh,
        in_specs=(
            P("inst", "axial", None, "span"),
            P("inst", "axial", None, "span"),
            P("inst", "axial", None, None, "span"),
            P("inst", "axial", None, None, "span"),
            P("inst", "axial", None, None, "span"),
            P("axial", "span"),
        ),
        out_specs=P("inst", "axial", None, "span"),
        check_vma=False,
    )
```

```python
import math

import jax
import jax.numpy as jnp
import numpy as np
from jax import lax
from jax.experimental import pallas as pl
from jax.experimental.pallas import tpu as pltpu
from jax.sharding import PartitionSpec as P

INST = 8
SWEEPS = 2
VARS = 5
STEPS = 8
TILES = 4
SEGMENTS = 16
F32 = jnp.float32
FIELD = STEPS * VARS * 8
MATRIX = STEPS * VARS * VARS * 8
SIZE = VARS * VARS
FULL_GROUPS = 24
VEC_GROUPS = 4
PACKED = 2 * MATRIX + 3 * SIZE * 8
PIVOT = PACKED
CELLS = PIVOT + MATRIX
LINES = CELLS + FIELD
UP = VARS * 8 + (SIZE + 1) // 2 * 8
BELOW = STEPS * VARS
ABOVE = BELOW + VARS


def spectral():
    index = np.arange(INST)
    diff = index[:, None] - index[None, :]
    sign = 1.0 - 2.0 * np.mod(diff, 2)
    safe = np.where(diff == 0, 0.5 * math.pi, math.pi * diff / INST)
    first = np.where(diff == 0, 0.0, 0.5 * sign * np.cos(safe) / np.sin(safe))
    second = np.where(diff == 0, -(INST * INST + 2.0) / 12.0, -0.5 * sign / np.sin(safe) ** 2)
    return first - 0.5 * second


def iotas():
    sub = lax.broadcasted_iota(jnp.int32, (8, 128), 0)
    lane = lax.broadcasted_iota(jnp.int32, (8, 128), 1)
    return sub, lane


def row(ref, index):
    return ref[pl.ds(pl.multiple_of(index * 8, 8), 8), :]


def rows(ref, start, count):
    return [row(ref, start + n) for n in range(count)]


def put(ref, index, value):
    ref[pl.ds(pl.multiple_of(index * 8, 8), 8), :] = value


def total(terms):
    terms = list(terms)
    while len(terms) > 1:
        terms = [terms[n] + terms[n + 1] if n + 1 < len(terms) else terms[n] for n in range(0, len(terms), 2)]
    return terms[0]


def matvec(m, v):
    return [total(m[i * VARS + j] * v[j] for j in range(VARS)) for i in range(VARS)]


def matmul(a, b):
    return [
        total(a[i * VARS + j] * b[j * VARS + m] for j in range(VARS))
        for i in range(VARS)
        for m in range(VARS)
    ]


def plus(a, b):
    return [x + y for x, y in zip(a, b)]


def minus(a, b):
    return [x - y for x, y in zip(a, b)]


def swap(a):
    return [pltpu.roll(x, 4, 0) for x in a]


def pick(mask, a, b):
    return [jnp.where(mask, x, y) for x, y in zip(a, b)]


def lane_roll(x, shift):
    shift = shift % 128
    return x if shift == 0 else pltpu.roll(x, shift, 1)


def blocks4(block, parts):
    out = parts[0]
    for p in range(1, 4):
        out = jnp.where(block == p, parts[p], out)
    return out


def blocks4(block, parts):
    out = parts[0]
    for p in range(1, 4):
        out = jnp.where(block == p, parts[p], out)
    return out


def pack_lines(out_ref, start, block, values, first, groups):
    for g in range((len(values) + 3) // 4):
        four = [values[min(4 * g + p, len(values) - 1)] for p in range(4)]
        for q in range(4):
            chunk = blocks4(block, [lane_roll(four[p], 32 * (p - q)) for p in range(4)])
            out_ref[pl.ds(start + q * groups + first + g, 4, stride=4 * groups), :] = chunk[:4]


def edge_lines(sub, lane, u, edges_ref):
    last = jnp.zeros((8, 128), F32)
    initial = jnp.zeros((8, 128), F32)
    for n in range(STEPS * VARS):
        last = jnp.where(lane == n, lane_roll(u[n], n - 127), last)
        initial = jnp.where(lane == n, lane_roll(u[n], n), initial)
    put(edges_ref, 0, pltpu.roll(last, 5, 0))
    put(edges_ref, 1, pltpu.roll(initial, 3, 0))


def field_to_packed(raw_ref, out_ref, start=0):
    for v in range(VARS):
        for half in range(2):
            for t in range(TILES):
                tile = raw_ref[v, half * STEPS : (half + 1) * STEPS, t * 128 : (t + 1) * 128]
                out_ref[pl.ds(start + v * 8 + half * TILES + t, STEPS, stride=VARS * 8), :] = tile


def matrix_to_packed(raw_ref, out_ref, start=0):
    for i in range(VARS):
        for j in range(VARS):
            for half in range(2):
                for t in range(TILES):
                    tile = raw_ref[i, j, half * STEPS : (half + 1) * STEPS, t * 128 : (t + 1) * 128]
                    begin = start + (i * VARS + j) * 8 + half * TILES + t
                    out_ref[pl.ds(begin, STEPS, stride=SIZE * 8), :] = tile


def fetch(source, target, sems, first):
    copies = [pltpu.make_async_copy(source.at[i], target.at[i], sems.at[first + i]) for i in range(VARS)]
    for copy in copies:
        copy.start()
    return copies


def arrive(copies):
    for copy in copies:
        copy.wait()


def pack_kernel(state_hbm, sent_ref, u_ref, edges_ref, state_ref, sems):
    sub, lane = iotas()
    arrive(fetch(state_hbm, state_ref, sems, 0))
    field_to_packed(state_ref, u_ref)
    sent_ref[...] = u_ref[...]
    edge_lines(sub, lane, rows(u_ref, 0, STEPS * VARS), edges_ref)


def time_kernel(weights, spread_ref, edges_ref, *rest):
    halos_ref = rest[0] if len(rest) > 3 else None
    out_ref, last_ref, first_ref = rest[-5:-2] if len(rest) > 3 else rest
    for v in range(VARS):
        fields = [row(spread_ref, j * VARS + v) for j in range(INST)]
        for i in range(INST):
            put(out_ref, i * VARS + v, total(fields[j] * F32(weights[i, j]) for j in range(INST)))
    last_ref[...] = row(edges_ref, 0)
    first_ref[...] = row(edges_ref, 1)
    if halos_ref is not None:
        up_ref, down_ref = rest[-2:]
        up_ref[...] = halos_ref[:UP, :]
        down_ref[...] = halos_ref[UP:, :]


def maps_kernel(
    u_ref, coupling_hbm, back_hbm, pivot_hbm, source_hbm, flags_hbm,
    halos_ref, lines_ref, packed_ref,
    prefix_ref, keep_ref, coupling_raw, back_raw, pivot_raw, source_raw, flags_ref, sems,
):
    sub, lane = iotas()
    block = lane // 32
    coupling_copies = fetch(coupling_hbm, coupling_raw, sems, 0)
    back_copies = fetch(back_hbm, back_raw, sems, VARS)
    pivot_copies = fetch(pivot_hbm, pivot_raw, sems, 2 * VARS)
    source_copies = fetch(source_hbm, source_raw, sems, 3 * VARS)
    flags_copy = pltpu.make_async_copy(flags_hbm, flags_ref, sems.at[4 * VARS])
    flags_copy.start()
    top = sub < TILES
    arrive(coupling_copies)
    matrix_to_packed(coupling_raw, lines_ref, 0)
    arrive(back_copies)
    matrix_to_packed(back_raw, lines_ref, MATRIX)
    arrive(pivot_copies)
    matrix_to_packed(pivot_raw, lines_ref, PIVOT)
    arrive(source_copies)
    field_to_packed(source_raw, lines_ref, CELLS)
    flags_copy.wait()
    for half in range(2):
        for t in range(TILES):
            flags = flags_ref[half * STEPS : (half + 1) * STEPS, t * 128 : (t + 1) * 128]
            keep_ref[pl.ds(half * TILES + t, STEPS, stride=8), :] = (1 - flags).astype(F32)

    def mask(k, carry):
        keep = row(keep_ref, k)
        for n in range(SIZE):
            put(lines_ref, PIVOT // 8 + k * SIZE + n, keep * row(lines_ref, PIVOT // 8 + k * SIZE + n))
        return carry

    lax.fori_loop(0, STEPS, mask, 0)

    def coupling(k):
        return rows(lines_ref, k * SIZE, SIZE)

    def back(k):
        return rows(lines_ref, STEPS * SIZE + k * SIZE, SIZE)

    def forward(k, p):
        p = [-x for x in matmul(coupling(k), p)]
        for n in range(SIZE):
            put(prefix_ref, k * SIZE + n, p[n])
        return p

    first = [-x for x in coupling(0)]
    for n in range(SIZE):
        put(prefix_ref, n, first[n])
    ahead = lax.fori_loop(1, STEPS, forward, first)

    def backward(step, carry):
        k = STEPS - 2 - step
        return minus(rows(prefix_ref, k * SIZE, SIZE), matmul(back(k), carry))

    mixed = lax.fori_loop(0, STEPS - 1, backward, ahead)

    def behind_step(step, carry):
        return [-x for x in matmul(back(STEPS - 2 - step), carry)]

    behind = lax.fori_loop(0, STEPS - 1, behind_step, [-x for x in back(STEPS - 1)])
    base = 2 * STEPS * SIZE
    for n in range(SIZE):
        put(lines_ref, base + n, ahead[n])
        put(lines_ref, base + SIZE + n, mixed[n])
        put(lines_ref, base + 2 * SIZE + n, behind[n])
    whole = matmul(swap(ahead), ahead)
    for n in range(SIZE):
        put(prefix_ref, n, whole[n])
    whole = plus(mixed, matmul(behind, matmul(swap(mixed), ahead)))
    for n in range(SIZE):
        put(prefix_ref, SIZE + n, whole[n])
    whole = matmul(behind, swap(behind))
    for n in range(SIZE):
        put(prefix_ref, 2 * SIZE + n, whole[n])
    pack_lines(packed_ref, 0, block, rows(prefix_ref, 0, 3 * SIZE), VEC_GROUPS, FULL_GROUPS)
    halos_ref[: VARS * 8, :] = u_ref[(STEPS - 1) * VARS * 8 :, :]
    last = back(STEPS - 1)
    for n in range(0, SIZE, 2):
        pair = jnp.where(top, pltpu.roll(last[n], 4, 0), last[min(n + 1, SIZE - 1)])
        put(halos_ref, VARS + n // 2, pair)
    halos_ref[UP:, :] = u_ref[: VARS * 8, :]


def stencil(
    sub, lane, u_ref, lines_ref, below_ref, below_at, above_ref, above_at, left_ref, right_ref, time_ref, out_ref
):
    top = sub < TILES
    left_all = left_ref[...]
    right_all = right_ref[...]
    for k in range(STEPS):
        for v in range(VARS):
            n = k * VARS + v
            u = row(u_ref, n)
            if k == 0:
                below = pltpu.roll(jnp.where(top, row(u_ref, (STEPS - 1) * VARS + v), row(below_ref, below_at + v)), 4, 0)
            else:
                below = row(u_ref, n - VARS)
            if k == STEPS - 1:
                above = pltpu.roll(jnp.where(top, row(above_ref, above_at + v), row(u_ref, v)), 4, 0)
            else:
                above = row(u_ref, n + VARS)
            turned = pltpu.roll(u, 1, 1)
            edge = jnp.where(sub % TILES == 0, lane_roll(left_all, -n), pltpu.roll(turned, 1, 0))
            left = jnp.where(lane == 0, edge, turned)
            turned = pltpu.roll(u, 127, 1)
            edge = jnp.where(sub % TILES == TILES - 1, lane_roll(right_all, 127 - n), pltpu.roll(turned, 7, 0))
            right = jnp.where(lane == 127, edge, turned)
            value = row(lines_ref, CELLS // 8 + n) - 0.1 * above + 0.5 * below - 0.8 * u + 0.2 * (left + right)
            put(out_ref, n, value + row(time_ref, n))


def local_kernel(time_ref, u_ref, lines_ref, left_ref, right_ref, *rest):
    sub, lane = iotas()
    block = lane // 32
    if len(rest) > 3:
        below_ref, above_ref, maps_hbm, source_ref, packed_ref, rhs_ref, sem = rest
        below_at, above_at, groups = 0, 0, FULL_GROUPS
        maps_copy = pltpu.make_async_copy(maps_hbm, packed_ref, sem)
        maps_copy.start()
    else:
        source_ref, packed_ref, rhs_ref = rest
        below_ref = above_ref = u_ref
        below_at, above_at, groups = BELOW, ABOVE, VEC_GROUPS
    stencil(
        sub, lane, u_ref, lines_ref, below_ref, below_at, above_ref, above_at, left_ref, right_ref, time_ref, rhs_ref
    )

    def source_step(k, carry):
        rhs = rows(rhs_ref, k * VARS, VARS)
        for v, value in enumerate(matvec(rows(lines_ref, PIVOT // 8 + k * SIZE, SIZE), rhs)):
            put(source_ref, k * VARS + v, value)
        return carry

    lax.fori_loop(0, STEPS, source_step, 0)
    y = rows(source_ref, 0, VARS)
    kept = [y]
    for k in range(1, STEPS):
        y = minus(rows(source_ref, k * VARS, VARS), matvec(rows(lines_ref, k * SIZE, SIZE), y))
        kept.append(y)
    end = y
    x = y
    for k in range(STEPS - 2, -1, -1):
        x = minus(kept[k], matvec(rows(lines_ref, (STEPS + k) * SIZE, SIZE), x))
    for v in range(VARS):
        put(source_ref, STEPS * VARS + v, end[v])
        put(source_ref, STEPS * VARS + VARS + v, x[v])
    base = 2 * STEPS * SIZE
    ahead = rows(lines_ref, base, SIZE)
    mixed = rows(lines_ref, base + SIZE, SIZE)
    behind = rows(lines_ref, base + 2 * SIZE, SIZE)
    whole_end = plus(swap(end), matvec(swap(ahead), end))
    inner = plus(swap(x), matvec(swap(mixed), end))
    whole_first = plus(x, matvec(behind, inner))
    values = whole_end + whole_first + [jnp.zeros((8, 128), F32)] * (4 * VEC_GROUPS - 2 * VARS)
    if groups == FULL_GROUPS:
        maps_copy.wait()
    pack_lines(packed_ref, 0, block, values, 0, groups)


def shift_in(sub, values, entry):
    return [jnp.where(sub == 0, e, pltpu.roll(x, 1, 0)) for x, e in zip(values, entry)]


def shift_out(sub, values, entry):
    return [jnp.where(sub == 7, e, pltpu.roll(x, 7, 0)) for x, e in zip(values, entry)]


def reduced_kernel(first, recv_ref, *rest):
    maps_recv_ref = recv_ref if first else rest[0]
    out_ref, maps_ref = rest[-2:]
    sub, lane = iotas()
    block = lane // 32

    def stacked(ref, groups, r, part):
        values = ref[pl.ds(part * 8 * groups + r // 4, 8, stride=groups), :]
        return lane_roll(values, -32 * (r % 4))

    def value(r, part):
        return stacked(recv_ref, FULL_GROUPS if first else VEC_GROUPS, r, part)

    for r in range(3 * SIZE):
        for part in range(2):
            put(maps_ref, part * 3 * SIZE + r, stacked(maps_recv_ref, FULL_GROUPS, 4 * VEC_GROUPS + r, part))
    zero = [jnp.zeros((8, 128), F32)] * VARS

    def solve(part, which, source, entry, shift):
        maps = rows(maps_ref, part * 3 * SIZE + which * SIZE, SIZE)

        def step(_, now):
            return plus(source, matvec(maps, shift(sub, now, entry)))

        out = lax.fori_loop(0, 7, step, plus(source, matvec(maps, shift(sub, zero, entry))))
        return out, shift(sub, out, entry)

    ends = [[value(r, part) for r in range(VARS)] for part in range(2)]
    firsts = [[value(VARS + r, part) for r in range(VARS)] for part in range(2)]
    out, low_entry = solve(0, 0, ends[0], zero, shift_in)
    out, high_entry = solve(1, 0, ends[1], [pltpu.roll(x, 1, 0) for x in out], shift_in)
    entries = [low_entry, high_entry]
    drive = [
        plus(firsts[part], matvec(rows(maps_ref, part * 3 * SIZE + SIZE, SIZE), entries[part])) for part in range(2)
    ]
    out, high_next = solve(1, 2, drive[1], zero, shift_out)
    out, low_next = solve(0, 2, drive[0], [pltpu.roll(x, 7, 0) for x in out], shift_out)
    nexts = [low_next, high_next]
    for part in range(2):
        values = entries[part] + nexts[part] + zero + zero[:1]
        for g in range(VEC_GROUPS):
            packed = blocks4(block, [lane_roll(values[4 * g + p], 32 * p) for p in range(4)])
            out_ref[pl.ds(part * 8 * VEC_GROUPS + g, 8, stride=VEC_GROUPS), :] = packed


def finish_kernel(last, recv_ref, u_ref, source_ref, lines_ref, *rest):
    if last:
        out_ref, new_ref = rest
    else:
        up_ref, above_ref, sent_ref, edges_ref, new_ref = rest
    sub, lane = iotas()
    block = lane // 32
    top = sub < TILES
    stacked = [
        [
            recv_ref[pl.ds(q * VEC_GROUPS + g, TILES, stride=4 * VEC_GROUPS), :]
            for g in range((2 * VARS + 3) // 4)
        ]
        for q in range(4)
    ]
    stacked = [[jnp.concatenate([x, x], axis=0) for x in line] for line in stacked]

    def value(r):
        return blocks4(block, [lane_roll(stacked[q][r // 4], 32 * (q - r % 4)) for q in range(4)])

    entry = [value(r) for r in range(VARS)]
    after = [value(VARS + r) for r in range(VARS)]
    base = 2 * STEPS * SIZE
    end = rows(source_ref, STEPS * VARS, VARS)
    begin = rows(source_ref, STEPS * VARS + VARS, VARS)
    middle = plus(end, matvec(rows(lines_ref, base, SIZE), entry))
    start = pick(top, entry, swap(middle))
    follow = plus(
        plus(begin, matvec(rows(lines_ref, base + SIZE, SIZE), start)),
        matvec(rows(lines_ref, base + 2 * SIZE, SIZE), after),
    )
    finish = pick(top, swap(follow), after)
    y = start
    kept = []
    for k in range(STEPS):
        y = minus(rows(source_ref, k * VARS, VARS), matvec(rows(lines_ref, k * SIZE, SIZE), y))
        kept.append(y)
    x = finish
    for k in range(STEPS - 1, -1, -1):
        x = minus(kept[k], matvec(rows(lines_ref, (STEPS + k) * SIZE, SIZE), x))
        for v in range(VARS):
            put(new_ref, k * VARS + v, row(u_ref, k * VARS + v) + x[v])
    if last:
        for v in range(VARS):
            for half in range(2):
                for t in range(TILES):
                    tile = new_ref[pl.ds(v * 8 + half * TILES + t, STEPS, stride=VARS * 8), :]
                    out_ref[v, half * STEPS : (half + 1) * STEPS, t * 128 : (t + 1) * 128] = tile
    else:
        edge_lines(sub, lane, rows(new_ref, 0, STEPS * VARS), edges_ref)
        pairs = rows(up_ref, VARS, (SIZE + 1) // 2)
        blocks = [pairs[n // 2] if n % 2 else pltpu.roll(pairs[n // 2], 4, 0) for n in range(SIZE)]
        before = minus(entry, matvec(blocks, swap(x)))
        for v in range(VARS):
            put(new_ref, BELOW + v, row(up_ref, v) + before[v])
            put(new_ref, ABOVE + v, row(above_ref, v) + after[v])
        sent_ref[...] = new_ref[:FIELD, :]


def call(kernel, shapes, *args, scratch=(), flops=100_000, limit=8, far=0, sent=()):
    outs = [pltpu.HBM(shape, F32) if n in sent else jax.ShapeDtypeStruct(shape, F32) for n, shape in enumerate(shapes)]
    moved = 4 * (sum(math.prod(shape) for shape in shapes) + sum(a.size for a in args))
    near = len(args) - far
    specs = [pl.BlockSpec(memory_space=pltpu.VMEM if n < near else pltpu.HBM) for n in range(len(args))]
    args = args[:near] + tuple(pltpu.with_memory_space_constraint(a, pltpu.HBM) for a in args[near:])
    return pl.pallas_call(
        kernel,
        out_shape=outs,
        in_specs=specs,
        out_specs=[pl.BlockSpec(memory_space=pltpu.VMEM)] * len(outs),
        scratch_shapes=[pltpu.VMEM(item, F32) if isinstance(item, tuple) else item for item in scratch],
        cost_estimate=pl.CostEstimate(flops=flops, bytes_accessed=moved, transcendentals=0),
        compiler_params=pltpu.CompilerParams(vmem_limit_bytes=limit * 1024 * 1024),
    )(*args)


def exchange(value, axis, count):
    shape = value.shape
    out = lax.all_to_all(value.reshape(count, shape[0] // count, 128), axis, 0, 0)
    return out.reshape(shape)


def moved(value, axis, step, wrap):
    count = lax.axis_size(axis)
    pairs = [(i, (i + step) % count) for i in range(count) if wrap or 0 <= i + step < count]
    return lax.ppermute(value, axis, pairs)


def body(state, source_terms, pivot_inverse, coupling, back_coupling, wall_flags):
    weights = np.float32(-0.5 * spectral())
    edge = (8, 128)
    halo = (VARS * 8, 128)
    raw_field = (VARS, 2 * STEPS, TILES * 128)
    raw_matrix = (VARS,) + raw_field
    sent, u, edges = call(
        pack_kernel, [(FIELD, 128), (FIELD, 128), (16, 128)], state[0].transpose(1, 0, 2),
        scratch=[raw_field, pltpu.SemaphoreType.DMA((VARS,))], far=1,
    )
    halos, lines, packed_maps = call(
        maps_kernel,
        [(UP + halo[0], 128), (LINES, 128), (SEGMENTS * FULL_GROUPS, 128)],
        u, coupling[0].transpose(1, 2, 0, 3), back_coupling[0].transpose(1, 2, 0, 3),
        pivot_inverse[0].transpose(1, 2, 0, 3), source_terms[0].transpose(1, 0, 2), wall_flags,
        scratch=[
            (MATRIX, 128), (STEPS * 8, 128), raw_matrix, raw_matrix, raw_matrix, raw_field,
            pltpu.VMEM((2 * STEPS, TILES * 128), jnp.int32), pltpu.SemaphoreType.DMA((4 * VARS + 1,)),
        ],
        flops=8_000_000,
        limit=16,
        far=5,
        sent=(2,),
    )
    for sweep in range(SWEEPS):
        first = sweep == 0
        last = sweep == SWEEPS - 1
        spread = exchange(sent, "inst", INST)
        term, left, right, *ends = call(
            lambda *refs: time_kernel(weights, *refs),
            [(FIELD, 128), edge, edge] + ([(UP, 128), halo] if first else []),
            spread, edges, *((halos,) if first else ()), sent=(0,),
        )
        if first:
            up = moved(ends[0], "axial", 1, False)
            above = moved(ends[1], "axial", -1, False)
        left = moved(left, "span", 1, True)
        right = moved(right, "span", -1, True)
        time = exchange(term, "inst", INST)
        groups = FULL_GROUPS if first else VEC_GROUPS
        source, packed = call(
            local_kernel,
            [(FIELD + 2 * VARS * 8, 128), (SEGMENTS * groups, 128)],
            time, u, lines, left, right, *((up, above, packed_maps) if first else ()),
            scratch=[(FIELD, 128)] + ([pltpu.SemaphoreType.DMA] if first else []), far=1 if first else 0,
        )
        recv = exchange(packed, "axial", SEGMENTS)
        if first:
            maps_recv = recv
        (solved,) = call(
            lambda *refs, f=first: reduced_kernel(f, *refs),
            [(SEGMENTS * VEC_GROUPS, 128)], recv, *(() if first else (maps_recv,)),
            scratch=[(6 * SIZE * 8, 128)],
        )
        back_recv = exchange(solved, "axial", SEGMENTS)
        common = (back_recv, u, source, lines)
        if last:
            (result,) = call(
                lambda *refs: finish_kernel(True, *refs), [raw_field], *common, scratch=[(FIELD, 128)],
            )
        else:
            sent, edges, u = call(
                lambda *refs: finish_kernel(False, *refs), [(FIELD, 128), (16, 128), (FIELD + 2 * halo[0], 128)],
                *common, up, above,
            )
    return result.transpose(1, 0, 2)[None]


def solution(mesh):
    return jax.shard_map(
        body,
        mesh=mesh,
        in_specs=(
            P("inst", "axial", None, "span"),
            P("inst", "axial", None, "span"),
            P("inst", "axial", None, None, "span"),
            P("inst", "axial", None, None, "span"),
            P("inst", "axial", None, None, "span"),
            P("axial", "span"),
        ),
        out_specs=P("inst", "axial", None, "span"),
        check_vma=False,
    )
```

```python
import math

import jax
import jax.numpy as jnp
import numpy as np
from jax import lax
from jax.experimental import pallas as pl
from jax.experimental.pallas import tpu as pltpu
from jax.sharding import PartitionSpec as P

INST = 8
SWEEPS = 2
VARS = 5
STEPS = 8
TILES = 4
SEGMENTS = 16
F32 = jnp.float32
FIELD = STEPS * VARS * 8
MATRIX = STEPS * VARS * VARS * 8
SIZE = VARS * VARS
FULL_GROUPS = 24
VEC_GROUPS = 4
PACKED = 2 * MATRIX + 3 * SIZE * 8
PIVOT = PACKED
CELLS = PIVOT + MATRIX
LINES = CELLS + FIELD
UP = VARS * 8 + (SIZE + 1) // 2 * 8
BELOW = STEPS * VARS
ABOVE = BELOW + VARS


def spectral():
    index = np.arange(INST)
    diff = index[:, None] - index[None, :]
    sign = 1.0 - 2.0 * np.mod(diff, 2)
    safe = np.where(diff == 0, 0.5 * math.pi, math.pi * diff / INST)
    first = np.where(diff == 0, 0.0, 0.5 * sign * np.cos(safe) / np.sin(safe))
    second = np.where(diff == 0, -(INST * INST + 2.0) / 12.0, -0.5 * sign / np.sin(safe) ** 2)
    return first - 0.5 * second


def iotas():
    sub = lax.broadcasted_iota(jnp.int32, (8, 128), 0)
    lane = lax.broadcasted_iota(jnp.int32, (8, 128), 1)
    return sub, lane


def row(ref, index):
    return ref[pl.ds(pl.multiple_of(index * 8, 8), 8), :]


def rows(ref, start, count):
    return [row(ref, start + n) for n in range(count)]


def put(ref, index, value):
    ref[pl.ds(pl.multiple_of(index * 8, 8), 8), :] = value


def total(terms):
    terms = list(terms)
    while len(terms) > 1:
        terms = [terms[n] + terms[n + 1] if n + 1 < len(terms) else terms[n] for n in range(0, len(terms), 2)]
    return terms[0]


def matvec(m, v):
    return [total(m[i * VARS + j] * v[j] for j in range(VARS)) for i in range(VARS)]


def matmul(a, b):
    return [
        total(a[i * VARS + j] * b[j * VARS + m] for j in range(VARS))
        for i in range(VARS)
        for m in range(VARS)
    ]


def plus(a, b):
    return [x + y for x, y in zip(a, b)]


def minus(a, b):
    return [x - y for x, y in zip(a, b)]


def swap(a):
    return [pltpu.roll(x, 4, 0) for x in a]


def pick(mask, a, b):
    return [jnp.where(mask, x, y) for x, y in zip(a, b)]


def lane_roll(x, shift):
    shift = shift % 128
    return x if shift == 0 else pltpu.roll(x, shift, 1)


def blocks4(block, parts):
    out = parts[0]
    for p in range(1, 4):
        out = jnp.where(block == p, parts[p], out)
    return out


def blocks4(block, parts):
    out = parts[0]
    for p in range(1, 4):
        out = jnp.where(block == p, parts[p], out)
    return out


def pack_lines(out_ref, start, block, values, first, groups):
    for g in range((len(values) + 3) // 4):
        four = [values[min(4 * g + p, len(values) - 1)] for p in range(4)]
        for q in range(4):
            chunk = blocks4(block, [lane_roll(four[p], 32 * (p - q)) for p in range(4)])
            out_ref[pl.ds(start + q * groups + first + g, 4, stride=4 * groups), :] = chunk[:4]


def edge_lines(sub, lane, u, last_ref, first_ref):
    last = jnp.zeros((8, 128), F32)
    initial = jnp.zeros((8, 128), F32)
    for n in range(STEPS * VARS):
        last = jnp.where(lane == n, lane_roll(u[n], n - 127), last)
        initial = jnp.where(lane == n, lane_roll(u[n], n), initial)
    last_ref[...] = pltpu.roll(last, 5, 0)
    first_ref[...] = pltpu.roll(initial, 3, 0)


def field_to_packed(raw_ref, out_ref, start=0):
    for v in range(VARS):
        for half in range(2):
            for t in range(TILES):
                tile = raw_ref[v, half * STEPS : (half + 1) * STEPS, t * 128 : (t + 1) * 128]
                out_ref[pl.ds(start + v * 8 + half * TILES + t, STEPS, stride=VARS * 8), :] = tile


def matrix_to_packed(raw_ref, out_ref, start=0):
    for i in range(VARS):
        for j in range(VARS):
            for half in range(2):
                for t in range(TILES):
                    tile = raw_ref[i, j, half * STEPS : (half + 1) * STEPS, t * 128 : (t + 1) * 128]
                    begin = start + (i * VARS + j) * 8 + half * TILES + t
                    out_ref[pl.ds(begin, STEPS, stride=SIZE * 8), :] = tile


def fetch(source, target, sems, first):
    copies = [pltpu.make_async_copy(source.at[i], target.at[i], sems.at[first + i]) for i in range(VARS)]
    for copy in copies:
        copy.start()
    return copies


def arrive(copies):
    for copy in copies:
        copy.wait()


def time_term(weights, spread_ref, out_ref):
    for v in range(VARS):
        fields = [row(spread_ref, j * VARS + v) for j in range(INST)]
        for i in range(INST):
            put(out_ref, i * VARS + v, total(fields[j] * F32(weights[i, j]) for j in range(INST)))


def time_kernel(weights, spread_ref, edges_ref, halos_ref, out_ref, last_ref, first_ref, up_ref, down_ref):
    time_term(weights, spread_ref, out_ref)
    last_ref[...] = row(edges_ref, 0)
    first_ref[...] = row(edges_ref, 1)
    up_ref[...] = halos_ref[:UP, :]
    down_ref[...] = halos_ref[UP:, :]


def late_time_kernel(weights, spread_ref, left_ref, line_ref, out_ref, first_ref):
    time_term(weights, spread_ref, out_ref)
    first_ref[...] = line_ref[...]


def maps_kernel(
    state_hbm, coupling_hbm, back_hbm, pivot_hbm, source_hbm, flags_hbm,
    u_ref, edges_ref, halos_ref, lines_ref, packed_ref,
    prefix_ref, keep_ref, state_raw, coupling_raw, back_raw, pivot_raw, source_raw, flags_ref, sems,
):
    sub, lane = iotas()
    block = lane // 32
    coupling_copies = fetch(coupling_hbm, coupling_raw, sems, 0)
    back_copies = fetch(back_hbm, back_raw, sems, VARS)
    pivot_copies = fetch(pivot_hbm, pivot_raw, sems, 2 * VARS)
    source_copies = fetch(source_hbm, source_raw, sems, 3 * VARS)
    state_copies = fetch(state_hbm, state_raw, sems, 4 * VARS)
    flags_copy = pltpu.make_async_copy(flags_hbm, flags_ref, sems.at[5 * VARS])
    flags_copy.start()
    top = sub < TILES
    arrive(coupling_copies)
    matrix_to_packed(coupling_raw, lines_ref, 0)
    arrive(back_copies)
    matrix_to_packed(back_raw, lines_ref, MATRIX)
    arrive(pivot_copies)
    matrix_to_packed(pivot_raw, lines_ref, PIVOT)
    arrive(source_copies)
    field_to_packed(source_raw, lines_ref, CELLS)
    arrive(state_copies)
    field_to_packed(state_raw, u_ref)
    edge_lines(sub, lane, rows(u_ref, 0, STEPS * VARS), edges_ref.at[:8], edges_ref.at[8:])
    flags_copy.wait()
    for half in range(2):
        for t in range(TILES):
            flags = flags_ref[half * STEPS : (half + 1) * STEPS, t * 128 : (t + 1) * 128]
            keep_ref[pl.ds(half * TILES + t, STEPS, stride=8), :] = (1 - flags).astype(F32)

    def mask(k, carry):
        keep = row(keep_ref, k)
        for n in range(SIZE):
            put(lines_ref, PIVOT // 8 + k * SIZE + n, keep * row(lines_ref, PIVOT // 8 + k * SIZE + n))
        return carry

    lax.fori_loop(0, STEPS, mask, 0)

    def coupling(k):
        return rows(lines_ref, k * SIZE, SIZE)

    def back(k):
        return rows(lines_ref, STEPS * SIZE + k * SIZE, SIZE)

    def forward(k, p):
        p = [-x for x in matmul(coupling(k), p)]
        for n in range(SIZE):
            put(prefix_ref, k * SIZE + n, p[n])
        return p

    first = [-x for x in coupling(0)]
    for n in range(SIZE):
        put(prefix_ref, n, first[n])
    ahead = lax.fori_loop(1, STEPS, forward, first)

    def backward(step, carry):
        k = STEPS - 2 - step
        return minus(rows(prefix_ref, k * SIZE, SIZE), matmul(back(k), carry))

    mixed = lax.fori_loop(0, STEPS - 1, backward, ahead)

    def behind_step(step, carry):
        return [-x for x in matmul(back(STEPS - 2 - step), carry)]

    behind = lax.fori_loop(0, STEPS - 1, behind_step, [-x for x in back(STEPS - 1)])
    base = 2 * STEPS * SIZE
    for n in range(SIZE):
        put(lines_ref, base + n, ahead[n])
        put(lines_ref, base + SIZE + n, mixed[n])
        put(lines_ref, base + 2 * SIZE + n, behind[n])
    whole = matmul(swap(ahead), ahead)
    for n in range(SIZE):
        put(prefix_ref, n, whole[n])
    whole = plus(mixed, matmul(behind, matmul(swap(mixed), ahead)))
    for n in range(SIZE):
        put(prefix_ref, SIZE + n, whole[n])
    whole = matmul(behind, swap(behind))
    for n in range(SIZE):
        put(prefix_ref, 2 * SIZE + n, whole[n])
    pack_lines(packed_ref, 0, block, rows(prefix_ref, 0, 3 * SIZE), VEC_GROUPS, FULL_GROUPS)
    halos_ref[: VARS * 8, :] = u_ref[(STEPS - 1) * VARS * 8 :, :]
    last = back(STEPS - 1)
    for n in range(0, SIZE, 2):
        pair = jnp.where(top, pltpu.roll(last[n], 4, 0), last[min(n + 1, SIZE - 1)])
        put(halos_ref, VARS + n // 2, pair)
    halos_ref[UP:, :] = u_ref[: VARS * 8, :]


def stencil(
    sub, lane, u_ref, lines_ref, below_ref, below_at, above_ref, above_at, left_ref, right_ref, time_ref, out_ref
):
    top = sub < TILES
    left_all = left_ref[...]
    right_all = right_ref[...]
    for k in range(STEPS):
        for v in range(VARS):
            n = k * VARS + v
            u = row(u_ref, n)
            if k == 0:
                below = pltpu.roll(jnp.where(top, row(u_ref, (STEPS - 1) * VARS + v), row(below_ref, below_at + v)), 4, 0)
            else:
                below = row(u_ref, n - VARS)
            if k == STEPS - 1:
                above = pltpu.roll(jnp.where(top, row(above_ref, above_at + v), row(u_ref, v)), 4, 0)
            else:
                above = row(u_ref, n + VARS)
            turned = pltpu.roll(u, 1, 1)
            edge = jnp.where(sub % TILES == 0, lane_roll(left_all, -n), pltpu.roll(turned, 1, 0))
            left = jnp.where(lane == 0, edge, turned)
            turned = pltpu.roll(u, 127, 1)
            edge = jnp.where(sub % TILES == TILES - 1, lane_roll(right_all, 127 - n), pltpu.roll(turned, 7, 0))
            right = jnp.where(lane == 127, edge, turned)
            value = row(lines_ref, CELLS // 8 + n) - 0.1 * above + 0.5 * below - 0.8 * u + 0.2 * (left + right)
            put(out_ref, n, value + row(time_ref, n))


def local_kernel(time_ref, u_ref, lines_ref, left_ref, right_ref, *rest):
    sub, lane = iotas()
    block = lane // 32
    if len(rest) > 3:
        below_ref, above_ref, maps_hbm, source_ref, packed_ref, rhs_ref, sem = rest
        below_at, above_at, groups = 0, 0, FULL_GROUPS
        maps_copy = pltpu.make_async_copy(maps_hbm, packed_ref, sem)
        maps_copy.start()
        for n in range(STEPS * VARS):
            v, tile = n // 8, n % 8
            rhs_ref[pl.ds(v * 8 + tile, STEPS, stride=VARS * 8), :] = row(time_ref, n)
        time_ref = rhs_ref
    else:
        source_ref, packed_ref, rhs_ref = rest
        below_ref = above_ref = u_ref
        below_at, above_at, groups = BELOW, ABOVE, VEC_GROUPS
    stencil(
        sub, lane, u_ref, lines_ref, below_ref, below_at, above_ref, above_at, left_ref, right_ref, time_ref, rhs_ref
    )

    def source_step(k, carry):
        rhs = rows(rhs_ref, k * VARS, VARS)
        for v, value in enumerate(matvec(rows(lines_ref, PIVOT // 8 + k * SIZE, SIZE), rhs)):
            put(source_ref, k * VARS + v, value)
        return carry

    lax.fori_loop(0, STEPS, source_step, 0)
    y = rows(source_ref, 0, VARS)
    kept = [y]
    for k in range(1, STEPS):
        y = minus(rows(source_ref, k * VARS, VARS), matvec(rows(lines_ref, k * SIZE, SIZE), y))
        kept.append(y)
    end = y
    x = y
    for k in range(STEPS - 2, -1, -1):
        x = minus(kept[k], matvec(rows(lines_ref, (STEPS + k) * SIZE, SIZE), x))
    for v in range(VARS):
        put(source_ref, STEPS * VARS + v, end[v])
        put(source_ref, STEPS * VARS + VARS + v, x[v])
    base = 2 * STEPS * SIZE
    ahead = rows(lines_ref, base, SIZE)
    mixed = rows(lines_ref, base + SIZE, SIZE)
    behind = rows(lines_ref, base + 2 * SIZE, SIZE)
    whole_end = plus(swap(end), matvec(swap(ahead), end))
    inner = plus(swap(x), matvec(swap(mixed), end))
    whole_first = plus(x, matvec(behind, inner))
    values = whole_end + whole_first + [jnp.zeros((8, 128), F32)] * (4 * VEC_GROUPS - 2 * VARS)
    if groups == FULL_GROUPS:
        maps_copy.wait()
    pack_lines(packed_ref, 0, block, values, 0, groups)


def shift_in(sub, values, entry):
    return [jnp.where(sub == 0, e, pltpu.roll(x, 1, 0)) for x, e in zip(values, entry)]


def shift_out(sub, values, entry):
    return [jnp.where(sub == 7, e, pltpu.roll(x, 7, 0)) for x, e in zip(values, entry)]


def reduced_kernel(first, recv_ref, *rest):
    maps_recv_ref = recv_ref if first else rest[0]
    out_ref, maps_ref = rest[-2:]
    sub, lane = iotas()
    block = lane // 32

    def stacked(ref, groups, r, part):
        values = ref[pl.ds(part * 8 * groups + r // 4, 8, stride=groups), :]
        return lane_roll(values, -32 * (r % 4))

    def value(r, part):
        return stacked(recv_ref, FULL_GROUPS if first else VEC_GROUPS, r, part)

    for r in range(3 * SIZE):
        for part in range(2):
            put(maps_ref, part * 3 * SIZE + r, stacked(maps_recv_ref, FULL_GROUPS, 4 * VEC_GROUPS + r, part))
    zero = [jnp.zeros((8, 128), F32)] * VARS

    def solve(part, which, source, entry, shift):
        maps = rows(maps_ref, part * 3 * SIZE + which * SIZE, SIZE)

        def step(_, now):
            return plus(source, matvec(maps, shift(sub, now, entry)))

        out = lax.fori_loop(0, 7, step, plus(source, matvec(maps, shift(sub, zero, entry))))
        return out, shift(sub, out, entry)

    ends = [[value(r, part) for r in range(VARS)] for part in range(2)]
    firsts = [[value(VARS + r, part) for r in range(VARS)] for part in range(2)]
    out, low_entry = solve(0, 0, ends[0], zero, shift_in)
    out, high_entry = solve(1, 0, ends[1], [pltpu.roll(x, 1, 0) for x in out], shift_in)
    entries = [low_entry, high_entry]
    drive = [
        plus(firsts[part], matvec(rows(maps_ref, part * 3 * SIZE + SIZE, SIZE), entries[part])) for part in range(2)
    ]
    out, high_next = solve(1, 2, drive[1], zero, shift_out)
    out, low_next = solve(0, 2, drive[0], [pltpu.roll(x, 7, 0) for x in out], shift_out)
    nexts = [low_next, high_next]
    for part in range(2):
        values = entries[part] + nexts[part] + zero + zero[:1]
        for g in range(VEC_GROUPS):
            packed = blocks4(block, [lane_roll(values[4 * g + p], 32 * p) for p in range(4)])
            out_ref[pl.ds(part * 8 * VEC_GROUPS + g, 8, stride=VEC_GROUPS), :] = packed


def finish_kernel(last, recv_ref, u_ref, source_ref, lines_ref, *rest):
    if last:
        out_ref, new_ref = rest
    else:
        above_ref, up_hbm, sent_ref, last_ref, first_ref, new_ref, up_ref, sem = rest
        up_copy = pltpu.make_async_copy(up_hbm, up_ref, sem)
        up_copy.start()
    sub, lane = iotas()
    block = lane // 32
    top = sub < TILES
    stacked = [
        [
            recv_ref[pl.ds(q * VEC_GROUPS + g, TILES, stride=4 * VEC_GROUPS), :]
            for g in range((2 * VARS + 3) // 4)
        ]
        for q in range(4)
    ]
    stacked = [[jnp.concatenate([x, x], axis=0) for x in line] for line in stacked]

    def value(r):
        return blocks4(block, [lane_roll(stacked[q][r // 4], 32 * (q - r % 4)) for q in range(4)])

    entry = [value(r) for r in range(VARS)]
    after = [value(VARS + r) for r in range(VARS)]
    base = 2 * STEPS * SIZE
    end = rows(source_ref, STEPS * VARS, VARS)
    begin = rows(source_ref, STEPS * VARS + VARS, VARS)
    middle = plus(end, matvec(rows(lines_ref, base, SIZE), entry))
    start = pick(top, entry, swap(middle))
    follow = plus(
        plus(begin, matvec(rows(lines_ref, base + SIZE, SIZE), start)),
        matvec(rows(lines_ref, base + 2 * SIZE, SIZE), after),
    )
    finish = pick(top, swap(follow), after)
    y = start
    kept = []
    for k in range(STEPS):
        y = minus(rows(source_ref, k * VARS, VARS), matvec(rows(lines_ref, k * SIZE, SIZE), y))
        kept.append(y)
    x = finish
    for k in range(STEPS - 1, -1, -1):
        x = minus(kept[k], matvec(rows(lines_ref, (STEPS + k) * SIZE, SIZE), x))
        for v in range(VARS):
            put(new_ref, k * VARS + v, row(u_ref, k * VARS + v) + x[v])
    if last:
        for v in range(VARS):
            for half in range(2):
                for t in range(TILES):
                    tile = new_ref[pl.ds(v * 8 + half * TILES + t, STEPS, stride=VARS * 8), :]
                    out_ref[v, half * STEPS : (half + 1) * STEPS, t * 128 : (t + 1) * 128] = tile
    else:
        edge_lines(sub, lane, rows(new_ref, 0, STEPS * VARS), last_ref, first_ref)
        up_copy.wait()
        pairs = rows(up_ref, VARS, (SIZE + 1) // 2)
        blocks = [pairs[n // 2] if n % 2 else pltpu.roll(pairs[n // 2], 4, 0) for n in range(SIZE)]
        before = minus(entry, matvec(blocks, swap(x)))
        for v in range(VARS):
            put(new_ref, BELOW + v, row(up_ref, v) + before[v])
            put(new_ref, ABOVE + v, row(above_ref, v) + after[v])
        sent_ref[...] = new_ref[:FIELD, :]


def call(kernel, shapes, *args, scratch=(), flops=100_000, limit=8, far=0, sent=()):
    outs = [pltpu.HBM(shape, F32) if n in sent else jax.ShapeDtypeStruct(shape, F32) for n, shape in enumerate(shapes)]
    moved = 4 * (sum(math.prod(shape) for shape in shapes) + sum(a.size for a in args))
    near = len(args) - far
    specs = [pl.BlockSpec(memory_space=pltpu.VMEM if n < near else pltpu.HBM) for n in range(len(args))]
    args = args[:near] + tuple(pltpu.with_memory_space_constraint(a, pltpu.HBM) for a in args[near:])
    return pl.pallas_call(
        kernel,
        out_shape=outs,
        in_specs=specs,
        out_specs=[pl.BlockSpec(memory_space=pltpu.VMEM)] * len(outs),
        scratch_shapes=[pltpu.VMEM(item, F32) if isinstance(item, tuple) else item for item in scratch],
        cost_estimate=pl.CostEstimate(flops=flops, bytes_accessed=moved, transcendentals=0),
        compiler_params=pltpu.CompilerParams(vmem_limit_bytes=limit * 1024 * 1024),
    )(*args)


def exchange(value, axis, count):
    shape = value.shape
    out = lax.all_to_all(value.reshape(count, shape[0] // count, 128), axis, 0, 0)
    return out.reshape(shape)


def moved(value, axis, step, wrap):
    count = lax.axis_size(axis)
    pairs = [(i, (i + step) % count) for i in range(count) if wrap or 0 <= i + step < count]
    return lax.ppermute(value, axis, pairs)


def body(state, source_terms, pivot_inverse, coupling, back_coupling, wall_flags):
    weights = np.float32(-0.5 * spectral())
    edge = (8, 128)
    halo = (VARS * 8, 128)
    raw_field = (VARS, 2 * STEPS, TILES * 128)
    raw_matrix = (VARS,) + raw_field
    cells_first = state[0].transpose(1, 0, 2)
    sent = cells_first.reshape(VARS, 2, STEPS, TILES, 128).transpose(0, 1, 3, 2, 4).reshape(FIELD, 128)
    u, edges, halos, lines, packed_maps = call(
        maps_kernel,
        [(FIELD, 128), (16, 128), (UP + halo[0], 128), (LINES, 128), (SEGMENTS * FULL_GROUPS, 128)],
        cells_first, coupling[0].transpose(1, 2, 0, 3), back_coupling[0].transpose(1, 2, 0, 3),
        pivot_inverse[0].transpose(1, 2, 0, 3), source_terms[0].transpose(1, 0, 2), wall_flags,
        scratch=[
            (MATRIX, 128), (STEPS * 8, 128), raw_field, raw_matrix, raw_matrix, raw_matrix, raw_field,
            pltpu.VMEM((2 * STEPS, TILES * 128), jnp.int32), pltpu.SemaphoreType.DMA((5 * VARS + 1,)),
        ],
        flops=8_000_000,
        limit=16,
        far=6,
        sent=(4,),
    )
    for sweep in range(SWEEPS):
        first = sweep == 0
        last = sweep == SWEEPS - 1
        spread = exchange(sent, "inst", INST)
        if first:
            term, left, right, up, above = call(
                lambda *refs: time_kernel(weights, *refs),
                [(FIELD, 128), edge, edge, (UP, 128), halo], spread, edges, halos, sent=(0,),
            )
            up = moved(up, "axial", 1, False)
            above = moved(above, "axial", -1, False)
            left = moved(left, "span", 1, True)
        else:
            left = moved(last_line, "span", 1, True)
            term, right = call(
                lambda *refs: late_time_kernel(weights, *refs), [(FIELD, 128), edge], spread, left, first_line,
                sent=(0,),
            )
        right = moved(right, "span", -1, True)
        time = exchange(term, "inst", INST)
        groups = FULL_GROUPS if first else VEC_GROUPS
        source, packed = call(
            local_kernel,
            [(FIELD + 2 * VARS * 8, 128), (SEGMENTS * groups, 128)],
            time, u, lines, left, right, *((up, above, packed_maps) if first else ()),
            scratch=[(FIELD, 128)] + ([pltpu.SemaphoreType.DMA] if first else []), far=1 if first else 0,
        )
        recv = exchange(packed, "axial", SEGMENTS)
        if first:
            maps_recv = recv
        (solved,) = call(
            lambda *refs, f=first: reduced_kernel(f, *refs),
            [(SEGMENTS * VEC_GROUPS, 128)], recv, *(() if first else (maps_recv,)),
            scratch=[(6 * SIZE * 8, 128)],
        )
        back_recv = exchange(solved, "axial", SEGMENTS)
        common = (back_recv, u, source, lines)
        if last:
            (result,) = call(
                lambda *refs: finish_kernel(True, *refs), [raw_field], *common, scratch=[(FIELD, 128)],
            )
        else:
            sent, last_line, first_line, u = call(
                lambda *refs: finish_kernel(False, *refs), [(FIELD, 128), edge, edge, (FIELD + 2 * halo[0], 128)],
                *common, above, up, scratch=[(UP, 128), pltpu.SemaphoreType.DMA], far=1, sent=(0,),
            )
    return result.transpose(1, 0, 2)[None]


def solution(mesh):
    return jax.shard_map(
        body,
        mesh=mesh,
        in_specs=(
            P("inst", "axial", None, "span"),
            P("inst", "axial", None, "span"),
            P("inst", "axial", None, None, "span"),
            P("inst", "axial", None, None, "span"),
            P("inst", "axial", None, None, "span"),
            P("axial", "span"),
        ),
        out_specs=P("inst", "axial", None, "span"),
        check_vma=False,
    )
```

```python
import math

import jax
import jax.numpy as jnp
import numpy as np
from jax import lax
from jax.experimental import pallas as pl
from jax.experimental.pallas import tpu as pltpu
from jax.sharding import PartitionSpec as P

INST = 8
SWEEPS = 2
VARS = 5
STEPS = 8
TILES = 4
SEGMENTS = 16
F32 = jnp.float32
FIELD = STEPS * VARS * 8
MATRIX = STEPS * VARS * VARS * 8
SIZE = VARS * VARS
FULL_GROUPS = 24
VEC_GROUPS = 4
PACKED = 2 * MATRIX + 3 * SIZE * 8
PIVOT = PACKED
CELLS = PIVOT + MATRIX
LINES = CELLS + FIELD
UP = VARS * 8 + (SIZE + 1) // 2 * 8
BELOW = STEPS * VARS
ABOVE = BELOW + VARS
KEPT = STEPS * VARS + 2 * VARS


def spectral():
    index = np.arange(INST)
    diff = index[:, None] - index[None, :]
    sign = 1.0 - 2.0 * np.mod(diff, 2)
    safe = np.where(diff == 0, 0.5 * math.pi, math.pi * diff / INST)
    first = np.where(diff == 0, 0.0, 0.5 * sign * np.cos(safe) / np.sin(safe))
    second = np.where(diff == 0, -(INST * INST + 2.0) / 12.0, -0.5 * sign / np.sin(safe) ** 2)
    return first - 0.5 * second


def iotas():
    sub = lax.broadcasted_iota(jnp.int32, (8, 128), 0)
    lane = lax.broadcasted_iota(jnp.int32, (8, 128), 1)
    return sub, lane


def row(ref, index):
    return ref[pl.ds(pl.multiple_of(index * 8, 8), 8), :]


def rows(ref, start, count):
    return [row(ref, start + n) for n in range(count)]


def put(ref, index, value):
    ref[pl.ds(pl.multiple_of(index * 8, 8), 8), :] = value


def total(terms):
    terms = list(terms)
    while len(terms) > 1:
        terms = [terms[n] + terms[n + 1] if n + 1 < len(terms) else terms[n] for n in range(0, len(terms), 2)]
    return terms[0]


def matvec(m, v):
    return [total(m[i * VARS + j] * v[j] for j in range(VARS)) for i in range(VARS)]


def matmul(a, b):
    return [
        total(a[i * VARS + j] * b[j * VARS + m] for j in range(VARS))
        for i in range(VARS)
        for m in range(VARS)
    ]


def plus(a, b):
    return [x + y for x, y in zip(a, b)]


def minus(a, b):
    return [x - y for x, y in zip(a, b)]


def swap(a):
    return [pltpu.roll(x, 4, 0) for x in a]


def pick(mask, a, b):
    return [jnp.where(mask, x, y) for x, y in zip(a, b)]


def lane_roll(x, shift):
    shift = shift % 128
    return x if shift == 0 else pltpu.roll(x, shift, 1)


def blocks4(block, parts):
    out = parts[0]
    for p in range(1, 4):
        out = jnp.where(block == p, parts[p], out)
    return out


def blocks4(block, parts):
    out = parts[0]
    for p in range(1, 4):
        out = jnp.where(block == p, parts[p], out)
    return out


def pack_lines(out_ref, start, block, values, first, groups):
    for g in range((len(values) + 3) // 4):
        four = [values[min(4 * g + p, len(values) - 1)] for p in range(4)]
        for q in range(4):
            chunk = blocks4(block, [lane_roll(four[p], 32 * (p - q)) for p in range(4)])
            out_ref[pl.ds(start + q * groups + first + g, 4, stride=4 * groups), :] = chunk[:4]


def edge_lines(sub, lane, u, last_ref, first_ref):
    last = jnp.zeros((8, 128), F32)
    initial = jnp.zeros((8, 128), F32)
    for n in range(STEPS * VARS):
        last = jnp.where(lane == n, lane_roll(u[n], n - 127), last)
        initial = jnp.where(lane == n, lane_roll(u[n], n), initial)
    last_ref[...] = pltpu.roll(last, 5, 0)
    first_ref[...] = pltpu.roll(initial, 3, 0)


def field_to_packed(raw_ref, out_ref, start=0):
    for v in range(VARS):
        for half in range(2):
            for t in range(TILES):
                tile = raw_ref[v, half * STEPS : (half + 1) * STEPS, t * 128 : (t + 1) * 128]
                out_ref[pl.ds(start + v * 8 + half * TILES + t, STEPS, stride=VARS * 8), :] = tile


def matrix_to_packed(raw_ref, out_ref, start=0):
    for i in range(VARS):
        for j in range(VARS):
            for half in range(2):
                for t in range(TILES):
                    tile = raw_ref[i, j, half * STEPS : (half + 1) * STEPS, t * 128 : (t + 1) * 128]
                    begin = start + (i * VARS + j) * 8 + half * TILES + t
                    out_ref[pl.ds(begin, STEPS, stride=SIZE * 8), :] = tile


def fetch(source, target, sems, first):
    copies = [pltpu.make_async_copy(source.at[i], target.at[i], sems.at[first + i]) for i in range(VARS)]
    for copy in copies:
        copy.start()
    return copies


def arrive(copies):
    for copy in copies:
        copy.wait()


def pack_kernel(state_hbm, u_ref, last_ref, first_ref, state_ref, sems):
    sub, lane = iotas()
    arrive(fetch(state_hbm, state_ref, sems, 0))
    field_to_packed(state_ref, u_ref)
    edge_lines(sub, lane, rows(u_ref, 0, STEPS * VARS), last_ref, first_ref)


def piece_out(stage_ref, out_hbm, sems, index, count):
    piece = pl.ds(index * count, count)
    copy = pltpu.make_async_copy(stage_ref.at[piece], out_hbm.at[piece], sems.at[index])
    copy.start()
    return copy


def time_term(weights, spread_ref, out_hbm, stage_ref, sems):
    copies = []
    for i in range(INST):
        for v in range(VARS):
            terms = [row(spread_ref, j * VARS + v) * F32(weights[i, j]) for j in range(INST)]
            put(stage_ref, i * VARS + v, total(terms))
        copies.append(piece_out(stage_ref, out_hbm, sems, i, VARS * 8))
    return copies


def time_kernel(
    weights, spread_ref, left_ref, line_ref, halos_ref,
    out_hbm, first_ref, up_ref, down_ref, stage_ref, sems,
):
    copies = time_term(weights, spread_ref, out_hbm, stage_ref, sems)
    first_ref[...] = line_ref[...]
    up_ref[...] = halos_ref[:UP, :]
    down_ref[...] = halos_ref[UP:, :]
    arrive(copies)


def late_time_kernel(weights, spread_ref, left_ref, line_ref, out_hbm, first_ref, stage_ref, sems):
    copies = time_term(weights, spread_ref, out_hbm, stage_ref, sems)
    first_ref[...] = line_ref[...]
    arrive(copies)


def maps_kernel(
    u_ref, coupling_hbm, back_hbm, pivot_hbm, source_hbm, flags_hbm,
    halos_ref, lines_ref, packed_hbm,
    prefix_ref, keep_ref, coupling_raw, back_raw, pivot_raw, source_raw, flags_ref, packed_ref, sems,
):
    sub, lane = iotas()
    block = lane // 32
    coupling_copies = fetch(coupling_hbm, coupling_raw, sems, 0)
    back_copies = fetch(back_hbm, back_raw, sems, VARS)
    pivot_copies = fetch(pivot_hbm, pivot_raw, sems, 2 * VARS)
    source_copies = fetch(source_hbm, source_raw, sems, 3 * VARS)
    flags_copy = pltpu.make_async_copy(flags_hbm, flags_ref, sems.at[4 * VARS])
    flags_copy.start()
    top = sub < TILES
    arrive(coupling_copies)
    matrix_to_packed(coupling_raw, lines_ref, 0)
    arrive(back_copies)
    matrix_to_packed(back_raw, lines_ref, MATRIX)
    def coupling(k):
        return rows(lines_ref, k * SIZE, SIZE)

    def back(k):
        return rows(lines_ref, STEPS * SIZE + k * SIZE, SIZE)

    def forward(k, p):
        p = [-x for x in matmul(coupling(k), p)]
        for n in range(SIZE):
            put(prefix_ref, k * SIZE + n, p[n])
        return p

    first = [-x for x in coupling(0)]
    for n in range(SIZE):
        put(prefix_ref, n, first[n])
    ahead = lax.fori_loop(1, STEPS, forward, first)

    def backward(step, carry):
        k = STEPS - 2 - step
        return minus(rows(prefix_ref, k * SIZE, SIZE), matmul(back(k), carry))

    mixed = lax.fori_loop(0, STEPS - 1, backward, ahead)

    def behind_step(step, carry):
        return [-x for x in matmul(back(STEPS - 2 - step), carry)]

    behind = lax.fori_loop(0, STEPS - 1, behind_step, [-x for x in back(STEPS - 1)])
    base = 2 * STEPS * SIZE
    for n in range(SIZE):
        put(lines_ref, base + n, ahead[n])
        put(lines_ref, base + SIZE + n, mixed[n])
        put(lines_ref, base + 2 * SIZE + n, behind[n])
    whole = matmul(swap(ahead), ahead)
    for n in range(SIZE):
        put(prefix_ref, n, whole[n])
    whole = plus(mixed, matmul(behind, matmul(swap(mixed), ahead)))
    for n in range(SIZE):
        put(prefix_ref, SIZE + n, whole[n])
    whole = matmul(behind, swap(behind))
    for n in range(SIZE):
        put(prefix_ref, 2 * SIZE + n, whole[n])
    pack_lines(packed_ref, 0, block, rows(prefix_ref, 0, 3 * SIZE), VEC_GROUPS, FULL_GROUPS)
    packed_copy = pltpu.make_async_copy(packed_ref, packed_hbm, sems.at[4 * VARS + 1])
    packed_copy.start()
    arrive(pivot_copies)
    matrix_to_packed(pivot_raw, lines_ref, PIVOT)
    arrive(source_copies)
    field_to_packed(source_raw, lines_ref, CELLS)
    flags_copy.wait()
    for half in range(2):
        for t in range(TILES):
            flags = flags_ref[half * STEPS : (half + 1) * STEPS, t * 128 : (t + 1) * 128]
            keep_ref[pl.ds(half * TILES + t, STEPS, stride=8), :] = (1 - flags).astype(F32)

    def mask(k, carry):
        keep = row(keep_ref, k)
        for n in range(SIZE):
            put(lines_ref, PIVOT // 8 + k * SIZE + n, keep * row(lines_ref, PIVOT // 8 + k * SIZE + n))
        return carry

    lax.fori_loop(0, STEPS, mask, 0)
    halos_ref[: VARS * 8, :] = u_ref[(STEPS - 1) * VARS * 8 :, :]
    last = back(STEPS - 1)
    for n in range(0, SIZE, 2):
        pair = jnp.where(top, pltpu.roll(last[n], 4, 0), last[min(n + 1, SIZE - 1)])
        put(halos_ref, VARS + n // 2, pair)
    halos_ref[UP:, :] = u_ref[: VARS * 8, :]
    packed_copy.wait()


def stencil(
    sub, lane, u_ref, lines_ref, below_ref, below_at, above_ref, above_at, left_ref, right_ref, time_ref, out_ref
):
    top = sub < TILES
    left_all = left_ref[...]
    right_all = right_ref[...]
    for k in range(STEPS):
        for v in range(VARS):
            n = k * VARS + v
            u = row(u_ref, n)
            if k == 0:
                below = pltpu.roll(jnp.where(top, row(u_ref, (STEPS - 1) * VARS + v), row(below_ref, below_at + v)), 4, 0)
            else:
                below = row(u_ref, n - VARS)
            if k == STEPS - 1:
                above = pltpu.roll(jnp.where(top, row(above_ref, above_at + v), row(u_ref, v)), 4, 0)
            else:
                above = row(u_ref, n + VARS)
            turned = pltpu.roll(u, 1, 1)
            edge = jnp.where(sub % TILES == 0, lane_roll(left_all, -n), pltpu.roll(turned, 1, 0))
            left = jnp.where(lane == 0, edge, turned)
            turned = pltpu.roll(u, 127, 1)
            edge = jnp.where(sub % TILES == TILES - 1, lane_roll(right_all, 127 - n), pltpu.roll(turned, 7, 0))
            right = jnp.where(lane == 127, edge, turned)
            value = row(lines_ref, CELLS // 8 + n) - 0.1 * above + 0.5 * below - 0.8 * u + 0.2 * (left + right)
            put(out_ref, n, value + row(time_ref, n))


def local_kernel(time_ref, u_ref, lines_ref, left_ref, right_ref, *rest):
    sub, lane = iotas()
    block = lane // 32
    if len(rest) > 3:
        below_ref, above_ref, maps_hbm, source_ref, packed_ref, rhs_ref, sems = rest
        below_at, above_at, groups = 0, 0, FULL_GROUPS
        maps_copies = [piece_out(maps_hbm, packed_ref, sems, n, SEGMENTS * FULL_GROUPS // 4) for n in range(4)]
        source_ref[KEPT * 8 : KEPT * 8 + UP, :] = below_ref[...]
        source_ref[KEPT * 8 + UP :, :] = above_ref[...]
        for n in range(STEPS * VARS):
            v, tile = n // 8, n % 8
            rhs_ref[pl.ds(v * 8 + tile, STEPS, stride=VARS * 8), :] = row(time_ref, n)
        time_ref = rhs_ref
    else:
        source_ref, packed_ref, rhs_ref = rest
        below_ref = above_ref = u_ref
        below_at, above_at, groups = BELOW, ABOVE, VEC_GROUPS
    stencil(
        sub, lane, u_ref, lines_ref, below_ref, below_at, above_ref, above_at, left_ref, right_ref, time_ref, rhs_ref
    )

    def source_step(k, carry):
        rhs = rows(rhs_ref, k * VARS, VARS)
        for v, value in enumerate(matvec(rows(lines_ref, PIVOT // 8 + k * SIZE, SIZE), rhs)):
            put(source_ref, k * VARS + v, value)
        return carry

    lax.fori_loop(0, STEPS, source_step, 0)
    y = rows(source_ref, 0, VARS)
    kept = [y]
    for k in range(1, STEPS):
        y = minus(rows(source_ref, k * VARS, VARS), matvec(rows(lines_ref, k * SIZE, SIZE), y))
        kept.append(y)
    end = y
    x = y
    for k in range(STEPS - 2, -1, -1):
        x = minus(kept[k], matvec(rows(lines_ref, (STEPS + k) * SIZE, SIZE), x))
    for v in range(VARS):
        put(source_ref, STEPS * VARS + v, end[v])
        put(source_ref, STEPS * VARS + VARS + v, x[v])
    base = 2 * STEPS * SIZE
    ahead = rows(lines_ref, base, SIZE)
    mixed = rows(lines_ref, base + SIZE, SIZE)
    behind = rows(lines_ref, base + 2 * SIZE, SIZE)
    whole_end = plus(swap(end), matvec(swap(ahead), end))
    inner = plus(swap(x), matvec(swap(mixed), end))
    whole_first = plus(x, matvec(behind, inner))
    values = whole_end + whole_first + [jnp.zeros((8, 128), F32)] * (4 * VEC_GROUPS - 2 * VARS)
    if groups == FULL_GROUPS:
        arrive(maps_copies)
    pack_lines(packed_ref, 0, block, values, 0, groups)


def shift_in(sub, values, entry):
    return [jnp.where(sub == 0, e, pltpu.roll(x, 1, 0)) for x, e in zip(values, entry)]


def shift_out(sub, values, entry):
    return [jnp.where(sub == 7, e, pltpu.roll(x, 7, 0)) for x, e in zip(values, entry)]


def reduced_kernel(first, recv_ref, *rest):
    maps_recv_ref = recv_ref if first else rest[0]
    out_ref, maps_ref = rest[-2:]
    sub, lane = iotas()
    block = lane // 32

    def stacked(ref, groups, r, part):
        values = ref[pl.ds(part * 8 * groups + r // 4, 8, stride=groups), :]
        return lane_roll(values, -32 * (r % 4))

    def value(r, part):
        return stacked(recv_ref, FULL_GROUPS if first else VEC_GROUPS, r, part)

    for r in range(3 * SIZE):
        for part in range(2):
            put(maps_ref, part * 3 * SIZE + r, stacked(maps_recv_ref, FULL_GROUPS, 4 * VEC_GROUPS + r, part))
    zero = [jnp.zeros((8, 128), F32)] * VARS

    def solve(part, which, source, entry, shift):
        maps = rows(maps_ref, part * 3 * SIZE + which * SIZE, SIZE)

        def step(_, now):
            return plus(source, matvec(maps, shift(sub, now, entry)))

        out = lax.fori_loop(0, 7, step, plus(source, matvec(maps, shift(sub, zero, entry))))
        return out, shift(sub, out, entry)

    ends = [[value(r, part) for r in range(VARS)] for part in range(2)]
    firsts = [[value(VARS + r, part) for r in range(VARS)] for part in range(2)]
    out, low_entry = solve(0, 0, ends[0], zero, shift_in)
    out, high_entry = solve(1, 0, ends[1], [pltpu.roll(x, 1, 0) for x in out], shift_in)
    entries = [low_entry, high_entry]
    drive = [
        plus(firsts[part], matvec(rows(maps_ref, part * 3 * SIZE + SIZE, SIZE), entries[part])) for part in range(2)
    ]
    out, high_next = solve(1, 2, drive[1], zero, shift_out)
    out, low_next = solve(0, 2, drive[0], [pltpu.roll(x, 7, 0) for x in out], shift_out)
    nexts = [low_next, high_next]
    for part in range(2):
        values = entries[part] + nexts[part] + zero + zero[:1]
        for g in range(VEC_GROUPS):
            packed = blocks4(block, [lane_roll(values[4 * g + p], 32 * p) for p in range(4)])
            out_ref[pl.ds(part * 8 * VEC_GROUPS + g, 8, stride=VEC_GROUPS), :] = packed


def finish_kernel(last, recv_ref, u_ref, source_ref, lines_ref, *rest):
    if last:
        out_hbm, new_ref, out_ref, sems = rest
    else:
        sent_hbm, last_ref, first_ref, new_ref, sems = rest
    copies = []
    sub, lane = iotas()
    block = lane // 32
    top = sub < TILES
    stacked = [
        [
            recv_ref[pl.ds(q * VEC_GROUPS + g, TILES, stride=4 * VEC_GROUPS), :]
            for g in range((2 * VARS + 3) // 4)
        ]
        for q in range(4)
    ]
    stacked = [[jnp.concatenate([x, x], axis=0) for x in line] for line in stacked]

    def value(r):
        return blocks4(block, [lane_roll(stacked[q][r // 4], 32 * (q - r % 4)) for q in range(4)])

    entry = [value(r) for r in range(VARS)]
    after = [value(VARS + r) for r in range(VARS)]
    base = 2 * STEPS * SIZE
    end = rows(source_ref, STEPS * VARS, VARS)
    begin = rows(source_ref, STEPS * VARS + VARS, VARS)
    middle = plus(end, matvec(rows(lines_ref, base, SIZE), entry))
    start = pick(top, entry, swap(middle))
    follow = plus(
        plus(begin, matvec(rows(lines_ref, base + SIZE, SIZE), start)),
        matvec(rows(lines_ref, base + 2 * SIZE, SIZE), after),
    )
    finish = pick(top, swap(follow), after)
    y = start
    kept = []
    for k in range(STEPS):
        y = minus(rows(source_ref, k * VARS, VARS), matvec(rows(lines_ref, k * SIZE, SIZE), y))
        kept.append(y)
    x = finish
    for k in range(STEPS - 1, -1, -1):
        x = minus(kept[k], matvec(rows(lines_ref, (STEPS + k) * SIZE, SIZE), x))
        for v in range(VARS):
            put(new_ref, k * VARS + v, row(u_ref, k * VARS + v) + x[v])
        if not last:
            copies.append(piece_out(new_ref, sent_hbm, sems, k, VARS * 8))
    if last:
        for v in range(VARS):
            for half in range(2):
                for t in range(TILES):
                    tile = new_ref[pl.ds(v * 8 + half * TILES + t, STEPS, stride=VARS * 8), :]
                    out_ref[v, half * STEPS : (half + 1) * STEPS, t * 128 : (t + 1) * 128] = tile
            copies.append(pltpu.make_async_copy(out_ref.at[v], out_hbm.at[v], sems.at[v]))
            copies[-1].start()
    else:
        edge_lines(sub, lane, rows(new_ref, 0, STEPS * VARS), last_ref, first_ref)
        pairs = rows(source_ref, KEPT + VARS, (SIZE + 1) // 2)
        blocks = [pairs[n // 2] if n % 2 else pltpu.roll(pairs[n // 2], 4, 0) for n in range(SIZE)]
        before = minus(entry, matvec(blocks, swap(x)))
        for v in range(VARS):
            put(new_ref, BELOW + v, row(source_ref, KEPT + v) + before[v])
            put(new_ref, ABOVE + v, row(source_ref, KEPT + UP // 8 + v) + after[v])
    arrive(copies)


def call(kernel, shapes, *args, scratch=(), flops=100_000, limit=8, far=0, sent=()):
    outs = [pltpu.HBM(shape, F32) if n in sent else jax.ShapeDtypeStruct(shape, F32) for n, shape in enumerate(shapes)]
    moved = 4 * (sum(math.prod(shape) for shape in shapes) + sum(a.size for a in args))
    near = len(args) - far
    specs = [pl.BlockSpec(memory_space=pltpu.VMEM if n < near else pltpu.HBM) for n in range(len(args))]
    args = args[:near] + tuple(pltpu.with_memory_space_constraint(a, pltpu.HBM) for a in args[near:])
    return pl.pallas_call(
        kernel,
        out_shape=outs,
        in_specs=specs,
        out_specs=[pl.BlockSpec(memory_space=pltpu.HBM if n in sent else pltpu.VMEM) for n in range(len(outs))],
        scratch_shapes=[pltpu.VMEM(item, F32) if isinstance(item, tuple) else item for item in scratch],
        cost_estimate=pl.CostEstimate(flops=flops, bytes_accessed=moved, transcendentals=0),
        compiler_params=pltpu.CompilerParams(vmem_limit_bytes=limit * 1024 * 1024),
    )(*args)


def exchange(value, axis, count):
    shape = value.shape
    out = lax.all_to_all(value.reshape(count, shape[0] // count, 128), axis, 0, 0)
    return out.reshape(shape)


def moved(value, axis, step, wrap):
    count = lax.axis_size(axis)
    pairs = [(i, (i + step) % count) for i in range(count) if wrap or 0 <= i + step < count]
    return lax.ppermute(value, axis, pairs)


def body(state, source_terms, pivot_inverse, coupling, back_coupling, wall_flags):
    weights = np.float32(-0.5 * spectral())
    edge = (8, 128)
    halo = (VARS * 8, 128)
    raw_field = (VARS, 2 * STEPS, TILES * 128)
    raw_matrix = (VARS,) + raw_field
    cells_first = state[0].transpose(1, 0, 2)
    sent = cells_first.reshape(VARS, 2, STEPS, TILES, 128).transpose(0, 1, 3, 2, 4).reshape(FIELD, 128)
    u, last_line, first_line = call(
        pack_kernel, [(FIELD, 128), edge, edge], cells_first,
        scratch=[raw_field, pltpu.SemaphoreType.DMA((VARS,))], far=1,
    )
    halos, lines, packed_maps = call(
        maps_kernel,
        [(UP + halo[0], 128), (LINES, 128), (SEGMENTS * FULL_GROUPS, 128)],
        u, coupling[0].transpose(1, 2, 0, 3), back_coupling[0].transpose(1, 2, 0, 3),
        pivot_inverse[0].transpose(1, 2, 0, 3), source_terms[0].transpose(1, 0, 2), wall_flags,
        scratch=[
            (MATRIX, 128), (STEPS * 8, 128), raw_matrix, raw_matrix, raw_matrix, raw_field,
            pltpu.VMEM((2 * STEPS, TILES * 128), jnp.int32), (SEGMENTS * FULL_GROUPS, 128),
            pltpu.SemaphoreType.DMA((4 * VARS + 2,)),
        ],
        flops=8_000_000,
        limit=16,
        far=5,
        sent=(2,),
    )
    stage = [(FIELD, 128), pltpu.SemaphoreType.DMA((INST,))]
    for sweep in range(SWEEPS):
        first = sweep == 0
        last = sweep == SWEEPS - 1
        spread = exchange(sent, "inst", INST)
        left = moved(last_line, "span", 1, True)
        if first:
            term, right, up, above = call(
                lambda *refs: time_kernel(weights, *refs),
                [(FIELD, 128), edge, (UP, 128), halo], spread, left, first_line, halos, scratch=stage, sent=(0,),
            )
            up = moved(up, "axial", 1, False)
            above = moved(above, "axial", -1, False)
        else:
            term, right = call(
                lambda *refs: late_time_kernel(weights, *refs), [(FIELD, 128), edge], spread, left, first_line,
                scratch=stage, sent=(0,),
            )
        right = moved(right, "span", -1, True)
        time = exchange(term, "inst", INST)
        groups = FULL_GROUPS if first else VEC_GROUPS
        source, packed = call(
            local_kernel,
            [(KEPT * 8 + (UP + halo[0] if first else 0), 128), (SEGMENTS * groups, 128)],
            time, u, lines, left, right, *((up, above, packed_maps) if first else ()),
            scratch=[(FIELD, 128)] + ([pltpu.SemaphoreType.DMA((4,))] if first else []), far=1 if first else 0,
        )
        recv = exchange(packed, "axial", SEGMENTS)
        if first:
            maps_recv = recv
        (solved,) = call(
            lambda *refs, f=first: reduced_kernel(f, *refs),
            [(SEGMENTS * VEC_GROUPS, 128)], recv, *(() if first else (maps_recv,)),
            scratch=[(6 * SIZE * 8, 128)],
        )
        back_recv = exchange(solved, "axial", SEGMENTS)
        common = (back_recv, u, source, lines)
        if last:
            (result,) = call(
                lambda *refs: finish_kernel(True, *refs), [raw_field], *common,
                scratch=[(FIELD, 128), raw_field, pltpu.SemaphoreType.DMA((VARS,))], sent=(0,),
            )
        else:
            sent, last_line, first_line, u = call(
                lambda *refs: finish_kernel(False, *refs), [(FIELD, 128), edge, edge, (FIELD + 2 * halo[0], 128)],
                *common, scratch=[pltpu.SemaphoreType.DMA((STEPS,))], sent=(0,),
            )
    return result.transpose(1, 0, 2)[None]


def solution(mesh):
    return jax.shard_map(
        body,
        mesh=mesh,
        in_specs=(
            P("inst", "axial", None, "span"),
            P("inst", "axial", None, "span"),
            P("inst", "axial", None, None, "span"),
            P("inst", "axial", None, None, "span"),
            P("inst", "axial", None, None, "span"),
            P("axial", "span"),
        ),
        out_specs=P("inst", "axial", None, "span"),
        check_vma=False,
    )
```

```python
import math

import jax
import jax.numpy as jnp
import numpy as np
from jax import lax
from jax.experimental import pallas as pl
from jax.experimental.pallas import tpu as pltpu
from jax.sharding import PartitionSpec as P

INST = 8
SWEEPS = 2
VARS = 5
STEPS = 8
TILES = 4
SEGMENTS = 16
F32 = jnp.float32
FIELD = STEPS * VARS * 8
MATRIX = STEPS * VARS * VARS * 8
SIZE = VARS * VARS
FULL_GROUPS = 24
VEC_GROUPS = 4
CHAIN = 2 * MATRIX
PIVOT = 3 * SIZE * 8
CELLS = PIVOT + MATRIX
LINES = CELLS + FIELD
UP = VARS * 8 + (SIZE + 1) // 2 * 8
BELOW = STEPS * VARS
ABOVE = BELOW + VARS
KEPT = STEPS * VARS + 2 * VARS


def spectral():
    index = np.arange(INST)
    diff = index[:, None] - index[None, :]
    sign = 1.0 - 2.0 * np.mod(diff, 2)
    safe = np.where(diff == 0, 0.5 * math.pi, math.pi * diff / INST)
    first = np.where(diff == 0, 0.0, 0.5 * sign * np.cos(safe) / np.sin(safe))
    second = np.where(diff == 0, -(INST * INST + 2.0) / 12.0, -0.5 * sign / np.sin(safe) ** 2)
    return first - 0.5 * second


def iotas():
    sub = lax.broadcasted_iota(jnp.int32, (8, 128), 0)
    lane = lax.broadcasted_iota(jnp.int32, (8, 128), 1)
    return sub, lane


def row(ref, index):
    return ref[pl.ds(pl.multiple_of(index * 8, 8), 8), :]


def rows(ref, start, count):
    return [row(ref, start + n) for n in range(count)]


def put(ref, index, value):
    ref[pl.ds(pl.multiple_of(index * 8, 8), 8), :] = value


def total(terms):
    terms = list(terms)
    while len(terms) > 1:
        terms = [terms[n] + terms[n + 1] if n + 1 < len(terms) else terms[n] for n in range(0, len(terms), 2)]
    return terms[0]


def matvec(m, v):
    return [total(m[i * VARS + j] * v[j] for j in range(VARS)) for i in range(VARS)]


def step_minus(source, m, v):
    out = []
    for i in range(VARS):
        t = [m[i * VARS + j] * v[j] for j in range(VARS)]
        out.append(((source[i] - t[0]) - (t[1] + t[2])) - (t[3] + t[4]))
    return out


def step_plus(source, m, v):
    out = []
    for i in range(VARS):
        t = [m[i * VARS + j] * v[j] for j in range(VARS)]
        out.append(((source[i] + t[0]) + (t[1] + t[2])) + (t[3] + t[4]))
    return out


def matmul(a, b):
    out = [None] * SIZE
    for m in range(VARS):
        column = [b[j * VARS + m] for j in range(VARS)]
        for i in range(VARS):
            t = [a[i * VARS + j] * column[j] for j in range(VARS)]
            out[i * VARS + m] = (t[0] + t[1]) + (t[2] + t[3]) + t[4]
    return out


def plus(a, b):
    return [x + y for x, y in zip(a, b)]


def minus(a, b):
    return [x - y for x, y in zip(a, b)]


def swap(a):
    return [pltpu.roll(x, 4, 0) for x in a]


def pick(mask, a, b):
    return [jnp.where(mask, x, y) for x, y in zip(a, b)]


def lane_roll(x, shift):
    shift = shift % 128
    return x if shift == 0 else pltpu.roll(x, shift, 1)


def blocks4(block, parts):
    out = parts[0]
    for p in range(1, 4):
        out = jnp.where(block == p, parts[p], out)
    return out


def blocks4(block, parts):
    out = parts[0]
    for p in range(1, 4):
        out = jnp.where(block == p, parts[p], out)
    return out


def pack_lines(out_ref, start, block, values, first, groups):
    for g in range((len(values) + 3) // 4):
        four = [values[min(4 * g + p, len(values) - 1)] for p in range(4)]
        for q in range(4):
            chunk = blocks4(block, [lane_roll(four[p], 32 * (p - q)) for p in range(4)])
            out_ref[pl.ds(start + q * groups + first + g, 4, stride=4 * groups), :] = chunk[:4]


def edge_lines(sub, lane, u, last_ref, first_ref):
    last = jnp.zeros((8, 128), F32)
    initial = jnp.zeros((8, 128), F32)
    for n in range(STEPS * VARS):
        last = jnp.where(lane == n, lane_roll(u[n], n - 127), last)
        initial = jnp.where(lane == n, lane_roll(u[n], n), initial)
    last_ref[...] = pltpu.roll(last, 5, 0)
    first_ref[...] = pltpu.roll(initial, 3, 0)


def field_to_packed(raw_ref, out_ref, start=0):
    for v in range(VARS):
        for half in range(2):
            for t in range(TILES):
                tile = raw_ref[v, half * STEPS : (half + 1) * STEPS, t * 128 : (t + 1) * 128]
                out_ref[pl.ds(start + v * 8 + half * TILES + t, STEPS, stride=VARS * 8), :] = tile


def matrix_to_packed(raw_ref, out_ref, start=0):
    for i in range(VARS):
        for j in range(VARS):
            for half in range(2):
                for t in range(TILES):
                    tile = raw_ref[i, j, half * STEPS : (half + 1) * STEPS, t * 128 : (t + 1) * 128]
                    begin = start + (i * VARS + j) * 8 + half * TILES + t
                    out_ref[pl.ds(begin, STEPS, stride=SIZE * 8), :] = tile


def fetch(source, target, sems, first):
    copies = [pltpu.make_async_copy(source.at[i], target.at[i], sems.at[first + i]) for i in range(VARS)]
    for copy in copies:
        copy.start()
    return copies


def arrive(copies):
    for copy in copies:
        copy.wait()


def pack_kernel(
    state_hbm, coupling_hbm, back_hbm, u_ref, last_ref, first_ref, chain_ref, up_ref, down_ref,
    state_ref, coupling_raw, back_raw, sems,
):
    sub, lane = iotas()
    state_copies = fetch(state_hbm, state_ref, sems, 0)
    coupling_copies = fetch(coupling_hbm, coupling_raw, sems, VARS)
    back_copies = fetch(back_hbm, back_raw, sems, 2 * VARS)
    arrive(state_copies)
    field_to_packed(state_ref, u_ref)
    edge_lines(sub, lane, rows(u_ref, 0, STEPS * VARS), last_ref, first_ref)
    arrive(coupling_copies)
    matrix_to_packed(coupling_raw, chain_ref, 0)
    arrive(back_copies)
    matrix_to_packed(back_raw, chain_ref, MATRIX)
    up_ref[: VARS * 8, :] = u_ref[(STEPS - 1) * VARS * 8 :, :]
    blocks = rows(chain_ref, (2 * STEPS - 1) * SIZE, SIZE)
    for n in range(0, SIZE, 2):
        pair = jnp.where(sub < TILES, pltpu.roll(blocks[n], 4, 0), blocks[min(n + 1, SIZE - 1)])
        put(up_ref, VARS + n // 2, pair)
    down_ref[...] = u_ref[: VARS * 8, :]


def piece_out(stage_ref, out_hbm, sems, index, count):
    piece = pl.ds(index * count, count)
    copy = pltpu.make_async_copy(stage_ref.at[piece], out_hbm.at[piece], sems.at[index])
    copy.start()
    return copy


def time_term(weights, spread_ref, out_hbm, stage_ref, sems):
    copies = []
    for i in range(INST):
        for v in range(VARS):
            terms = [row(spread_ref, j * VARS + v) * F32(weights[i, j]) for j in range(INST)]
            put(stage_ref, i * VARS + v, total(terms))
        copies.append(piece_out(stage_ref, out_hbm, sems, i, VARS * 8))
    return copies


def time_kernel(weights, count, spread_ref, *rest):
    out_hbm, *passed_refs, stage_ref, sems = rest[-3 - count :]
    copies = time_term(weights, spread_ref, out_hbm, stage_ref, sems)
    for line_ref, passed_ref in zip(rest, passed_refs):
        passed_ref[...] = line_ref[...]
    arrive(copies)


def maps_kernel(
    chain_ref, after_ref, pivot_hbm, source_hbm, flags_hbm,
    lines_ref, packed_hbm,
    prefix_ref, keep_ref, pivot_raw, source_raw, flags_ref, packed_ref, sems,
):
    sub, lane = iotas()
    block = lane // 32
    pivot_copies = fetch(pivot_hbm, pivot_raw, sems, 0)
    source_copies = fetch(source_hbm, source_raw, sems, VARS)
    flags_copy = pltpu.make_async_copy(flags_hbm, flags_ref, sems.at[2 * VARS])
    flags_copy.start()
    top = sub < TILES
    def coupling(k):
        return rows(chain_ref, k * SIZE, SIZE)

    def back(k):
        return rows(chain_ref, STEPS * SIZE + k * SIZE, SIZE)

    def forward(k, p):
        p = [-x for x in matmul(coupling(k), p)]
        for n in range(SIZE):
            put(prefix_ref, k * SIZE + n, p[n])
        return p

    first = [-x for x in coupling(0)]
    for n in range(SIZE):
        put(prefix_ref, n, first[n])
    ahead = lax.fori_loop(1, STEPS, forward, first)

    def backward(step, carry):
        k = STEPS - 2 - step
        return minus(rows(prefix_ref, k * SIZE, SIZE), matmul(back(k), carry))

    mixed = lax.fori_loop(0, STEPS - 1, backward, ahead)

    def behind_step(step, carry):
        return [-x for x in matmul(back(STEPS - 2 - step), carry)]

    behind = lax.fori_loop(0, STEPS - 1, behind_step, [-x for x in back(STEPS - 1)])
    for n in range(SIZE):
        put(lines_ref, n, ahead[n])
        put(lines_ref, SIZE + n, mixed[n])
        put(lines_ref, 2 * SIZE + n, behind[n])
    whole = matmul(swap(ahead), ahead)
    for n in range(SIZE):
        put(prefix_ref, n, whole[n])
    whole = plus(mixed, matmul(behind, matmul(swap(mixed), ahead)))
    for n in range(SIZE):
        put(prefix_ref, SIZE + n, whole[n])
    whole = matmul(behind, swap(behind))
    for n in range(SIZE):
        put(prefix_ref, 2 * SIZE + n, whole[n])
    pack_lines(packed_ref, 0, block, rows(prefix_ref, 0, 3 * SIZE), VEC_GROUPS, FULL_GROUPS)
    packed_copy = pltpu.make_async_copy(packed_ref, packed_hbm, sems.at[2 * VARS + 1])
    packed_copy.start()
    arrive(pivot_copies)
    matrix_to_packed(pivot_raw, lines_ref, PIVOT)
    arrive(source_copies)
    field_to_packed(source_raw, lines_ref, CELLS)
    flags_copy.wait()
    for half in range(2):
        for t in range(TILES):
            flags = flags_ref[half * STEPS : (half + 1) * STEPS, t * 128 : (t + 1) * 128]
            keep_ref[pl.ds(half * TILES + t, STEPS, stride=8), :] = (1 - flags).astype(F32)

    def mask(k, carry):
        keep = row(keep_ref, k)
        for n in range(SIZE):
            put(lines_ref, PIVOT // 8 + k * SIZE + n, keep * row(lines_ref, PIVOT // 8 + k * SIZE + n))
        return carry

    lax.fori_loop(0, STEPS, mask, 0)
    packed_copy.wait()


def stencil(
    sub, lane, u_ref, lines_ref, below_ref, below_at, above_ref, above_at, left_ref, right_ref, time_ref, out_ref
):
    top = sub < TILES
    left_all = left_ref[...]
    right_all = right_ref[...]
    for k in range(STEPS):
        for v in range(VARS):
            n = k * VARS + v
            u = row(u_ref, n)
            if k == 0:
                below = pltpu.roll(jnp.where(top, row(u_ref, (STEPS - 1) * VARS + v), row(below_ref, below_at + v)), 4, 0)
            else:
                below = row(u_ref, n - VARS)
            if k == STEPS - 1:
                above = pltpu.roll(jnp.where(top, row(above_ref, above_at + v), row(u_ref, v)), 4, 0)
            else:
                above = row(u_ref, n + VARS)
            turned = pltpu.roll(u, 1, 1)
            edge = jnp.where(sub % TILES == 0, lane_roll(left_all, -n), pltpu.roll(turned, 1, 0))
            left = jnp.where(lane == 0, edge, turned)
            turned = pltpu.roll(u, 127, 1)
            edge = jnp.where(sub % TILES == TILES - 1, lane_roll(right_all, 127 - n), pltpu.roll(turned, 7, 0))
            right = jnp.where(lane == 127, edge, turned)
            value = row(lines_ref, CELLS // 8 + n) - 0.1 * above + 0.5 * below - 0.8 * u + 0.2 * (left + right)
            put(out_ref, n, value + row(time_ref, n))


def local_kernel(time_ref, u_ref, chain_ref, lines_ref, left_ref, right_ref, *rest):
    sub, lane = iotas()
    block = lane // 32
    if len(rest) > 3:
        below_ref, above_ref, maps_hbm, source_ref, packed_ref, rhs_ref, sems = rest
        below_at, above_at, groups = 0, 0, FULL_GROUPS
        maps_copies = [piece_out(maps_hbm, packed_ref, sems, n, SEGMENTS * FULL_GROUPS // 4) for n in range(4)]
        source_ref[KEPT * 8 : KEPT * 8 + UP, :] = below_ref[...]
        source_ref[KEPT * 8 + UP :, :] = above_ref[...]
        for n in range(STEPS * VARS):
            v, tile = n // 8, n % 8
            rhs_ref[pl.ds(v * 8 + tile, STEPS, stride=VARS * 8), :] = row(time_ref, n)
        time_ref = rhs_ref
    else:
        source_ref, packed_ref, rhs_ref = rest
        below_ref = above_ref = u_ref
        below_at, above_at, groups = BELOW, ABOVE, VEC_GROUPS
    stencil(
        sub, lane, u_ref, lines_ref, below_ref, below_at, above_ref, above_at, left_ref, right_ref, time_ref, rhs_ref
    )

    def source_step(k, carry):
        rhs = rows(rhs_ref, k * VARS, VARS)
        for v, value in enumerate(matvec(rows(lines_ref, PIVOT // 8 + k * SIZE, SIZE), rhs)):
            put(source_ref, k * VARS + v, value)
        return carry

    lax.fori_loop(0, STEPS, source_step, 0)
    y = rows(source_ref, 0, VARS)
    kept = [y]
    for k in range(1, STEPS):
        y = step_minus(rows(source_ref, k * VARS, VARS), rows(chain_ref, k * SIZE, SIZE), y)
        kept.append(y)
    end = y
    x = y
    for k in range(STEPS - 2, -1, -1):
        x = step_minus(kept[k], rows(chain_ref, (STEPS + k) * SIZE, SIZE), x)
    for v in range(VARS):
        put(source_ref, STEPS * VARS + v, end[v])
        put(source_ref, STEPS * VARS + VARS + v, x[v])
    ahead = rows(lines_ref, 0, SIZE)
    mixed = rows(lines_ref, SIZE, SIZE)
    behind = rows(lines_ref, 2 * SIZE, SIZE)
    whole_end = plus(swap(end), matvec(swap(ahead), end))
    inner = plus(swap(x), matvec(swap(mixed), end))
    whole_first = plus(x, matvec(behind, inner))
    values = whole_end + whole_first + [jnp.zeros((8, 128), F32)] * (4 * VEC_GROUPS - 2 * VARS)
    if groups == FULL_GROUPS:
        arrive(maps_copies)
    pack_lines(packed_ref, 0, block, values, 0, groups)


def shift_in(sub, values, entry):
    return [jnp.where(sub == 0, e, pltpu.roll(x, 1, 0)) for x, e in zip(values, entry)]


def shift_out(sub, values, entry):
    return [jnp.where(sub == 7, e, pltpu.roll(x, 7, 0)) for x, e in zip(values, entry)]


def reduced_kernel(first, recv_ref, *rest):
    maps_recv_ref = recv_ref if first else rest[0]
    out_ref, maps_ref = rest[-2:]
    sub, lane = iotas()
    block = lane // 32

    def stacked(ref, groups, r, part):
        values = ref[pl.ds(part * 8 * groups + r // 4, 8, stride=groups), :]
        return lane_roll(values, -32 * (r % 4))

    def value(r, part):
        return stacked(recv_ref, FULL_GROUPS if first else VEC_GROUPS, r, part)

    for r in range(3 * SIZE):
        for part in range(2):
            put(maps_ref, part * 3 * SIZE + r, stacked(maps_recv_ref, FULL_GROUPS, 4 * VEC_GROUPS + r, part))
    zero = [jnp.zeros((8, 128), F32)] * VARS

    def solve(part, which, source, entry, shift):
        maps = rows(maps_ref, part * 3 * SIZE + which * SIZE, SIZE)

        def step(_, now):
            return step_plus(source, maps, shift(sub, now, entry))

        out = lax.fori_loop(0, 7, step, step_plus(source, maps, shift(sub, zero, entry)))
        return out, shift(sub, out, entry)

    ends = [[value(r, part) for r in range(VARS)] for part in range(2)]
    firsts = [[value(VARS + r, part) for r in range(VARS)] for part in range(2)]
    out, low_entry = solve(0, 0, ends[0], zero, shift_in)
    out, high_entry = solve(1, 0, ends[1], [pltpu.roll(x, 1, 0) for x in out], shift_in)
    entries = [low_entry, high_entry]
    drive = [
        plus(firsts[part], matvec(rows(maps_ref, part * 3 * SIZE + SIZE, SIZE), entries[part])) for part in range(2)
    ]
    out, high_next = solve(1, 2, drive[1], zero, shift_out)
    out, low_next = solve(0, 2, drive[0], [pltpu.roll(x, 7, 0) for x in out], shift_out)
    nexts = [low_next, high_next]
    for part in range(2):
        values = entries[part] + nexts[part] + zero + zero[:1]
        for g in range(VEC_GROUPS):
            packed = blocks4(block, [lane_roll(values[4 * g + p], 32 * p) for p in range(4)])
            out_ref[pl.ds(part * 8 * VEC_GROUPS + g, 8, stride=VEC_GROUPS), :] = packed


def finish_kernel(last, recv_ref, u_ref, source_ref, chain_ref, lines_ref, *rest):
    if last:
        out_hbm, new_ref, out_ref, sems = rest
    else:
        sent_hbm, last_ref, first_ref, new_ref, sems = rest
    copies = []
    sub, lane = iotas()
    block = lane // 32
    top = sub < TILES
    stacked = [
        [
            recv_ref[pl.ds(q * VEC_GROUPS + g, TILES, stride=4 * VEC_GROUPS), :]
            for g in range((2 * VARS + 3) // 4)
        ]
        for q in range(4)
    ]
    stacked = [[jnp.concatenate([x, x], axis=0) for x in line] for line in stacked]

    def value(r):
        return blocks4(block, [lane_roll(stacked[q][r // 4], 32 * (q - r % 4)) for q in range(4)])

    entry = [value(r) for r in range(VARS)]
    after = [value(VARS + r) for r in range(VARS)]
    end = rows(source_ref, STEPS * VARS, VARS)
    begin = rows(source_ref, STEPS * VARS + VARS, VARS)
    middle = plus(end, matvec(rows(lines_ref, 0, SIZE), entry))
    start = pick(top, entry, swap(middle))
    follow = plus(
        plus(begin, matvec(rows(lines_ref, SIZE, SIZE), start)),
        matvec(rows(lines_ref, 2 * SIZE, SIZE), after),
    )
    finish = pick(top, swap(follow), after)
    y = start
    kept = []
    for k in range(STEPS):
        y = step_minus(rows(source_ref, k * VARS, VARS), rows(chain_ref, k * SIZE, SIZE), y)
        kept.append(y)
    x = finish
    for k in range(STEPS - 1, -1, -1):
        x = step_minus(kept[k], rows(chain_ref, (STEPS + k) * SIZE, SIZE), x)
        for v in range(VARS):
            put(new_ref, k * VARS + v, row(u_ref, k * VARS + v) + x[v])
        if not last:
            copies.append(piece_out(new_ref, sent_hbm, sems, k, VARS * 8))
    if last:
        for v in range(VARS):
            for half in range(2):
                for t in range(TILES):
                    tile = new_ref[pl.ds(v * 8 + half * TILES + t, STEPS, stride=VARS * 8), :]
                    out_ref[v, half * STEPS : (half + 1) * STEPS, t * 128 : (t + 1) * 128] = tile
            copies.append(pltpu.make_async_copy(out_ref.at[v], out_hbm.at[v], sems.at[v]))
            copies[-1].start()
    else:
        edge_lines(sub, lane, rows(new_ref, 0, STEPS * VARS), last_ref, first_ref)
        pairs = rows(source_ref, KEPT + VARS, (SIZE + 1) // 2)
        blocks = [pairs[n // 2] if n % 2 else pltpu.roll(pairs[n // 2], 4, 0) for n in range(SIZE)]
        before = minus(entry, matvec(blocks, swap(x)))
        for v in range(VARS):
            put(new_ref, BELOW + v, row(source_ref, KEPT + v) + before[v])
            put(new_ref, ABOVE + v, row(source_ref, KEPT + UP // 8 + v) + after[v])
    arrive(copies)


def call(kernel, shapes, *args, scratch=(), flops=100_000, limit=8, far=0, sent=()):
    outs = [pltpu.HBM(shape, F32) if n in sent else jax.ShapeDtypeStruct(shape, F32) for n, shape in enumerate(shapes)]
    moved = 4 * (sum(math.prod(shape) for shape in shapes) + sum(a.size for a in args))
    near = len(args) - far
    specs = [pl.BlockSpec(memory_space=pltpu.VMEM if n < near else pltpu.HBM) for n in range(len(args))]
    args = args[:near] + tuple(pltpu.with_memory_space_constraint(a, pltpu.HBM) for a in args[near:])
    return pl.pallas_call(
        kernel,
        out_shape=outs,
        in_specs=specs,
        out_specs=[pl.BlockSpec(memory_space=pltpu.HBM if n in sent else pltpu.VMEM) for n in range(len(outs))],
        scratch_shapes=[pltpu.VMEM(item, F32) if isinstance(item, tuple) else item for item in scratch],
        cost_estimate=pl.CostEstimate(flops=flops, bytes_accessed=moved, transcendentals=0),
        compiler_params=pltpu.CompilerParams(vmem_limit_bytes=limit * 1024 * 1024),
    )(*args)


def exchange(value, axis, count):
    shape = value.shape
    out = lax.all_to_all(value.reshape(count, shape[0] // count, 128), axis, 0, 0)
    return out.reshape(shape)


def moved(value, axis, step, wrap):
    count = lax.axis_size(axis)
    pairs = [(i, (i + step) % count) for i in range(count) if wrap or 0 <= i + step < count]
    return lax.ppermute(value, axis, pairs)


def body(state, source_terms, pivot_inverse, coupling, back_coupling, wall_flags):
    weights = np.float32(-0.5 * spectral())
    edge = (8, 128)
    halo = (VARS * 8, 128)
    raw_field = (VARS, 2 * STEPS, TILES * 128)
    raw_matrix = (VARS,) + raw_field
    cells_first = state[0].transpose(1, 0, 2)
    sent = cells_first.reshape(VARS, 2, STEPS, TILES, 128).transpose(0, 1, 3, 2, 4).reshape(FIELD, 128)
    u, last_line, first_line, chain, up, above = call(
        pack_kernel, [(FIELD, 128), edge, edge, (CHAIN, 128), (UP, 128), halo],
        cells_first, coupling[0].transpose(1, 2, 0, 3), back_coupling[0].transpose(1, 2, 0, 3),
        scratch=[raw_field, raw_matrix, raw_matrix, pltpu.SemaphoreType.DMA((3 * VARS,))], far=3,
        limit=12,
    )
    up = moved(up, "axial", 1, False)
    above = moved(above, "axial", -1, False)
    stage = [(FIELD, 128), pltpu.SemaphoreType.DMA((INST,))]
    for sweep in range(SWEEPS):
        first = sweep == 0
        last = sweep == SWEEPS - 1
        spread = exchange(sent, "inst", INST)
        if first:
            term, right, left = call(
                lambda *refs: time_kernel(weights, 2, *refs), [(FIELD, 128), edge, edge],
                spread, first_line, last_line, up, above, scratch=stage, sent=(0,),
            )
            left = moved(left, "span", 1, True)
        else:
            left = moved(last_line, "span", 1, True)
            term, right = call(
                lambda *refs: time_kernel(weights, 1, *refs), [(FIELD, 128), edge],
                spread, first_line, left, scratch=stage, sent=(0,),
            )
        if first:
            lines, packed_maps = call(
                maps_kernel,
                [(LINES, 128), (SEGMENTS * FULL_GROUPS, 128)],
                chain, right, pivot_inverse[0].transpose(1, 2, 0, 3), source_terms[0].transpose(1, 0, 2), wall_flags,
                scratch=[
                    (MATRIX, 128), (STEPS * 8, 128), raw_matrix, raw_field,
                    pltpu.VMEM((2 * STEPS, TILES * 128), jnp.int32), (SEGMENTS * FULL_GROUPS, 128),
                    pltpu.SemaphoreType.DMA((2 * VARS + 2,)),
                ],
                flops=8_000_000,
                limit=16,
                far=3,
                sent=(1,),
            )
        right = moved(right, "span", -1, True)
        time = exchange(term, "inst", INST)
        groups = FULL_GROUPS if first else VEC_GROUPS
        source, packed = call(
            local_kernel,
            [(KEPT * 8 + (UP + halo[0] if first else 0), 128), (SEGMENTS * groups, 128)],
            time, u, chain, lines, left, right, *((up, above, packed_maps) if first else ()),
            scratch=[(FIELD, 128)] + ([pltpu.SemaphoreType.DMA((4,))] if first else []), far=1 if first else 0,
        )
        recv = exchange(packed, "axial", SEGMENTS)
        if first:
            maps_recv = recv
        (solved,) = call(
            lambda *refs, f=first: reduced_kernel(f, *refs),
            [(SEGMENTS * VEC_GROUPS, 128)], recv, *(() if first else (maps_recv,)),
            scratch=[(6 * SIZE * 8, 128)],
        )
        back_recv = exchange(solved, "axial", SEGMENTS)
        common = (back_recv, u, source, chain, lines)
        if last:
            (result,) = call(
                lambda *refs: finish_kernel(True, *refs), [raw_field], *common,
                scratch=[(FIELD, 128), raw_field, pltpu.SemaphoreType.DMA((VARS,))], sent=(0,),
            )
        else:
            sent, last_line, first_line, u = call(
                lambda *refs: finish_kernel(False, *refs), [(FIELD, 128), edge, edge, (FIELD + 2 * halo[0], 128)],
                *common, scratch=[pltpu.SemaphoreType.DMA((STEPS,))], sent=(0,),
            )
    return result.transpose(1, 0, 2)[None]


def solution(mesh):
    return jax.shard_map(
        body,
        mesh=mesh,
        in_specs=(
            P("inst", "axial", None, "span"),
            P("inst", "axial", None, "span"),
            P("inst", "axial", None, None, "span"),
            P("inst", "axial", None, None, "span"),
            P("inst", "axial", None, None, "span"),
            P("axial", "span"),
        ),
        out_specs=P("inst", "axial", None, "span"),
        check_vma=False,
    )
```

```python
import math

import jax
import jax.numpy as jnp
import numpy as np
from jax import lax
from jax.experimental import pallas as pl
from jax.experimental.pallas import tpu as pltpu
from jax.sharding import PartitionSpec as P

INST = 8
SWEEPS = 2
VARS = 5
STEPS = 8
TILES = 4
SEGMENTS = 16
F32 = jnp.float32
FIELD = STEPS * VARS * 8
MATRIX = STEPS * VARS * VARS * 8
SIZE = VARS * VARS
FULL_GROUPS = 24
VEC_GROUPS = 4
CHAIN = 2 * MATRIX
PIVOT = 3 * SIZE * 8
CELLS = PIVOT + MATRIX
LINES = CELLS + FIELD
UP = VARS * 8 + (SIZE + 1) // 2 * 8
BELOW = STEPS * VARS
ABOVE = BELOW + VARS
KEPT = STEPS * VARS + 2 * VARS


def spectral():
    index = np.arange(INST)
    diff = index[:, None] - index[None, :]
    sign = 1.0 - 2.0 * np.mod(diff, 2)
    safe = np.where(diff == 0, 0.5 * math.pi, math.pi * diff / INST)
    first = np.where(diff == 0, 0.0, 0.5 * sign * np.cos(safe) / np.sin(safe))
    second = np.where(diff == 0, -(INST * INST + 2.0) / 12.0, -0.5 * sign / np.sin(safe) ** 2)
    return first - 0.5 * second


def iotas():
    sub = lax.broadcasted_iota(jnp.int32, (8, 128), 0)
    lane = lax.broadcasted_iota(jnp.int32, (8, 128), 1)
    return sub, lane


def row(ref, index):
    return ref[pl.ds(pl.multiple_of(index * 8, 8), 8), :]


def rows(ref, start, count):
    return [row(ref, start + n) for n in range(count)]


def put(ref, index, value):
    ref[pl.ds(pl.multiple_of(index * 8, 8), 8), :] = value


def total(terms):
    terms = list(terms)
    while len(terms) > 1:
        terms = [terms[n] + terms[n + 1] if n + 1 < len(terms) else terms[n] for n in range(0, len(terms), 2)]
    return terms[0]


def matvec(m, v):
    return [total(m[i * VARS + j] * v[j] for j in range(VARS)) for i in range(VARS)]


def step_minus(source, m, v):
    out = []
    for i in range(VARS):
        t = [m[i * VARS + j] * v[j] for j in range(VARS)]
        out.append(((source[i] - t[0]) - (t[1] + t[2])) - (t[3] + t[4]))
    return out


def step_plus(source, m, v):
    out = []
    for i in range(VARS):
        t = [m[i * VARS + j] * v[j] for j in range(VARS)]
        out.append(((source[i] + t[0]) + (t[1] + t[2])) + (t[3] + t[4]))
    return out


def matmul(a, b):
    out = [None] * SIZE
    for m in range(VARS):
        column = [b[j * VARS + m] for j in range(VARS)]
        for i in range(VARS):
            t = [a[i * VARS + j] * column[j] for j in range(VARS)]
            out[i * VARS + m] = (t[0] + t[1]) + (t[2] + t[3]) + t[4]
    return out


def plus(a, b):
    return [x + y for x, y in zip(a, b)]


def minus(a, b):
    return [x - y for x, y in zip(a, b)]


def swap(a):
    return [pltpu.roll(x, 4, 0) for x in a]


def pick(mask, a, b):
    return [jnp.where(mask, x, y) for x, y in zip(a, b)]


def lane_roll(x, shift):
    shift = shift % 128
    return x if shift == 0 else pltpu.roll(x, shift, 1)


def blocks4(block, parts):
    out = parts[0]
    for p in range(1, 4):
        out = jnp.where(block == p, parts[p], out)
    return out


def blocks4(block, parts):
    out = parts[0]
    for p in range(1, 4):
        out = jnp.where(block == p, parts[p], out)
    return out


def pack_lines(out_ref, start, block, values, first, groups):
    for g in range((len(values) + 3) // 4):
        four = [values[min(4 * g + p, len(values) - 1)] for p in range(4)]
        for q in range(4):
            chunk = blocks4(block, [lane_roll(four[p], 32 * (p - q)) for p in range(4)])
            out_ref[pl.ds(start + q * groups + first + g, 4, stride=4 * groups), :] = chunk[:4]


def edge_lines(sub, lane, u, last_ref, first_ref):
    last = jnp.zeros((8, 128), F32)
    initial = jnp.zeros((8, 128), F32)
    for n in range(STEPS * VARS):
        last = jnp.where(lane == n, lane_roll(u[n], n - 127), last)
        initial = jnp.where(lane == n, lane_roll(u[n], n), initial)
    last_ref[...] = pltpu.roll(last, 5, 0)
    first_ref[...] = pltpu.roll(initial, 3, 0)


def field_to_packed(raw_ref, out_ref, start=0):
    for v in range(VARS):
        for half in range(2):
            for t in range(TILES):
                tile = raw_ref[v, half * STEPS : (half + 1) * STEPS, t * 128 : (t + 1) * 128]
                out_ref[pl.ds(start + v * 8 + half * TILES + t, STEPS, stride=VARS * 8), :] = tile


def matrix_to_packed(raw_ref, out_ref, start=0):
    for i in range(VARS):
        for j in range(VARS):
            for half in range(2):
                for t in range(TILES):
                    tile = raw_ref[i, j, half * STEPS : (half + 1) * STEPS, t * 128 : (t + 1) * 128]
                    begin = start + (i * VARS + j) * 8 + half * TILES + t
                    out_ref[pl.ds(begin, STEPS, stride=SIZE * 8), :] = tile


def fetch(source, target, sems, first):
    copies = [pltpu.make_async_copy(source.at[i], target.at[i], sems.at[first + i]) for i in range(VARS)]
    for copy in copies:
        copy.start()
    return copies


def arrive(copies):
    for copy in copies:
        copy.wait()


def halo_kernel(state_hbm, back_hbm, up_ref, down_ref, state_ref, back_ref, sems):
    copies = fetch(state_hbm, state_ref, sems, 0)
    for i in range(VARS):
        upper = back_hbm.at[i, :, pl.ds(STEPS, STEPS), :]
        copies.append(pltpu.make_async_copy(upper, back_ref.at[i], sems.at[VARS + i]))
        copies[-1].start()
    up_ref[...] = jnp.zeros(up_ref.shape, F32)
    down_ref[...] = jnp.zeros(down_ref.shape, F32)
    arrive(copies)
    for t in range(TILES):
        lines = slice(t * 128, (t + 1) * 128)
        for v in range(VARS):
            begin = v * 8 + TILES + t
            up_ref[begin : begin + 1, :] = state_ref[v, 2 * STEPS - 1 : 2 * STEPS, lines]
            down_ref[v * 8 + t : v * 8 + t + 1, :] = state_ref[v, 0:1, lines]
        for n in range(SIZE):
            begin = (VARS + n // 2) * 8 + n % 2 * TILES + t
            up_ref[begin : begin + 1, :] = back_ref[n // VARS, n % VARS, STEPS - 1 : STEPS, lines]


def pack_kernel(
    state_hbm, coupling_hbm, back_hbm, u_ref, last_ref, first_ref, chain_ref,
    state_ref, coupling_raw, back_raw, sems,
):
    sub, lane = iotas()
    state_copies = fetch(state_hbm, state_ref, sems, 0)
    coupling_copies = fetch(coupling_hbm, coupling_raw, sems, VARS)
    back_copies = fetch(back_hbm, back_raw, sems, 2 * VARS)
    arrive(state_copies)
    field_to_packed(state_ref, u_ref)
    edge_lines(sub, lane, rows(u_ref, 0, STEPS * VARS), last_ref, first_ref)
    arrive(coupling_copies)
    matrix_to_packed(coupling_raw, chain_ref, 0)
    arrive(back_copies)
    matrix_to_packed(back_raw, chain_ref, MATRIX)


def piece_out(stage_ref, out_hbm, sems, index, count):
    piece = pl.ds(index * count, count)
    copy = pltpu.make_async_copy(stage_ref.at[piece], out_hbm.at[piece], sems.at[index])
    copy.start()
    return copy


def time_term(weights, spread_ref, out_hbm, stage_ref, sems):
    copies = []
    for i in range(INST):
        for v in range(VARS):
            terms = [row(spread_ref, j * VARS + v) * F32(weights[i, j]) for j in range(INST)]
            put(stage_ref, i * VARS + v, total(terms))
        copies.append(piece_out(stage_ref, out_hbm, sems, i, VARS * 8))
    return copies


def time_kernel(weights, count, spread_ref, *rest):
    out_hbm, *passed_refs, stage_ref, sems = rest[-3 - count :]
    copies = time_term(weights, spread_ref, out_hbm, stage_ref, sems)
    for line_ref, passed_ref in zip(rest, passed_refs):
        passed_ref[...] = line_ref[...]
    arrive(copies)


def maps_kernel(
    chain_ref, after_ref, pivot_hbm, source_hbm, flags_hbm,
    lines_ref, packed_hbm,
    prefix_ref, keep_ref, pivot_raw, source_raw, flags_ref, packed_ref, sems,
):
    sub, lane = iotas()
    block = lane // 32
    pivot_copies = fetch(pivot_hbm, pivot_raw, sems, 0)
    source_copies = fetch(source_hbm, source_raw, sems, VARS)
    flags_copy = pltpu.make_async_copy(flags_hbm, flags_ref, sems.at[2 * VARS])
    flags_copy.start()
    top = sub < TILES
    def coupling(k):
        return rows(chain_ref, k * SIZE, SIZE)

    def back(k):
        return rows(chain_ref, STEPS * SIZE + k * SIZE, SIZE)

    def forward(k, p):
        p = [-x for x in matmul(coupling(k), p)]
        for n in range(SIZE):
            put(prefix_ref, k * SIZE + n, p[n])
        return p

    first = [-x for x in coupling(0)]
    for n in range(SIZE):
        put(prefix_ref, n, first[n])
    ahead = lax.fori_loop(1, STEPS, forward, first)

    def backward(step, carry):
        k = STEPS - 2 - step
        return minus(rows(prefix_ref, k * SIZE, SIZE), matmul(back(k), carry))

    mixed = lax.fori_loop(0, STEPS - 1, backward, ahead)

    def behind_step(step, carry):
        return [-x for x in matmul(back(STEPS - 2 - step), carry)]

    behind = lax.fori_loop(0, STEPS - 1, behind_step, [-x for x in back(STEPS - 1)])
    for n in range(SIZE):
        put(lines_ref, n, ahead[n])
        put(lines_ref, SIZE + n, mixed[n])
        put(lines_ref, 2 * SIZE + n, behind[n])
    whole = matmul(swap(ahead), ahead)
    for n in range(SIZE):
        put(prefix_ref, n, whole[n])
    whole = plus(mixed, matmul(behind, matmul(swap(mixed), ahead)))
    for n in range(SIZE):
        put(prefix_ref, SIZE + n, whole[n])
    whole = matmul(behind, swap(behind))
    for n in range(SIZE):
        put(prefix_ref, 2 * SIZE + n, whole[n])
    pack_lines(packed_ref, 0, block, rows(prefix_ref, 0, 3 * SIZE), VEC_GROUPS, FULL_GROUPS)
    packed_copy = pltpu.make_async_copy(packed_ref, packed_hbm, sems.at[2 * VARS + 1])
    packed_copy.start()
    arrive(pivot_copies)
    matrix_to_packed(pivot_raw, lines_ref, PIVOT)
    arrive(source_copies)
    field_to_packed(source_raw, lines_ref, CELLS)
    flags_copy.wait()
    for half in range(2):
        for t in range(TILES):
            flags = flags_ref[half * STEPS : (half + 1) * STEPS, t * 128 : (t + 1) * 128]
            keep_ref[pl.ds(half * TILES + t, STEPS, stride=8), :] = (1 - flags).astype(F32)

    def mask(k, carry):
        keep = row(keep_ref, k)
        for n in range(SIZE):
            put(lines_ref, PIVOT // 8 + k * SIZE + n, keep * row(lines_ref, PIVOT // 8 + k * SIZE + n))
        return carry

    lax.fori_loop(0, STEPS, mask, 0)
    packed_copy.wait()


def stencil(
    sub, lane, u_ref, lines_ref, below_ref, below_at, above_ref, above_at, left_ref, right_ref, time_ref, out_ref
):
    top = sub < TILES
    left_all = left_ref[...]
    right_all = right_ref[...]
    for k in range(STEPS):
        for v in range(VARS):
            n = k * VARS + v
            u = row(u_ref, n)
            if k == 0:
                below = pltpu.roll(jnp.where(top, row(u_ref, (STEPS - 1) * VARS + v), row(below_ref, below_at + v)), 4, 0)
            else:
                below = row(u_ref, n - VARS)
            if k == STEPS - 1:
                above = pltpu.roll(jnp.where(top, row(above_ref, above_at + v), row(u_ref, v)), 4, 0)
            else:
                above = row(u_ref, n + VARS)
            turned = pltpu.roll(u, 1, 1)
            edge = jnp.where(sub % TILES == 0, lane_roll(left_all, -n), pltpu.roll(turned, 1, 0))
            left = jnp.where(lane == 0, edge, turned)
            turned = pltpu.roll(u, 127, 1)
            edge = jnp.where(sub % TILES == TILES - 1, lane_roll(right_all, 127 - n), pltpu.roll(turned, 7, 0))
            right = jnp.where(lane == 127, edge, turned)
            value = row(lines_ref, CELLS // 8 + n) - 0.1 * above + 0.5 * below - 0.8 * u + 0.2 * (left + right)
            put(out_ref, n, value + row(time_ref, n))


def local_kernel(time_ref, u_ref, chain_ref, lines_ref, left_ref, right_ref, *rest):
    sub, lane = iotas()
    block = lane // 32
    if len(rest) > 3:
        below_ref, above_ref, maps_hbm, source_ref, packed_ref, rhs_ref, sems = rest
        below_at, above_at, groups = 0, 0, FULL_GROUPS
        maps_copies = [piece_out(maps_hbm, packed_ref, sems, n, SEGMENTS * FULL_GROUPS // 4) for n in range(4)]
        source_ref[KEPT * 8 : KEPT * 8 + UP, :] = below_ref[...]
        source_ref[KEPT * 8 + UP :, :] = above_ref[...]
        for n in range(STEPS * VARS):
            v, tile = n // 8, n % 8
            rhs_ref[pl.ds(v * 8 + tile, STEPS, stride=VARS * 8), :] = row(time_ref, n)
        time_ref = rhs_ref
    else:
        source_ref, packed_ref, rhs_ref = rest
        below_ref = above_ref = u_ref
        below_at, above_at, groups = BELOW, ABOVE, VEC_GROUPS
    stencil(
        sub, lane, u_ref, lines_ref, below_ref, below_at, above_ref, above_at, left_ref, right_ref, time_ref, rhs_ref
    )

    def source_step(k, carry):
        rhs = rows(rhs_ref, k * VARS, VARS)
        for v, value in enumerate(matvec(rows(lines_ref, PIVOT // 8 + k * SIZE, SIZE), rhs)):
            put(source_ref, k * VARS + v, value)
        return carry

    lax.fori_loop(0, STEPS, source_step, 0, unroll=True)
    y = rows(source_ref, 0, VARS)
    kept = [y]
    for k in range(1, STEPS):
        y = step_minus(rows(source_ref, k * VARS, VARS), rows(chain_ref, k * SIZE, SIZE), y)
        kept.append(y)
    end = y
    x = y
    for k in range(STEPS - 2, -1, -1):
        x = step_minus(kept[k], rows(chain_ref, (STEPS + k) * SIZE, SIZE), x)
    for v in range(VARS):
        put(source_ref, STEPS * VARS + v, end[v])
        put(source_ref, STEPS * VARS + VARS + v, x[v])
    ahead = rows(lines_ref, 0, SIZE)
    mixed = rows(lines_ref, SIZE, SIZE)
    behind = rows(lines_ref, 2 * SIZE, SIZE)
    whole_end = plus(swap(end), matvec(swap(ahead), end))
    inner = plus(swap(x), matvec(swap(mixed), end))
    whole_first = plus(x, matvec(behind, inner))
    values = whole_end + whole_first + [jnp.zeros((8, 128), F32)] * (4 * VEC_GROUPS - 2 * VARS)
    if groups == FULL_GROUPS:
        arrive(maps_copies)
    pack_lines(packed_ref, 0, block, values, 0, groups)


def shift_in(sub, values, entry):
    return [jnp.where(sub == 0, e, pltpu.roll(x, 1, 0)) for x, e in zip(values, entry)]


def shift_out(sub, values, entry):
    return [jnp.where(sub == 7, e, pltpu.roll(x, 7, 0)) for x, e in zip(values, entry)]


def reduced_kernel(first, recv_ref, *rest):
    maps_recv_ref = recv_ref if first else rest[0]
    out_ref, maps_ref = rest[-2:]
    sub, lane = iotas()
    block = lane // 32

    def stacked(ref, groups, r, part):
        values = ref[pl.ds(part * 8 * groups + r // 4, 8, stride=groups), :]
        return lane_roll(values, -32 * (r % 4))

    def value(r, part):
        return stacked(recv_ref, FULL_GROUPS if first else VEC_GROUPS, r, part)

    for r in range(3 * SIZE):
        for part in range(2):
            put(maps_ref, part * 3 * SIZE + r, stacked(maps_recv_ref, FULL_GROUPS, 4 * VEC_GROUPS + r, part))
    zero = [jnp.zeros((8, 128), F32)] * VARS

    def solve(part, which, source, entry, shift):
        maps = rows(maps_ref, part * 3 * SIZE + which * SIZE, SIZE)

        def step(_, now):
            return step_plus(source, maps, shift(sub, now, entry))

        out = lax.fori_loop(0, 7, step, step_plus(source, maps, shift(sub, zero, entry)), unroll=True)
        return out, shift(sub, out, entry)

    ends = [[value(r, part) for r in range(VARS)] for part in range(2)]
    firsts = [[value(VARS + r, part) for r in range(VARS)] for part in range(2)]
    out, low_entry = solve(0, 0, ends[0], zero, shift_in)
    out, high_entry = solve(1, 0, ends[1], [pltpu.roll(x, 1, 0) for x in out], shift_in)
    entries = [low_entry, high_entry]
    drive = [
        plus(firsts[part], matvec(rows(maps_ref, part * 3 * SIZE + SIZE, SIZE), entries[part])) for part in range(2)
    ]
    out, high_next = solve(1, 2, drive[1], zero, shift_out)
    out, low_next = solve(0, 2, drive[0], [pltpu.roll(x, 7, 0) for x in out], shift_out)
    nexts = [low_next, high_next]
    for part in range(2):
        values = entries[part] + nexts[part] + zero + zero[:1]
        for g in range(VEC_GROUPS):
            packed = blocks4(block, [lane_roll(values[4 * g + p], 32 * p) for p in range(4)])
            out_ref[pl.ds(part * 8 * VEC_GROUPS + g, 8, stride=VEC_GROUPS), :] = packed


def finish_kernel(last, recv_ref, u_ref, source_ref, chain_ref, lines_ref, *rest):
    if last:
        out_hbm, new_ref, out_ref, sems = rest
    else:
        sent_hbm, last_ref, first_ref, new_ref, sems = rest
    copies = []
    sub, lane = iotas()
    block = lane // 32
    top = sub < TILES
    stacked = [
        [
            recv_ref[pl.ds(q * VEC_GROUPS + g, TILES, stride=4 * VEC_GROUPS), :]
            for g in range((2 * VARS + 3) // 4)
        ]
        for q in range(4)
    ]
    stacked = [[jnp.concatenate([x, x], axis=0) for x in line] for line in stacked]

    def value(r):
        return blocks4(block, [lane_roll(stacked[q][r // 4], 32 * (q - r % 4)) for q in range(4)])

    entry = [value(r) for r in range(VARS)]
    after = [value(VARS + r) for r in range(VARS)]
    end = rows(source_ref, STEPS * VARS, VARS)
    begin = rows(source_ref, STEPS * VARS + VARS, VARS)
    middle = plus(end, matvec(rows(lines_ref, 0, SIZE), entry))
    start = pick(top, entry, swap(middle))
    follow = plus(
        plus(begin, matvec(rows(lines_ref, SIZE, SIZE), start)),
        matvec(rows(lines_ref, 2 * SIZE, SIZE), after),
    )
    finish = pick(top, swap(follow), after)
    y = start
    kept = []
    for k in range(STEPS):
        y = step_minus(rows(source_ref, k * VARS, VARS), rows(chain_ref, k * SIZE, SIZE), y)
        kept.append(y)
    x = finish
    for k in range(STEPS - 1, -1, -1):
        x = step_minus(kept[k], rows(chain_ref, (STEPS + k) * SIZE, SIZE), x)
        for v in range(VARS):
            put(new_ref, k * VARS + v, row(u_ref, k * VARS + v) + x[v])
        if not last:
            copies.append(piece_out(new_ref, sent_hbm, sems, k, VARS * 8))
    if last:
        for v in range(VARS):
            for half in range(2):
                for t in range(TILES):
                    tile = new_ref[pl.ds(v * 8 + half * TILES + t, STEPS, stride=VARS * 8), :]
                    out_ref[v, half * STEPS : (half + 1) * STEPS, t * 128 : (t + 1) * 128] = tile
            copies.append(pltpu.make_async_copy(out_ref.at[v], out_hbm.at[v], sems.at[v]))
            copies[-1].start()
    else:
        edge_lines(sub, lane, rows(new_ref, 0, STEPS * VARS), last_ref, first_ref)
        pairs = rows(source_ref, KEPT + VARS, (SIZE + 1) // 2)
        blocks = [pairs[n // 2] if n % 2 else pltpu.roll(pairs[n // 2], 4, 0) for n in range(SIZE)]
        before = minus(entry, matvec(blocks, swap(x)))
        for v in range(VARS):
            put(new_ref, BELOW + v, row(source_ref, KEPT + v) + before[v])
            put(new_ref, ABOVE + v, row(source_ref, KEPT + UP // 8 + v) + after[v])
    arrive(copies)


def call(kernel, shapes, *args, scratch=(), flops=100_000, limit=8, far=0, sent=()):
    outs = [pltpu.HBM(shape, F32) if n in sent else jax.ShapeDtypeStruct(shape, F32) for n, shape in enumerate(shapes)]
    moved = 4 * (sum(math.prod(shape) for shape in shapes) + sum(a.size for a in args))
    near = len(args) - far
    specs = [pl.BlockSpec(memory_space=pltpu.VMEM if n < near else pltpu.HBM) for n in range(len(args))]
    args = args[:near] + tuple(pltpu.with_memory_space_constraint(a, pltpu.HBM) for a in args[near:])
    return pl.pallas_call(
        kernel,
        out_shape=outs,
        in_specs=specs,
        out_specs=[pl.BlockSpec(memory_space=pltpu.HBM if n in sent else pltpu.VMEM) for n in range(len(outs))],
        scratch_shapes=[pltpu.VMEM(item, F32) if isinstance(item, tuple) else item for item in scratch],
        cost_estimate=pl.CostEstimate(flops=flops, bytes_accessed=moved, transcendentals=0),
        compiler_params=pltpu.CompilerParams(vmem_limit_bytes=limit * 1024 * 1024),
    )(*args)


def exchange(value, axis, count):
    shape = value.shape
    out = lax.all_to_all(value.reshape(count, shape[0] // count, 128), axis, 0, 0)
    return out.reshape(shape)


def moved(value, axis, step, wrap):
    count = lax.axis_size(axis)
    pairs = [(i, (i + step) % count) for i in range(count) if wrap or 0 <= i + step < count]
    return lax.ppermute(value, axis, pairs)


def body(state, source_terms, pivot_inverse, coupling, back_coupling, wall_flags):
    weights = np.float32(-0.5 * spectral())
    edge = (8, 128)
    halo = (VARS * 8, 128)
    raw_field = (VARS, 2 * STEPS, TILES * 128)
    raw_matrix = (VARS,) + raw_field
    cells_first = state[0].transpose(1, 0, 2)
    sent = cells_first.reshape(VARS, 2, STEPS, TILES, 128).transpose(0, 1, 3, 2, 4).reshape(FIELD, 128)
    backs = back_coupling[0].transpose(1, 2, 0, 3)
    up, above = call(
        halo_kernel, [(UP, 128), halo], cells_first, backs,
        scratch=[raw_field, (VARS, VARS, STEPS, TILES * 128), pltpu.SemaphoreType.DMA((2 * VARS,))], far=2,
    )
    u, last_line, first_line, chain = call(
        pack_kernel, [(FIELD, 128), edge, edge, (CHAIN, 128)],
        cells_first, coupling[0].transpose(1, 2, 0, 3), backs,
        scratch=[raw_field, raw_matrix, raw_matrix, pltpu.SemaphoreType.DMA((3 * VARS,))], far=3,
        limit=12,
    )
    up = moved(up, "axial", 1, False)
    above = moved(above, "axial", -1, False)
    stage = [(FIELD, 128), pltpu.SemaphoreType.DMA((INST,))]
    for sweep in range(SWEEPS):
        first = sweep == 0
        last = sweep == SWEEPS - 1
        spread = exchange(sent, "inst", INST)
        if first:
            term, right, left = call(
                lambda *refs: time_kernel(weights, 2, *refs), [(FIELD, 128), edge, edge],
                spread, first_line, last_line, up, above, scratch=stage, sent=(0,),
            )
            left = moved(left, "span", 1, True)
        else:
            left = moved(last_line, "span", 1, True)
            term, right = call(
                lambda *refs: time_kernel(weights, 1, *refs), [(FIELD, 128), edge],
                spread, first_line, left, scratch=stage, sent=(0,),
            )
        if first:
            lines, packed_maps = call(
                maps_kernel,
                [(LINES, 128), (SEGMENTS * FULL_GROUPS, 128)],
                chain, right, pivot_inverse[0].transpose(1, 2, 0, 3), source_terms[0].transpose(1, 0, 2), wall_flags,
                scratch=[
                    (MATRIX, 128), (STEPS * 8, 128), raw_matrix, raw_field,
                    pltpu.VMEM((2 * STEPS, TILES * 128), jnp.int32), (SEGMENTS * FULL_GROUPS, 128),
                    pltpu.SemaphoreType.DMA((2 * VARS + 2,)),
                ],
                flops=8_000_000,
                limit=16,
                far=3,
                sent=(1,),
            )
        right = moved(right, "span", -1, True)
        time = exchange(term, "inst", INST)
        groups = FULL_GROUPS if first else VEC_GROUPS
        source, packed = call(
            local_kernel,
            [(KEPT * 8 + (UP + halo[0] if first else 0), 128), (SEGMENTS * groups, 128)],
            time, u, chain, lines, left, right, *((up, above, packed_maps) if first else ()),
            scratch=[(FIELD, 128)] + ([pltpu.SemaphoreType.DMA((4,))] if first else []), far=1 if first else 0,
        )
        recv = exchange(packed, "axial", SEGMENTS)
        if first:
            maps_recv = recv
        (solved,) = call(
            lambda *refs, f=first: reduced_kernel(f, *refs),
            [(SEGMENTS * VEC_GROUPS, 128)], recv, *(() if first else (maps_recv,)),
            scratch=[(6 * SIZE * 8, 128)],
        )
        back_recv = exchange(solved, "axial", SEGMENTS)
        common = (back_recv, u, source, chain, lines)
        if last:
            (result,) = call(
                lambda *refs: finish_kernel(True, *refs), [raw_field], *common,
                scratch=[(FIELD, 128), raw_field, pltpu.SemaphoreType.DMA((VARS,))], sent=(0,),
            )
        else:
            sent, last_line, first_line, u = call(
                lambda *refs: finish_kernel(False, *refs), [(FIELD, 128), edge, edge, (FIELD + 2 * halo[0], 128)],
                *common, scratch=[pltpu.SemaphoreType.DMA((STEPS,))], sent=(0,),
            )
    return result.transpose(1, 0, 2)[None]


def solution(mesh):
    return jax.shard_map(
        body,
        mesh=mesh,
        in_specs=(
            P("inst", "axial", None, "span"),
            P("inst", "axial", None, "span"),
            P("inst", "axial", None, None, "span"),
            P("inst", "axial", None, None, "span"),
            P("inst", "axial", None, None, "span"),
            P("axial", "span"),
        ),
        out_specs=P("inst", "axial", None, "span"),
        check_vma=False,
    )
```
